32 devices in a mesh: dp: 8 (over z, y), zero: 4 (over x, core).
Axes of the slice: x: 2, y: 2, z: 4, core: 2. Of those that a mesh axis runs over, the one named last changes fastest.
Arguments:
- tokens: bfloat16 [64, 1024, 576], P(('dp', 'zero')), may hold values from -6 to 6
- cotangent: bfloat16 [64, 1024, 576], P(('dp', 'zero')), may hold values from -6 to 6
- lengths: int32 [64], replicated, may hold values from 128 to 1024, as said below
- balance: int32 [4, 16], replicated, may hold values from 0 to 15, as said below
- master: float32 [3545408], P('zero'), may hold values from -3 to 3, as said below
- moment_one: float32 [3545408], P('zero'), may hold values from -640 to 640
- moment_two: float32 [3545408], P('zero'), may hold values from 100 to 100000
Outputs:
- output: bfloat16 [64, 1024, 576], P(('dp', 'zero'))
- grad_tokens: bfloat16 [64, 1024, 576], P(('dp', 'zero'))
- grads: float32 [3545408], P('zero')
- update_dir: float32 [3545408], P('zero')
- new_moment_one: float32 [3545408], P('zero')
- new_moment_two: float32 [3545408], P('zero')
- grad_gains: float32 [2, 576], P(None, 'zero')
The draws below stay inside these ranges and needn't reach their ends.
Inputs may be any that keep to these rules, and one draw needn't show every extreme that they name: `lengths`: in every draw one sequence has exactly 1024 tokens and one exactly 128. `balance`: each row is a permutation. The 2 sequences that one balanced device holds come from 2 different data indices, and the 2 sequences of one loader device go to 2 different data indices. `master`: the flat vector in the order of the steps.
All inputs are finite; a program needn't handle non-finite values.
Results may differ from the reference program's by a relative error of at most 0.014.
The reference program's roundings to bfloat16 on the way count: a program that leaves them out, or rounds other values in their place, can miss the bound.
Values may be sent and summed in bfloat16 or wider, within the bound.
A program may use at most 384 MiB of HBM per device.

```python
import math
import jax
import jax.numpy as jnp
from jax import lax

D = 576
HEADS = 9
KV_HEADS = 3
HEAD_DIM = 64
FF = 1536
SEQ_DEV = 2
LANE = 1024
LMIN = 128
QKVG = 969
PARAMS = 3545408
LANES = 64
N_DP = 8
N_ZERO = 4


def draw_lengths(key, part):
    key_level, key_long, key_short, key_top, key_bottom = jax.random.split(key, 5)
    level_flag = jax.random.randint(key_level, (N_DP * N_ZERO, 1), 0, 2)
    level_flag = jnp.broadcast_to(level_flag, (N_DP * N_ZERO, SEQ_DEV)).reshape(-1)
    long_draw = jax.random.randint(key_long, (LANES,), LANE // 2, LANE + 1)
    short_draw = jax.random.randint(key_short, (LANES,), LMIN, LANE // 2 + 1)
    picked = jnp.where(level_flag == 1, long_draw, short_draw)
    top_index = jax.random.randint(key_top, (), 0, LANES)
    bottom_index = (top_index + 1 + jax.random.randint(key_bottom, (), 0, LANES - 1)) % LANES
    picked = picked.at[top_index].set(LANE).at[bottom_index].set(LMIN)
    return picked.astype(jnp.int32)


def draw_balance(key, part):
    rows_list = []
    for zero_pos in range(N_ZERO):
        key_order, key_lanes = jax.random.split(jax.random.fold_in(key, zero_pos))
        order = jax.random.permutation(key_order, N_DP)
        inverse = jnp.argsort(order)
        lane_keys = jax.random.split(key_lanes, N_DP)
        shuffles = jax.vmap(lambda sub_key: jax.random.permutation(sub_key, SEQ_DEV))(lane_keys)
        target_dev = jnp.arange(N_DP, dtype=jnp.int32)[:, None]
        slot_index = jnp.arange(SEQ_DEV, dtype=jnp.int32)[None, :]
        source_dev = inverse[(target_dev - slot_index) % N_DP]
        lane_index = shuffles[source_dev, jnp.broadcast_to(slot_index, (N_DP, SEQ_DEV))]
        rows_list.append((source_dev * SEQ_DEV + lane_index).reshape(-1))
    return jnp.stack(rows_list).astype(jnp.int32)


def draw_master(key, part):
    shapes_list = [(D * QKVG, D ** (-0.5)), (HEADS * HEAD_DIM * D, 10.0 * (HEADS * HEAD_DIM) ** (-0.5)), (2 * D * FF, D ** (-0.5)), (FF * D, FF ** (-0.5))]
    keys_all = jax.random.split(key, 6)
    pieces = []
    for index_pos, shape_pair in enumerate(shapes_list):
        sample = jnp.clip(jnp.clip(jax.random.normal(keys_all[index_pos], (shape_pair[0],), jnp.float32), -6.0, 6.0) * shape_pair[1], -3.0, 3.0)
        pieces.append(sample)
    pieces.append(1.0 + 0.1 * jax.random.uniform(keys_all[4], (2 * D,), jnp.float32, -1.0, 1.0))
    pieces.append(1.4 * (1.0 + 0.1 * jax.random.uniform(keys_all[5], (2 * HEAD_DIM,), jnp.float32, -1.0, 1.0)))
    return jnp.concatenate(pieces)


def block_levels(own_key, dims, cuts, smallest, high):
    factor_of, own = 1.0, jax.random.fold_in(own_key, 6)
    for dim, parts in cuts:
        steps = jnp.exp(jax.random.uniform(jax.random.fold_in(own, dim), (parts,), jnp.float32, smallest / len(cuts), high / len(cuts)))
        factor_of = factor_of * jnp.repeat(steps, dims[dim] // parts).reshape([-1 if axis == dim else 1 for axis in range(len(dims))])
    return factor_of


def scatter_about(stream_key, shape, width, bound, cuts=(), kind=jnp.bfloat16):
    loudness = block_levels(stream_key, shape, cuts, -0.22, 0.18) if cuts else 1.0
    values = jax.random.normal(stream_key, shape, jnp.float32) * width * loudness
    return jnp.minimum(jnp.maximum(values, -bound), bound).astype(kind)


def setup_inputs(seed: int = 0) -> dict:
    key_of = jax.random.split(jax.random.key(seed), 8)
    tokens = scatter_about(key_of[0], (LANES, LANE, D), 1.0, 6.0, ((0, 32),))
    cotangent = scatter_about(key_of[1], (LANES, LANE, D), 1.0, 6.0, ((0, 32),))
    lengths = draw_lengths(jax.random.fold_in(key_of[7], 71), 0)
    balance = draw_balance(jax.random.fold_in(key_of[7], 71), 0)
    master = draw_master(jax.random.fold_in(key_of[7], 71), 0)
    moment_one = scatter_about(key_of[5], (PARAMS,), 100.0, 640.0, ((0, 4),), jnp.float32)
    moment_two = jnp.clip(jnp.exp(math.log(100000.0) - 6.9077553 * jax.random.uniform(key_of[6], (PARAMS,), jnp.float32) ** block_levels(key_of[6], (PARAMS,), ((0, 4),), -0.2, 0.2)), 100.0, 100000.0)
    return dict(tokens=tokens, cotangent=cotangent, lengths=lengths, balance=balance, master=master, moment_one=moment_one, moment_two=moment_two)


EPSILON = 1e-05
ROPE_BASE = 100000.0
BETA_ONE = 0.9
BETA_TWO = 0.95
BIAS_ONE = 1.0 - BETA_ONE ** 10
BIAS_TWO = 1.0 - BETA_TWO ** 10
MASK_VALUE = -1e+30

@jax.custom_vjp
def low(v):
    return lax.optimization_barrier(v.astype(jnp.bfloat16)).astype(jnp.float32)

@jax.custom_vjp
def low_back(v):
    return v

def low_keep(v):
    return (low(v), None)

def low_pass(kept, grad):
    return (grad,)

def back_keep(v):
    return (v, None)

def back_low(kept, grad):
    return (low(grad),)
low.defvjp(low_keep, low_pass)
low_back.defvjp(back_keep, back_low)

def split_flat(flat):
    sizes_list = [D * QKVG, HEADS * HEAD_DIM * D, 2 * D * FF, FF * D, 2 * D, 2 * HEAD_DIM]
    shapes_list = [(D, QKVG), (HEADS * HEAD_DIM, D), (D, 2 * FF), (FF, D), (2, D), (2, HEAD_DIM)]
    pieces = []
    offset = 0
    for entry_count, shape_pair in zip(sizes_list, shapes_list):
        pieces.append(flat[offset:offset + entry_count].reshape(shape_pair))
        offset = offset + entry_count
    return pieces

def rms_gain(values, gain_vec):
    return values * lax.rsqrt(lax.optimization_barrier(jnp.mean(values * values, axis=-1, keepdims=True)) + EPSILON) * gain_vec

def rotate(values, positions):
    half_width = values.shape[-1] // 2
    frequency = ROPE_BASE ** (-(jnp.arange(half_width, dtype=jnp.float32) * 2.0) / values.shape[-1])
    angles = positions[:, None] * frequency[None, :]
    cosine = jnp.cos(angles)[:, None, :]
    sine_part = jnp.sin(angles)[:, None, :]
    first_half = values[..., :half_width]
    second_half = values[..., half_width:]
    return jnp.concatenate([first_half * cosine - second_half * sine_part, second_half * cosine + first_half * sine_part], axis=-1)

def layer(moved, flat32, lane_length):
    high = lax.Precision.HIGHEST
    w_in, w_out, w_mlp, w_down, gains, head_gains = split_flat(low(flat32))
    group_count = moved.shape[0]
    positions = jnp.arange(LANE, dtype=jnp.float32)
    row_pos = jnp.arange(LANE, dtype=jnp.int32)
    valid_rows = row_pos[None, :] < lane_length[:, None]
    normed = low(rms_gain(moved, gains[0]))
    projected = low_back(jnp.einsum('gld,de->gle', normed, w_in, precision=high))
    width_q = HEADS * HEAD_DIM
    width_k = KV_HEADS * HEAD_DIM
    query_raw = projected[..., :width_q].reshape(group_count, LANE, HEADS, HEAD_DIM)
    key_raw = projected[..., width_q:width_q + width_k].reshape(group_count, LANE, KV_HEADS, HEAD_DIM)
    value_raw = projected[..., width_q + width_k:width_q + 2 * width_k].reshape(group_count, LANE, KV_HEADS, HEAD_DIM)
    gate_logit = projected[..., width_q + 2 * width_k:]
    queries = low(rotate(rms_gain(query_raw, head_gains[0]), positions))
    keys_rot = low(rotate(rms_gain(key_raw, head_gains[1]), positions))
    values_low = low(value_raw)
    grouped = queries.reshape(group_count, LANE, KV_HEADS, HEADS // KV_HEADS, HEAD_DIM)
    scores = low_back(jnp.einsum('bqkrd,bnkd->bkrqn', grouped, keys_rot, precision=high) * (1.0 / math.sqrt(HEAD_DIM)))
    allowed = (row_pos[None, :] <= row_pos[:, None])[None] & valid_rows[:, None, :]
    scores = jnp.where(allowed[:, None, None], scores, MASK_VALUE)
    probs_low = low(jax.nn.softmax(scores, axis=-1))
    attended = low_back(jnp.einsum('bkrqn,bnkd->bqkrd', probs_low, values_low, precision=high))
    attended = attended.reshape(group_count, LANE, HEADS, HEAD_DIM)
    gated_out = low((attended * jax.nn.sigmoid(gate_logit)[..., None]).reshape(group_count, LANE, width_q))
    branch = low_back(jnp.einsum('gle,ed->gld', gated_out, w_out, precision=high))
    hidden_in = moved + branch
    mixed_in = low(rms_gain(hidden_in, gains[1]))
    gate_up = low_back(jnp.einsum('gld,de->gle', mixed_in, w_mlp, precision=high))
    activated = low(jax.nn.silu(gate_up[..., :FF]) * gate_up[..., FF:])
    result = hidden_in + jnp.einsum('glf,fd->gld', activated, w_down, precision=high)
    return result * valid_rows[..., None].astype(jnp.float32)

def balanced_sources(balance):
    data_pos = jnp.arange(N_DP, dtype=jnp.int32)[:, None, None]
    zero_pos = jnp.arange(N_ZERO, dtype=jnp.int32)[None, :, None]
    slot_pos = jnp.arange(SEQ_DEV, dtype=jnp.int32)[None, None, :]
    entry = balance[zero_pos, data_pos * SEQ_DEV + slot_pos]
    source = (entry // SEQ_DEV * N_ZERO + zero_pos) * SEQ_DEV + entry % SEQ_DEV
    return source.reshape(-1).astype(jnp.int32)

def reference(tokens, cotangent, lengths, balance, master, moment_one, moment_two):
    source_lane = balanced_sources(balance)
    lane_length = jnp.take(lengths, source_lane)
    moved = jnp.take(tokens, source_lane, axis=0).astype(jnp.float32)
    group_total = LANES // SEQ_DEV
    moved_groups = moved.reshape(group_total, SEQ_DEV, LANE, D)
    length_groups = lane_length.reshape(group_total, SEQ_DEV)
    cot_groups = cotangent.astype(jnp.float32).reshape(group_total, SEQ_DEV, LANE, D)

    def group_step(grad_sum_all, packed):
        lanes_in, lengths_in, cot_in = packed
        lane_out, pullback = jax.vjp(lambda first_arg, second_arg: layer(first_arg, second_arg, lengths_in), lanes_in, master)
        grad_lanes, grad_flat = pullback(cot_in)
        return (grad_sum_all + grad_flat, (lane_out.astype(jnp.bfloat16), grad_lanes.astype(jnp.bfloat16)))
    grads, (outputs_all, grad_all) = lax.scan(group_step, jnp.zeros_like(master), (moved_groups, length_groups, cot_groups))
    output = outputs_all.reshape(LANES, LANE, D)
    grad_tokens = jnp.zeros((LANES, LANE, D), jnp.bfloat16).at[source_lane].set(grad_all.reshape(LANES, LANE, D))
    gain_start = PARAMS - 2 * D - 2 * HEAD_DIM
    grad_gains = grads[gain_start:gain_start + 2 * D].reshape(2, D)
    new_one = BETA_ONE * moment_one + (1.0 - BETA_ONE) * grads
    new_two = BETA_TWO * moment_two + (1.0 - BETA_TWO) * grads * grads
    update_dir = new_one / BIAS_ONE / jnp.sqrt(new_two / BIAS_TWO)
    return (output, grad_tokens, grads, update_dir, new_one, new_two, grad_gains)
```

```python
import functools
import math

import jax
import jax.numpy as jnp
import numpy as np
from jax import lax
from jax.experimental import pallas as pl
from jax.experimental.pallas import tpu as pltpu
from jax.sharding import PartitionSpec as P

D = 576
HEADS = 9
KV_HEADS = 3
GROUP = HEADS // KV_HEADS
HEAD_DIM = 64
HALF = HEAD_DIM // 2
FF = 1536
LANE = 1024
QKVG = 969
QKVG_PAD = 1024
WIDTH_Q = HEADS * HEAD_DIM
WIDTH_K = KV_HEADS * HEAD_DIM
PARAMS = 3545408
EPSILON = 1e-05
ROPE_BASE = 100000.0
BETA_ONE = 0.9
BETA_TWO = 0.95
BIAS_ONE = 1.0 - BETA_ONE**10
BIAS_TWO = 1.0 - BETA_TWO**10
SCALE = HEAD_DIM ** (-0.5)
EXP_SCALE = SCALE * math.log2(math.e)
F32 = jnp.float32
BF16 = jnp.bfloat16
BLOCK = 256
BLOCKS = LANE // BLOCK
FF_CHUNK = 768
MLP_BLOCK = 512
MLP_BLOCKS = LANE // MLP_BLOCK
PROJ_BLOCK = 512
PROJ_BLOCKS = LANE // PROJ_BLOCK
VMEM_LIMIT = 60 * 1024 * 1024


def dot(a, b, ca, cb):
    return lax.dot_general(a, b, (((ca,), (cb,)), ((), ())), preferred_element_type=F32)


def rope_tables():
    frequency = ROPE_BASE ** (-(np.arange(HALF, dtype=np.float32) * np.float32(2.0)) / np.float32(HEAD_DIM))
    angles = np.arange(LANE, dtype=np.float32)[None, :] * frequency.astype(np.float32)[:, None]
    return np.cos(angles).astype(np.float32), np.sin(angles).astype(np.float32)


def mean_square_scale(values, axis):
    return lax.rsqrt(jnp.mean(values * values, axis=axis, keepdims=True) + EPSILON)


def block_spec(shape, index):
    return pl.BlockSpec(shape, index)


def whole(shape):
    return pl.BlockSpec(shape, lambda *_: (0,) * len(shape), pipeline_mode=pl.Buffered(1))


def full_col_map(lane, block, lens):
    return (lane, 0, block)


def last_block(lens, lane, block):
    return jnp.minimum(block, (lens[lane] - 1) // BLOCK)


def project_kernel(lens, tok_t, w_in, gain_cols, head_gains, cosine, sine, q_t, k_n, k_t, v_n, v_t, raw, gate, w_in_t):
    lane, block = pl.program_id(0), pl.program_id(1)

    @pl.when((lane == 0) & (block == 0))
    def _():
        w_in_t[...] = w_in[...].T

    @pl.when(block * PROJ_BLOCK < lens[lane])
    def _():
        x = tok_t[0].astype(F32)
        normed = (x * mean_square_scale(x, 0) * gain_cols[0]).astype(BF16)
        projected = dot(w_in_t[...], normed, 1, 0)
        raw[0] = projected[: WIDTH_Q + WIDTH_K]
        cos, sin = cosine[...], sine[...]
        for head in range(HEADS + KV_HEADS):
            u = projected[head * HEAD_DIM : (head + 1) * HEAD_DIM]
            y = u * mean_square_scale(u, 0) * head_gains[0 if head < HEADS else 1]
            y1, y2 = y[:HALF], y[HALF:]
            turned = jnp.concatenate([y1 * cos - y2 * sin, y2 * cos + y1 * sin], axis=0)
            if head < HEADS:
                q_t[0, head * HEAD_DIM : (head + 1) * HEAD_DIM] = turned.astype(BF16)
            else:
                k = head - HEADS
                k_t[0, k * HEAD_DIM : (k + 1) * HEAD_DIM] = turned.astype(BF16)
                k_n[0, k] = turned.T.astype(BF16)
        values = projected[WIDTH_Q + WIDTH_K : WIDTH_Q + 2 * WIDTH_K]
        v_t[0] = values.astype(BF16)
        for k in range(KV_HEADS):
            v_n[0, k] = values[k * HEAD_DIM : (k + 1) * HEAD_DIM].T.astype(BF16)
        gate[0] = projected[WIDTH_Q + 2 * WIDTH_K : WIDTH_Q + 2 * WIDTH_K + 16]

    @pl.when(block * PROJ_BLOCK >= lens[lane])
    def _():
        for ref in (q_t, k_n, k_t, v_n, v_t):
            ref[...] = jnp.zeros_like(ref)


def col_map(lane, block, lens):
    return (lane, 0, last_block(lens, lane, block))


def mlp_row_map(lane, block, lens):
    return (lane, jnp.minimum(block, (lens[lane] - 1) // MLP_BLOCK), 0)


def mlp_col_map(lane, block, lens):
    return (lane, 0, jnp.minimum(block, (lens[lane] - 1) // MLP_BLOCK))


def proj_col_map(lane, block, lens):
    return (lane, 0, jnp.minimum(block, (lens[lane] - 1) // PROJ_BLOCK))


def proj_table_map(lane, block, lens):
    return (0, jnp.minimum(block, (lens[lane] - 1) // PROJ_BLOCK))


def full_head_map(lane, block, lens):
    return (lane, 0, block, 0)


def project(lens, tokens_t, w_in, gain_cols, head_gains, cosine, sine):
    lanes = tokens_t.shape[0]
    shape = jax.ShapeDtypeStruct
    return pl.pallas_call(
        project_kernel,
        name="project",
        grid_spec=pltpu.PrefetchScalarGridSpec(
            num_scalar_prefetch=1,
            grid=(lanes, PROJ_BLOCKS),
            in_specs=[
                pl.BlockSpec((1, D, PROJ_BLOCK), proj_col_map),
                whole((D, QKVG_PAD)),
                whole((2, D, 1)),
                whole((2, HEAD_DIM, 1)),
                pl.BlockSpec((HALF, PROJ_BLOCK), proj_table_map),
                pl.BlockSpec((HALF, PROJ_BLOCK), proj_table_map),
            ],
            out_specs=[
                pl.BlockSpec((1, WIDTH_Q, PROJ_BLOCK), full_col_map),
                pl.BlockSpec((1, KV_HEADS, PROJ_BLOCK, HEAD_DIM), full_head_map),
                pl.BlockSpec((1, WIDTH_K, PROJ_BLOCK), full_col_map),
                pl.BlockSpec((1, KV_HEADS, PROJ_BLOCK, HEAD_DIM), full_head_map),
                pl.BlockSpec((1, WIDTH_K, PROJ_BLOCK), full_col_map),
                pl.BlockSpec((1, WIDTH_Q + WIDTH_K, PROJ_BLOCK), proj_col_map),
                pl.BlockSpec((1, 16, PROJ_BLOCK), proj_col_map),
            ],
            scratch_shapes=[pltpu.VMEM((QKVG_PAD, D), BF16)],
        ),
        out_shape=[
            shape((lanes, WIDTH_Q, LANE), BF16),
            shape((lanes, KV_HEADS, LANE, HEAD_DIM), BF16),
            shape((lanes, WIDTH_K, LANE), BF16),
            shape((lanes, KV_HEADS, LANE, HEAD_DIM), BF16),
            shape((lanes, WIDTH_K, LANE), BF16),
            shape((lanes, WIDTH_Q + WIDTH_K, LANE), F32),
            shape((lanes, 16, LANE), F32),
        ],
        cost_estimate=pl.CostEstimate(flops=0, bytes_accessed=0, transcendentals=0),
        compiler_params=pltpu.CompilerParams(vmem_limit_bytes=VMEM_LIMIT),
    )(lens, tokens_t, w_in, gain_cols, head_gains, cosine, sine)


def causal_tile(values, fill):
    key_pos = lax.broadcasted_iota(jnp.int32, values.shape, 0)
    query_pos = lax.broadcasted_iota(jnp.int32, values.shape, 1)
    return jnp.where(key_pos <= query_pos, values, fill)


def attend_kernel(lens, q_t, k_n, v_t, out_t, log_total):
    lane, block = pl.program_id(0), pl.program_id(1)
    log_total[0] = jnp.zeros((16, BLOCK), F32)

    for level in range(BLOCKS):

        @pl.when((block == level) & (level * BLOCK < lens[lane]))
        def _():
            before = level * BLOCK
            for head in range(HEADS):
                g = head // GROUP
                query = q_t[0, head * HEAD_DIM : (head + 1) * HEAD_DIM]
                values = v_t.at[0, g * HEAD_DIM : (g + 1) * HEAD_DIM]
                weights = jnp.exp2(dot(k_n[0, g, before : before + BLOCK], query, 1, 0) * EXP_SCALE)
                weights = causal_tile(weights, 0.0)
                total = jnp.sum(weights, axis=0, keepdims=True)
                mixed = dot(values[:, before : before + BLOCK], weights.astype(BF16), 1, 0)
                if before:
                    weights = jnp.exp2(dot(k_n[0, g, :before], query, 1, 0) * EXP_SCALE)
                    total += jnp.sum(weights, axis=0, keepdims=True)
                    mixed += dot(values[:, :before], weights.astype(BF16), 1, 0)
                out_t[0, head * HEAD_DIM : (head + 1) * HEAD_DIM] = mixed * (1.0 / total)
                log_total[0, head : head + 1] = jnp.log2(total)


def attend(lens, q_t, k_n, v_t):
    lanes = q_t.shape[0]
    shape = jax.ShapeDtypeStruct
    return pl.pallas_call(
        attend_kernel,
        name="attend",
        grid_spec=pltpu.PrefetchScalarGridSpec(
            num_scalar_prefetch=1,
            grid=(lanes, BLOCKS),
            in_specs=[
                pl.BlockSpec((1, WIDTH_Q, BLOCK), col_map),
                pl.BlockSpec((1, KV_HEADS, LANE, HEAD_DIM), lambda lane, block, lens: (lane, 0, 0, 0)),
                pl.BlockSpec((1, WIDTH_K, LANE), lambda lane, block, lens: (lane, 0, 0)),
            ],
            out_specs=[
                pl.BlockSpec((1, WIDTH_Q, BLOCK), col_map),
                pl.BlockSpec((1, 16, BLOCK), full_col_map),
            ],
        ),
        out_shape=[
            shape((lanes, WIDTH_Q, LANE), F32),
            shape((lanes, 16, LANE), F32),
        ],
        cost_estimate=pl.CostEstimate(flops=0, bytes_accessed=0, transcendentals=0),
        compiler_params=pltpu.CompilerParams(vmem_limit_bytes=VMEM_LIMIT),
    )(lens, q_t, k_n, v_t)


OUT_ROWS = WIDTH_Q * D // 128
MLP_ROWS = D * 2 * FF // 128
DOWN_ROWS = FF * D // 128
LATE_ROWS = OUT_ROWS + MLP_ROWS + DOWN_ROWS
WIDE_TILES = 2 * FF // 128
WIDE_STEP = 48
PAIR_STEP = 32
PAIR_ROWS = PAIR_STEP * 9


def pack_wide(source, target, stage, first_row):
    @pl.loop(0, D // WIDE_STEP)
    def _(piece):
        rows = pl.ds(pl.multiple_of(piece * WIDE_STEP, WIDE_STEP), WIDE_STEP)
        for tile in range(WIDE_TILES):
            stage[pl.ds(tile, WIDE_STEP, stride=WIDE_TILES), :] = source[rows, tile * 128 : (tile + 1) * 128]
        size = WIDE_STEP * WIDE_TILES
        target[pl.ds(pl.multiple_of(first_row + piece * size, 16), size), :] = stage[:size].astype(BF16)


def set_tiles(target, value):
    for t in range(4):
        target[t] = value[:, t * 128 : (t + 1) * 128]
    target[4, :, :64] = value[:, 512:]


def pack_pairs(rows_ref, stage):
    tiles = [rows_ref[t, pl.ds(parity, PAIR_STEP, stride=2), :] for parity in range(2) for t in range(5)]
    even, odd = tiles[:5], tiles[5:]
    for t in range(4):
        stage[pl.ds(t, PAIR_STEP, stride=9), :] = even[t]
    stage[pl.ds(4, PAIR_STEP, stride=9), :] = jnp.concatenate([even[4][:, :64], odd[0][:, :64]], axis=1)
    for t in range(4):
        right = odd[t + 1][:, :64]
        stage[pl.ds(5 + t, PAIR_STEP, stride=9), :] = jnp.concatenate([odd[t][:, 64:], right], axis=1)


def mlp_kernel(lens, att_t, gate, tok_t, gains, w_out, w_mlp, w_down, out_parts, hidden_in, act_low, gate_slope, up_slope, total):
    lane, block = pl.program_id(0), pl.program_id(1)

    @pl.when(block * MLP_BLOCK >= lens[lane])
    def _():
        out_parts[...] = jnp.zeros_like(out_parts)

    @pl.when(block * MLP_BLOCK < lens[lane])
    def _():
        att = att_t[0].reshape(HEADS, HEAD_DIM, MLP_BLOCK)
        sig = jax.nn.sigmoid(gate[0, :HEADS])[:, None, :]
        gated_t = (att * sig).reshape(WIDTH_Q, MLP_BLOCK).astype(BF16)
        hidden = tok_t[0].T.astype(F32) + dot(gated_t, w_out[...], 0, 0)
        hidden_in[0] = hidden
        mixed = (hidden * mean_square_scale(hidden, 1) * gains[1:2]).astype(BF16)
        valid_t = lax.broadcasted_iota(jnp.int32, (1, MLP_BLOCK), 1) + block * MLP_BLOCK < lens[lane]
        total[...] = hidden

        @pl.loop(0, FF // FF_CHUNK, unroll=True)
        def _(chunk):
            low = pl.ds(pl.multiple_of(chunk * FF_CHUNK, FF_CHUNK), FF_CHUNK)
            high = pl.ds(pl.multiple_of(FF + chunk * FF_CHUNK, FF_CHUNK), FF_CHUNK)
            g = dot(mixed, w_mlp[:, low], 1, 0)
            u = dot(mixed, w_mlp[:, high], 1, 0)
            s = jax.nn.sigmoid(g)
            gs = g * s
            act = (gs * u).astype(BF16)
            total[...] += dot(act, w_down[low, :], 1, 0)
            act_low[0, :, low] = act
            gate_slope[0, :, low] = (u * (s * (1.0 + g * (1.0 - s)))).astype(BF16)
            up_slope[0, :, low] = gs.astype(BF16)

        out_t = jnp.where(valid_t, total[...].T, 0.0).astype(BF16)
        width = out_parts.shape[3]
        for part in range(out_parts.shape[0]):
            out_parts[part, 0] = out_t[:, part * width : (part + 1) * width]


def part_map(lane, block, lens):
    return (block, lane, 0, 0)


def kept_part_map(lane, block, lens):
    return (jnp.minimum(block, (lens[lane] - 1) // MLP_BLOCK), lane, 0, 0)


def mlp(lens, att_t, gate, tokens_t, gains, w_out, w_mlp, w_down, dp_size):
    lanes = tokens_t.shape[0]
    width = LANE // dp_size
    shape = jax.ShapeDtypeStruct
    return pl.pallas_call(
        mlp_kernel,
        name="mlp",
        grid_spec=pltpu.PrefetchScalarGridSpec(
            num_scalar_prefetch=1,
            grid=(lanes, MLP_BLOCKS),
            in_specs=[
                pl.BlockSpec((1, WIDTH_Q, MLP_BLOCK), mlp_col_map),
                pl.BlockSpec((1, 16, MLP_BLOCK), mlp_col_map),
                pl.BlockSpec((1, D, MLP_BLOCK), mlp_col_map),
                whole((2, D)),
                whole((WIDTH_Q, D)),
                whole((D, 2 * FF)),
                whole((FF, D)),
            ],
            out_specs=[
                pl.BlockSpec((dp_size // MLP_BLOCKS, 1, D, width), part_map),
                pl.BlockSpec((1, MLP_BLOCK, D), mlp_row_map),
                pl.BlockSpec((1, MLP_BLOCK, FF), mlp_row_map),
                pl.BlockSpec((1, MLP_BLOCK, FF), mlp_row_map),
                pl.BlockSpec((1, MLP_BLOCK, FF), mlp_row_map),
            ],
            scratch_shapes=[pltpu.VMEM((MLP_BLOCK, D), F32)],
        ),
        out_shape=[
            shape((dp_size, lanes, D, width), BF16),
            shape((lanes, LANE, D), F32),
            shape((lanes, LANE, FF), BF16),
            shape((lanes, LANE, FF), BF16),
            shape((lanes, LANE, FF), BF16),
        ],
        compiler_params=pltpu.CompilerParams(vmem_limit_bytes=VMEM_LIMIT),
    )(lens, att_t, gate, tokens_t, gains, w_out, w_mlp, w_down)


def mlp_back_kernel(lens, att_t, gate, cot_parts, hidden_in, act_low, gate_slope, up_slope, gains, w_out, w_mlp, w_down,
                    grad_hidden_t, grad_att_t, logit_delta, late, g_gain,
                    back, g_out, g_mlp, g_down_t, stage, pair_rows):
    lane, block = pl.program_id(0), pl.program_id(1)

    @pl.when((lane == 0) & (block == 0))
    def _():
        g_out[...] = jnp.zeros_like(g_out)
        g_mlp[...] = jnp.zeros_like(g_mlp)
        g_down_t[...] = jnp.zeros_like(g_down_t)
        g_gain[...] = jnp.zeros_like(g_gain)

    @pl.when(block * MLP_BLOCK >= lens[lane])
    def _():
        grad_att_t[...] = jnp.zeros_like(grad_att_t)
        logit_delta[...] = jnp.zeros_like(logit_delta)

    @pl.when(block * MLP_BLOCK < lens[lane])
    def _():
        att = att_t[0].reshape(HEADS, HEAD_DIM, MLP_BLOCK)
        sig = jax.nn.sigmoid(gate[0, :HEADS])[:, None, :]
        gated_t = (att * sig).reshape(WIDTH_Q, MLP_BLOCK).astype(BF16)
        hidden = hidden_in[0]
        scale = mean_square_scale(hidden, 1)
        gain = gains[1:2]
        mixed_t = (hidden * scale * gain).astype(BF16).T
        valid_t = lax.broadcasted_iota(jnp.int32, (1, MLP_BLOCK), 1) + block * MLP_BLOCK < lens[lane]
        cot_t = jnp.concatenate([cot_parts[part, 0] for part in range(cot_parts.shape[0])], axis=1)
        grad_low_t = jnp.where(valid_t, cot_t.astype(F32), 0.0).astype(BF16)
        grad_low = grad_low_t.T
        back[...] = jnp.zeros_like(back)

        @pl.loop(0, FF // FF_CHUNK, unroll=True)
        def _(chunk):
            low = pl.ds(pl.multiple_of(chunk * FF_CHUNK, FF_CHUNK), FF_CHUNK)
            high = pl.ds(pl.multiple_of(FF + chunk * FF_CHUNK, FF_CHUNK), FF_CHUNK)
            a = dot(grad_low, w_down[low, :], 1, 1)
            grad_gate = (a * gate_slope[0, :, low].astype(F32)).astype(BF16)
            grad_up = (a * up_slope[0, :, low].astype(F32)).astype(BF16)
            back[...] += dot(grad_gate, w_mlp[:, low], 1, 1) + dot(grad_up, w_mlp[:, high], 1, 1)
            g_mlp[:, low] += dot(mixed_t, grad_gate, 1, 0)
            g_mlp[:, high] += dot(mixed_t, grad_up, 1, 0)
            g_down_t[:, low] += dot(grad_low_t, act_low[0, :, low], 1, 0)

        b = back[...]
        g_gain[0:1] += jnp.sum(b * hidden * scale, axis=0, keepdims=True)
        bg = b * gain
        grad_h = grad_low.astype(F32) + scale * bg - hidden * (scale * scale * scale * jnp.mean(hidden * bg, axis=1, keepdims=True))
        grad_hidden_t[0] = grad_h.T
        branch = grad_h.astype(BF16)
        g_out[...] += dot(gated_t, branch, 1, 0)
        c = dot(w_out[...], branch, 1, 1).reshape(HEADS, HEAD_DIM, MLP_BLOCK)
        grad_att = (c * sig).astype(BF16)
        grad_att_t[0] = grad_att.reshape(WIDTH_Q, MLP_BLOCK)
        sig2 = sig[:, 0, :]
        logit_delta[0, :HEADS] = jnp.sum(c * att, axis=1) * (sig2 * (1.0 - sig2))
        logit_delta[0, 16 : 16 + HEADS] = jnp.sum(grad_att.astype(F32) * att, axis=1)

    @pl.when((lane == pl.num_programs(0) - 1) & (block == pl.num_programs(1) - 1))
    def _():
        @pl.loop(0, WIDTH_Q // (2 * PAIR_STEP))
        def _(piece):
            set_tiles(pair_rows, g_out[pl.ds(pl.multiple_of(piece * 2 * PAIR_STEP, 2 * PAIR_STEP), 2 * PAIR_STEP), :])
            pack_pairs(pair_rows, stage)
            late[pl.ds(pl.multiple_of(piece * PAIR_ROWS, 16), PAIR_ROWS), :] = stage[:PAIR_ROWS].astype(BF16)

        pack_wide(g_mlp, late, stage, OUT_ROWS)

        @pl.loop(0, FF // 128)
        def _(piece):
            turned = g_down_t[:, pl.ds(pl.multiple_of(piece * 128, 128), 128)].T
            for h in range(128 // (2 * PAIR_STEP)):
                set_tiles(pair_rows, turned[h * 2 * PAIR_STEP : (h + 1) * 2 * PAIR_STEP])
                pack_pairs(pair_rows, stage)
                start = OUT_ROWS + MLP_ROWS + (piece * 2 + h) * PAIR_ROWS
                late[pl.ds(pl.multiple_of(start, 16), PAIR_ROWS), :] = stage[:PAIR_ROWS].astype(BF16)

        late[LATE_ROWS:] = jnp.zeros((late.shape[0] - LATE_ROWS, 128), BF16)


def mlp_back(lens, att_t, gate, cot_parts, hidden_in, act_low, gate_slope, up_slope, gains, w_out, w_mlp, w_down, late_rows):
    dp_size, lanes, _, width = cot_parts.shape
    shape = jax.ShapeDtypeStruct
    return pl.pallas_call(
        mlp_back_kernel,
        name="mlp_back",
        grid_spec=pltpu.PrefetchScalarGridSpec(
            num_scalar_prefetch=1,
            grid=(lanes, MLP_BLOCKS),
            in_specs=[
                pl.BlockSpec((1, WIDTH_Q, MLP_BLOCK), mlp_col_map),
                pl.BlockSpec((1, 16, MLP_BLOCK), mlp_col_map),
                pl.BlockSpec((dp_size // MLP_BLOCKS, 1, D, width), kept_part_map),
                pl.BlockSpec((1, MLP_BLOCK, D), mlp_row_map),
                pl.BlockSpec((1, MLP_BLOCK, FF), mlp_row_map),
                pl.BlockSpec((1, MLP_BLOCK, FF), mlp_row_map),
                pl.BlockSpec((1, MLP_BLOCK, FF), mlp_row_map),
                whole((2, D)),
                whole((WIDTH_Q, D)),
                whole((D, 2 * FF)),
                whole((FF, D)),
            ],
            out_specs=[
                pl.BlockSpec((1, D, MLP_BLOCK), mlp_col_map),
                pl.BlockSpec((1, WIDTH_Q, MLP_BLOCK), full_col_map),
                pl.BlockSpec((1, 32, MLP_BLOCK), full_col_map),
                whole((late_rows, 128)),
                whole((8, D)),
            ],
            scratch_shapes=[
                pltpu.VMEM((MLP_BLOCK, D), F32),
                pltpu.VMEM((WIDTH_Q, D), F32),
                pltpu.VMEM((D, 2 * FF), F32),
                pltpu.VMEM((D, FF), F32),
                pltpu.VMEM((WIDE_STEP * WIDE_TILES, 128), F32),
                pltpu.VMEM((5, 2 * PAIR_STEP, 128), F32),
            ],
        ),
        out_shape=[
            shape((lanes, D, LANE), F32),
            shape((lanes, WIDTH_Q, LANE), BF16),
            shape((lanes, 32, LANE), F32),
            shape((late_rows, 128), BF16),
            shape((8, D), F32),
        ],
        compiler_params=pltpu.CompilerParams(vmem_limit_bytes=VMEM_LIMIT),
    )(lens, att_t, gate, cot_parts, hidden_in, act_low, gate_slope, up_slope, gains, w_out, w_mlp, w_down)


def project_back_kernel(lens, dq_t, dk_t, dv_t, logit_delta, raw, tok_t, grad_hidden_t, w_in, gain_cols, head_gains,
                        cosine, sine, grad_tok_t, g_in, g_gain, g_head, dproj, head_sum, gain_sum):
    lane, block = pl.program_id(0), pl.program_id(1)

    @pl.when((lane == 0) & (block == 0))
    def _():
        g_in[...] = jnp.zeros_like(g_in)
        gain_sum[...] = jnp.zeros_like(gain_sum)
        head_sum[...] = jnp.zeros_like(head_sum)

    @pl.when(block * PROJ_BLOCK >= lens[lane])
    def _():
        grad_tok_t[...] = jnp.zeros_like(grad_tok_t)

    @pl.when(block * PROJ_BLOCK < lens[lane])
    def _():
        cos, sin = cosine[...], sine[...]
        for head in range(HEADS + KV_HEADS):
            rows = slice(head * HEAD_DIM, (head + 1) * HEAD_DIM)
            side = 0 if head < HEADS else 1
            source = dq_t if head < HEADS else dk_t
            at = (head if head < HEADS else head - HEADS) * HEAD_DIM
            d1, d2 = source[0, at : at + HALF], source[0, at + HALF : at + HEAD_DIM]
            d = jnp.concatenate([d1 * cos + d2 * sin, d2 * cos - d1 * sin], axis=0)
            u = raw[0, rows]
            r = mean_square_scale(u, 0)
            ur = u * r
            head_sum[side] += d * ur
            dg = d * head_gains[side]
            dproj[rows] = (r * (dg - ur * jnp.mean(ur * dg, axis=0, keepdims=True))).astype(BF16)
        dproj[WIDTH_Q + WIDTH_K : WIDTH_Q + 2 * WIDTH_K] = dv_t[0].astype(BF16)
        row = lax.broadcasted_iota(jnp.int32, (16, PROJ_BLOCK), 0)
        logits = jnp.where(row < HEADS, logit_delta[0], 0.0).astype(BF16)
        dproj[WIDTH_Q + 2 * WIDTH_K :] = jnp.concatenate(
            [logits, jnp.zeros((QKVG_PAD - WIDTH_Q - 2 * WIDTH_K - 16, PROJ_BLOCK), BF16)], axis=0
        )
        x = tok_t[0].astype(F32)
        scale = mean_square_scale(x, 0)
        xs = x * scale
        gain = gain_cols[0]
        normed = (xs * gain).astype(BF16)
        g_in[...] += dot(normed, dproj[...], 1, 1)
        back = dot(w_in[...], dproj[...], 1, 0)
        gain_sum[...] += back * xs
        bg = back * gain
        grad_x = scale * (bg - xs * jnp.mean(xs * bg, axis=0, keepdims=True))
        grad_tok_t[0] = (grad_hidden_t[0] + grad_x).astype(BF16)

    @pl.when((lane == pl.num_programs(0) - 1) & (block == pl.num_programs(1) - 1))
    def _():
        g_head[...] = jnp.sum(head_sum[...], axis=2)
        g_gain[...] = jnp.sum(gain_sum[...], axis=1)[None]


def project_back(lens, dq_t, dk_t, dv_t, logit_delta, raw, tokens_t, grad_hidden_t, w_in, gain_cols, head_gains, cosine, sine):
    lanes = tokens_t.shape[0]
    shape = jax.ShapeDtypeStruct
    full_col = lambda lane, block, lens: (lane, 0, block)
    return pl.pallas_call(
        project_back_kernel,
        name="project_back",
        grid_spec=pltpu.PrefetchScalarGridSpec(
            num_scalar_prefetch=1,
            grid=(lanes, PROJ_BLOCKS),
            in_specs=[
                pl.BlockSpec((1, WIDTH_Q, PROJ_BLOCK), proj_col_map),
                pl.BlockSpec((1, WIDTH_K, PROJ_BLOCK), proj_col_map),
                pl.BlockSpec((1, WIDTH_K, PROJ_BLOCK), proj_col_map),
                pl.BlockSpec((1, 16, PROJ_BLOCK), proj_col_map),
                pl.BlockSpec((1, WIDTH_Q + WIDTH_K, PROJ_BLOCK), proj_col_map),
                pl.BlockSpec((1, D, PROJ_BLOCK), proj_col_map),
                pl.BlockSpec((1, D, PROJ_BLOCK), proj_col_map),
                whole((D, QKVG_PAD)),
                whole((2, D, 1)),
                whole((2, HEAD_DIM, 1)),
                pl.BlockSpec((HALF, PROJ_BLOCK), proj_table_map),
                pl.BlockSpec((HALF, PROJ_BLOCK), proj_table_map),
            ],
            out_specs=[
                pl.BlockSpec((1, D, PROJ_BLOCK), full_col),
                whole((D, QKVG_PAD)),
                whole((1, D)),
                whole((2, HEAD_DIM)),
            ],
            scratch_shapes=[
                pltpu.VMEM((QKVG_PAD, PROJ_BLOCK), BF16),
                pltpu.VMEM((2, HEAD_DIM, PROJ_BLOCK), F32),
                pltpu.VMEM((D, PROJ_BLOCK), F32),
            ],
        ),
        out_shape=[
            shape((lanes, D, LANE), BF16),
            shape((D, QKVG_PAD), F32),
            shape((1, D), F32),
            shape((2, HEAD_DIM), F32),
        ],
        compiler_params=pltpu.CompilerParams(vmem_limit_bytes=VMEM_LIMIT),
    )(lens, dq_t, dk_t, dv_t, logit_delta, raw, tokens_t, grad_hidden_t, w_in, gain_cols, head_gains, cosine, sine)


def layer_forward(tokens_t, lens, weights):
    w_in, gains, head_gains = weights
    gain_cols, head_gains = gains[:, :, None], head_gains[:, :, None]
    cosine, sine = (jnp.asarray(t) for t in rope_tables())
    q_t, k_n, k_t, v_n, v_t, raw, gate = project(lens, tokens_t, w_in, gain_cols, head_gains, cosine, sine)
    att_t, log_total = attend(lens, q_t, k_n, v_t)
    return att_t, gate, (q_t, k_n, k_t, v_n, log_total, raw)


def head_groups(rows):
    return rows[:, :HEADS].reshape(rows.shape[0], KV_HEADS, GROUP, LANE)


SHARD = PARAMS // 4
LANES128 = 128
EDGE = 16
STEP = 6928
BODY = STEP - EDGE
SPAN = STEP + EDGE
IN_ROWS = 4361
SPLIT_AT = D * QKVG
MESH = pl.DeviceIdType.MESH


def shard_shift(s):
    offset = EDGE * LANES128 - (STEP * LANES128 - SHARD) * s + (64 if s else 0)
    return offset // LANES128, offset % LANES128


def flip(index, bit):
    return index + (1 - 2 * (index // (1 << bit) % 2)) * (1 << bit)


def bit_of(index, bit):
    return index // (1 << bit) % 2


def greet(partners):
    barrier = pltpu.get_barrier_semaphore()
    for partner in partners:
        pl.semaphore_signal(barrier, inc=1, device_id=partner, device_id_type=MESH)
    pl.semaphore_wait(barrier, len(partners))


PACK_TILE = 496
FIRST_ROWS = 4368
LAST_TILE = 32
GAIN_AT = EDGE + IN_ROWS + LATE_ROWS - 3 * STEP - (SPAN - LAST_TILE)
FIRST_CUTS = (0, 1088, 2176, 3264, FIRST_ROWS)


def pack_kernel(master, own, first_rows, last_rows, rows_in, packed, load_sem, keep_sem, own_sem, send_sem, recv_sem):
    dp, zero = lax.axis_index("dp"), lax.axis_index("zero")
    core, across, side = (dp, flip(zero, 0)), (dp, flip(zero, 1)), (flip(dp, 0), zero)
    y = bit_of(dp, 0)
    load = pltpu.make_async_copy(master, rows_in.at[pl.ds(24, STEP)], load_sem)
    load.start()
    rows_in[:24] = jnp.zeros((24, LANES128), F32)
    rows_in[24 + STEP :] = jnp.zeros((24, LANES128), F32)
    greet((core, across, side))
    load.wait()
    lane = lax.broadcasted_iota(jnp.int32, (PACK_TILE, LANES128), 1)

    def shifted(start, a, k):
        if k == 0:
            return rows_in[pl.ds(start + 24 - a, PACK_TILE), :]
        here = pltpu.roll(rows_in[pl.ds(start + 24 - a, PACK_TILE), :], k, 1)
        above = pltpu.roll(rows_in[pl.ds(start + 23 - a, PACK_TILE), :], k, 1)
        return jnp.where(lane >= k, here, above)

    def pack(s, start):
        if s == 0 and start + PACK_TILE <= EDGE + IN_ROWS:
            value = shifted(start, EDGE, 0)
        elif s == 0 and start < EDGE + IN_ROWS:
            row = lax.broadcasted_iota(jnp.int32, (PACK_TILE, LANES128), 0) + start
            value = jnp.where(row < EDGE + IN_ROWS, shifted(start, EDGE, 0), shifted(start, EDGE, 64))
        elif s == 0:
            value = shifted(start, EDGE, 64)
        else:
            value = shifted(start, *shard_shift(s))
        packed[pl.ds(start, PACK_TILE), :] = value.astype(BF16)

    def piece_rows(piece):
        return pl.ds(EDGE + FIRST_CUTS[piece], FIRST_CUTS[piece + 1] - FIRST_CUTS[piece])

    def mine(piece):
        return packed.at[piece_rows(piece)]

    def theirs(piece):
        return first_rows.at[piece_rows(piece)]

    def copy(source, target, device, slot):
        return pltpu.make_async_remote_copy(source, target, send_sem.at[slot], recv_sem.at[slot],
                                            device_id=device, device_id_type=MESH)

    for s in range(4):

        @pl.when(zero == s)
        def _():
            for t in range(SPAN // PACK_TILE):
                pack(s, t * PACK_TILE)

    keep = pltpu.make_async_copy(packed, own, own_sem)
    keep.start()
    tail = packed.at[pl.ds(SPAN - LAST_TILE, LAST_TILE)]

    @pl.when(zero == 3)
    def _():
        copy(tail, last_rows, across, 9).start()
        copy(tail, last_rows, core, 8).start()
        stay = pltpu.make_async_copy(tail, last_rows, keep_sem)
        stay.start()
        stay.wait()
        copy(tail, last_rows, across, 9).wait_send()
        copy(tail, last_rows, core, 8).wait_send()

    @pl.when(zero == 1)
    def _():
        copy(last_rows, last_rows, across, 9).wait_recv()
        copy(last_rows, last_rows, core, 8).start()
        copy(last_rows, last_rows, core, 8).wait_send()

    for half in range(2):
        pieces = (2 * half, 2 * half + 1)
        others = (2 - 2 * half, 3 - 2 * half)

        @pl.when((zero == 0) & (y == half))
        def _():
            for piece in pieces:
                copy(mine(piece), theirs(piece), across, piece).start()
            for piece in range(4):
                copy(mine(piece), theirs(piece), core, 4 + piece).start()
            stay = pltpu.make_async_copy(packed.at[pl.ds(EDGE, FIRST_ROWS)], first_rows.at[pl.ds(EDGE, FIRST_ROWS)], keep_sem)
            stay.start()
            for piece in pieces:
                copy(mine(piece), theirs(piece), across, piece).wait_send()
            for piece in range(4):
                copy(mine(piece), theirs(piece), core, 4 + piece).wait_send()
            stay.wait()

        @pl.when((zero == 2) & (y == half))
        def _():
            for piece in pieces:
                copy(theirs(piece), theirs(piece), across, piece).wait_recv()
                copy(theirs(piece), theirs(piece), side, piece).start()
                copy(theirs(piece), theirs(piece), core, 4 + piece).start()
            for piece in others:
                copy(theirs(piece), theirs(piece), side, piece).wait_recv()
                copy(theirs(piece), theirs(piece), core, 4 + piece).start()
            for piece in pieces:
                copy(theirs(piece), theirs(piece), side, piece).wait_send()
            for piece in range(4):
                copy(theirs(piece), theirs(piece), core, 4 + piece).wait_send()

    @pl.when(bit_of(zero, 0) == 0)
    def _():
        copy(last_rows, last_rows, core, 8).wait_recv()

    @pl.when(bit_of(zero, 0) == 1)
    def _():
        for piece in range(4):
            copy(theirs(piece), theirs(piece), core, 4 + piece).wait_recv()

    keep.wait()


def pack_master(master):
    rows = jnp.pad(master, (0, STEP * LANES128 - SHARD)).reshape(STEP, LANES128)
    shape = jax.ShapeDtypeStruct
    return pl.pallas_call(
        pack_kernel,
        name="pack_master",
        out_shape=[shape((SPAN, LANES128), BF16), shape((EDGE + FIRST_ROWS, LANES128), BF16), shape((LAST_TILE, LANES128), BF16)],
        in_specs=[pl.BlockSpec(memory_space=pl.ANY)],
        out_specs=[pl.BlockSpec(memory_space=pl.ANY)] * 3,
        scratch_shapes=[
            pltpu.VMEM((24 + STEP + 24, LANES128), F32),
            pltpu.VMEM((SPAN, LANES128), BF16),
            pltpu.SemaphoreType.DMA,
            pltpu.SemaphoreType.DMA,
            pltpu.SemaphoreType.DMA,
            pltpu.SemaphoreType.DMA((10,)),
            pltpu.SemaphoreType.DMA((10,)),
        ],
        cost_estimate=pl.CostEstimate(flops=0, bytes_accessed=0, transcendentals=0),
        compiler_params=pltpu.CompilerParams(collective_id=0, has_side_effects=True, vmem_limit_bytes=VMEM_LIMIT),
    )(rows)


REDUCE_PARTS = 11


def window_start(s):
    return jnp.minimum(s, 1) * (((s * SHARD + 64) // LANES128 - IN_ROWS) // 16 * 16)


LAST_WINDOW = ((3 * SHARD + 64) // LANES128 - IN_ROWS) // 16 * 16


def window_rows(dp_size):
    unit = REDUCE_PARTS * 16 * dp_size
    return -(-(SHARD // LANES128 + 17) // unit) * unit


CLASSES = ((0, 6), (6, 5))


def bit_order(bits, kind):
    order = list(range(bits))
    if kind and bits > 1:
        order[0], order[1] = 1, 0
    return order


def part_region(dp, rows, bits, kind, count):
    offset, size = 0, rows
    for k in bit_order(bits, kind)[:count]:
        size = size // 2
        offset = offset + bit_of(dp, k) * size
    return offset, size


def aligned(offset, size):
    return pl.ds(pl.multiple_of(offset, 16), size)


def zero_sum(rows, late, window, own, first, second, local_sem, send_sem, recv_sem):
    dp, zero = lax.axis_index("dp"), lax.axis_index("zero")
    core, across = (dp, flip(zero, 0)), (dp, flip(zero, 1))
    low, high = bit_of(zero, 0), bit_of(zero, 1)
    parts = range(REDUCE_PARTS)

    def local(h, part):
        source = late.at[aligned(window_start(2 * h + low) + part * rows, rows)]
        return pltpu.make_async_copy(source, own.at[part, h], local_sem.at[h, part])

    def flight(step, part):
        if step < 2:
            source = late.at[aligned(window_start(2 * step + 1 - low) + part * rows, rows)]
            target, device = first.at[part, step], core
        else:
            source, target, device = own.at[part, 1 - high], second.at[part], across
        return pltpu.make_async_remote_copy(source, target, send_sem.at[step, part], recv_sem.at[step, part],
                                            device_id=device, device_id_type=MESH)

    def begin():
        greet([core, across])
        for part in parts:
            for h in range(2):
                flight(h, part).start()
                local(h, part).start()

    def receive(step, part):
        if step == 1:
            for h in range(2):
                local(h, part).wait()
                flight(h, part).wait_recv()
            for h in range(2):
                own[part, h] = (own[part, h].astype(F32) + first[part, h].astype(F32)).astype(BF16)
            flight(2, part).start()
        else:
            flight(2, part).wait_recv()
            window[part] = (own[part, high].astype(F32) + second[part].astype(F32)).astype(BF16)

    def finish():
        for part in parts:
            for step in range(3):
                flight(step, part).wait_send()

    return begin, receive, finish


LATE_HOP = 12.0
HOP = 1.5


def arrival_order(chains, hops):
    free, order = {}, []
    pending = [(0.0, index, 0) for index in range(len(chains))]
    while pending:
        pending.sort()
        start, index, step = pending.pop(0)
        link, span = chains[index][step]
        end = max(start, free.get(link, 0.0)) + span
        free[link] = end
        hop = hops[index]
        order.append((end + hop, index, step))
        if step + 1 < len(chains[index]):
            pending.append((end + hop, index, step + 1))
    return sorted(order)


SLOTS = (((0, 0), 0.13), ((0, 2), 0.4), ((1, 2), 0.7), ((3, 2), 1.0))


def receive_slots(step_us):
    chains = [[("core", 0.8), ("x", 40.0 / REDUCE_PARTS)]] * REDUCE_PARTS
    ends = [(step + done) * step_us for step in range(LANE_STEPS) for _, done in SLOTS]
    table = [[] for _ in ends]
    place = 0
    for at, part, step in arrival_order(chains, [HOP] * len(chains)):
        while place + 1 < len(ends) and ends[place] < at:
            place += 1
        table[place].append((step + 1, part))
    return table


def attend_back_kernel(rows, q_t, k_n, k_t, v_n, grad_t, log_total, delta, late, dq_t, dk_t, dv_t, window,
                       own, first, second, local_sem, send_sem, recv_sem):
    begin, receive, finish = zero_sum(rows, late, window, own, first, second, local_sem, send_sem, recv_sem)
    step = pl.program_id(0) * KV_HEADS + pl.program_id(1)
    table = receive_slots(8.6)
    pl.when(step == 0)(begin)
    dq_t[...] = jnp.zeros_like(dq_t)

    def advance(slot):
        for place in range(slot, len(table), len(SLOTS)):
            if table[place]:

                @pl.when(step == place // len(SLOTS))
                def _():
                    for receipt in table[place]:
                        receive(*receipt)

    for block in range(BLOCKS):
        keys = pl.ds(block * BLOCK, BLOCK)
        k_rows, v_rows, k_cols = k_n[0, 0, keys, :], v_n[0, 0, keys, :], k_t[0, :, keys]
        dk = jnp.zeros((HEAD_DIM, BLOCK), F32)
        dv = jnp.zeros((HEAD_DIM, BLOCK), F32)
        for r in range(GROUP):
            head = slice(r * HEAD_DIM, (r + 1) * HEAD_DIM)
            for part in range(block, BLOCKS):
                cols = pl.ds(part * BLOCK, BLOCK)
                query, grad = q_t[0, head, cols], grad_t[0, head, cols]
                logs = log_total[0, 0, r : r + 1, cols]
                prob = jnp.exp2(dot(k_rows, query, 1, 0) * EXP_SCALE - logs)
                if part == block:
                    prob = causal_tile(prob, 0.0)
                grad_prob = dot(v_rows, grad, 1, 0) - delta[0, 0, r : r + 1, cols]
                grad_score = (prob * grad_prob).astype(BF16)
                dv += dot(grad, prob.astype(BF16), 1, 1)
                dk += dot(query, grad_score, 1, 1)
                dq_t[0, head, cols] += dot(k_cols, grad_score, 1, 0) * SCALE
            for slot, (after, _) in enumerate(SLOTS):
                if after == (block, r) and r + 1 < GROUP:
                    advance(slot)
        dk_t[0, :, keys] = dk * SCALE
        dv_t[0, :, keys] = dv
        for slot, (after, _) in enumerate(SLOTS):
            if after == (block, GROUP - 1):
                advance(slot)
    pl.when(step == LANE_STEPS - 1)(finish)


LANE_STEPS = 2 * KV_HEADS


def attend_back(q_t, k_n, k_t, v_n, grad_t, log_total, delta, late, dp_size):
    lanes = q_t.shape[0]
    rows = window_rows(dp_size) // REDUCE_PARTS
    shape = jax.ShapeDtypeStruct
    group_rows = lambda lane, g: (lane, g, 0)
    group_heads = lambda lane, g: (lane, g, 0, 0)
    held = lambda *dims: pltpu.VMEM((REDUCE_PARTS, *dims, LANES128), BF16)
    return pl.pallas_call(
        functools.partial(attend_back_kernel, rows),
        name="attend_back",
        grid=(lanes, KV_HEADS),
        in_specs=[
            pl.BlockSpec((1, GROUP * HEAD_DIM, LANE), group_rows),
            pl.BlockSpec((1, 1, LANE, HEAD_DIM), group_heads),
            pl.BlockSpec((1, HEAD_DIM, LANE), group_rows),
            pl.BlockSpec((1, 1, LANE, HEAD_DIM), group_heads),
            pl.BlockSpec((1, GROUP * HEAD_DIM, LANE), group_rows),
            pl.BlockSpec((1, 1, GROUP, LANE), group_heads),
            pl.BlockSpec((1, 1, GROUP, LANE), group_heads),
            pl.BlockSpec(memory_space=pl.ANY),
        ],
        out_specs=[
            pl.BlockSpec((1, GROUP * HEAD_DIM, LANE), group_rows),
            pl.BlockSpec((1, HEAD_DIM, LANE), group_rows),
            pl.BlockSpec((1, HEAD_DIM, LANE), group_rows),
            whole((REDUCE_PARTS, rows, LANES128)),
        ],
        out_shape=[
            shape((lanes, WIDTH_Q, LANE), F32),
            shape((lanes, WIDTH_K, LANE), F32),
            shape((lanes, WIDTH_K, LANE), F32),
            shape((REDUCE_PARTS, rows, LANES128), BF16),
        ],
        scratch_shapes=[
            held(2, rows),
            held(2, rows),
            held(rows),
            pltpu.SemaphoreType.DMA((2, REDUCE_PARTS)),
            pltpu.SemaphoreType.DMA((3, REDUCE_PARTS)),
            pltpu.SemaphoreType.DMA((3, REDUCE_PARTS)),
        ],
        compiler_params=pltpu.CompilerParams(collective_id=1, has_side_effects=True, vmem_limit_bytes=VMEM_LIMIT),
    )(q_t, k_n, k_t, v_n, grad_t, log_total, delta, late)


TAIL_AT = 4368


HEAD_PARTS = 3
HEAD_HOP = 3.0
LATE_GROUPS = ((0, 0, 3), (1, 0, 3), (0, 3, 3), (1, 3, 2))


def head_rows(dp_size):
    unit = 2 * HEAD_PARTS * 16 * 2 * dp_size
    return -(-(TAIL_AT + 16) // unit) * unit


def sum_head_kernel(bits, rows, late_rows, source, gain_rows, share_one, share_two, result, late_sum, total, *rest):
    received, (load_sem, send_sem, recv_sem, late_send, late_recv) = rest[:-5], rest[-5:]
    dp, zero = lax.axis_index("dp"), lax.axis_index("zero")
    axes = [("zero", 1)] + [("dp", k) for k in range(bits)]

    def partner(axis, k):
        return (flip(dp, k), zero) if axis == "dp" else (dp, flip(zero, k))

    def bit(axis, k):
        return bit_of(dp if axis == "dp" else zero, k)

    load = pltpu.make_async_copy(source, total, load_sem)
    load.start()
    load.wait()
    total[TAIL_AT : TAIL_AT + 16] = gain_rows[...]
    greet([partner("zero", 0)] + [partner(*axis) for axis in axes])

    def step(index, slot, source_ref, target_ref, axis):
        copy = pltpu.make_async_remote_copy(source_ref, target_ref, send_sem.at[index, slot], recv_sem.at[index, slot],
                                            device_id=partner(*axis), device_id_type=MESH)
        copy.start()
        return copy

    def order_of(index):
        return [("zero", 0)] + [axes[(index + j) % len(axes)] for j in range(len(axes))]

    def spans_of(index):
        spans = [(axis, 0.5 if axis == ("zero", 0) else 9.0 / HEAD_PARTS / (1 << slot)) for slot, axis in enumerate(order_of(index))]
        return spans + spans[::-1]

    def chain_of(index):
        order = order_of(index)
        size = rows // HEAD_PARTS
        offset = index * size
        regions = []
        for slot, axis in enumerate(order):
            half = size // 2
            mine, other = offset + bit(*axis) * half, offset + (1 - bit(*axis)) * half
            landing = received[slot].at[index]
            yield step(index, slot, total.at[aligned(other, half)], landing, axis)
            at = aligned(mine, half)
            target = total if slot + 1 < len(order) else result
            target[at] = (total[at].astype(F32) + landing[...].astype(F32)).astype(BF16)
            offset, size = mine, half
            regions.append(at)
        for slot in reversed(range(len(order))):
            place = result.at[regions[slot]]
            yield step(index, 2 * len(order) - 1 - slot, place, place, order[slot])

    def late_spans(index):
        kind, _, count = LATE_GROUPS[index]
        spans = [(("dp", k), 20.0 / (1 << slot) * count / REDUCE_PARTS) for slot, k in enumerate(bit_order(bits, kind))]
        return spans[::-1]

    def late_chain(index):
        kind, start, count = LATE_GROUPS[index]
        parts = pl.ds(CLASSES[kind][0] + start, count)
        share = (share_one, share_two)[kind]
        late_sum[parts, aligned(*part_region(dp, late_rows, bits, kind, bits))] = share[start : start + count]
        for slot, k in reversed(list(enumerate(bit_order(bits, kind)))):
            place = late_sum.at[parts, aligned(*part_region(dp, late_rows, bits, kind, slot + 1))]
            copy = pltpu.make_async_remote_copy(place, place, late_send.at[index, slot], late_recv.at[index, slot],
                                                device_id=partner("dp", k), device_id_type=MESH)
            copy.start()
            yield copy

    chains = [chain_of(i) for i in range(HEAD_PARTS)] + [late_chain(i) for i in range(len(LATE_GROUPS))]
    spans = [spans_of(i) for i in range(HEAD_PARTS)] + [late_spans(i) for i in range(len(LATE_GROUPS))]
    flying = [next(chain) for chain in chains]
    sent = list(flying)
    for _, index, _ in arrival_order(spans, [HEAD_HOP] * HEAD_PARTS + [LATE_HOP] * len(LATE_GROUPS)):
        flying[index].wait_recv()
        following = next(chains[index], None)
        if following is not None:
            flying[index] = following
            sent.append(following)
    for copy in sent:
        copy.wait_send()


def sum_head(source, gain_rows, shares, late_rows, dp_size):
    bits = dp_size.bit_length() - 1
    rows = source.shape[0]
    steps = bits + 2
    shape = jax.ShapeDtypeStruct
    return pl.pallas_call(
        functools.partial(sum_head_kernel, bits, rows, late_rows),
        name="sum_head",
        out_shape=[shape((rows, LANES128), BF16), shape((REDUCE_PARTS, late_rows, LANES128), BF16)],
        in_specs=[pl.BlockSpec(memory_space=pl.ANY)] + [pl.BlockSpec(memory_space=pltpu.VMEM)] * 3,
        out_specs=[pl.BlockSpec(memory_space=pltpu.VMEM)] * 2,
        scratch_shapes=[
            pltpu.VMEM((rows, LANES128), BF16),
            *[pltpu.VMEM((HEAD_PARTS, rows // HEAD_PARTS >> (k + 1), LANES128), BF16) for k in range(steps)],
            pltpu.SemaphoreType.DMA,
            pltpu.SemaphoreType.DMA((HEAD_PARTS, 2 * steps)),
            pltpu.SemaphoreType.DMA((HEAD_PARTS, 2 * steps)),
            pltpu.SemaphoreType.DMA((len(LATE_GROUPS), bits)),
            pltpu.SemaphoreType.DMA((len(LATE_GROUPS), bits)),
        ],
        compiler_params=pltpu.CompilerParams(collective_id=2, has_side_effects=True, vmem_limit_bytes=VMEM_LIMIT),
    )(source, gain_rows, *shares)


def flat_rows(g_in, rows):
    flat = g_in[:, :QKVG].astype(BF16).reshape(-1)
    return jnp.pad(flat, (0, rows * LANES128 - SPLIT_AT)).reshape(rows, LANES128)


def pack_gains(g_gain_one, g_gain_two, g_head):
    flat = jnp.concatenate([g_gain_one[0], g_gain_two[0], g_head.reshape(-1)]).astype(BF16)
    return jnp.pad(flat.reshape(10, LANES128), ((0, 6), (0, 0)))


def unpack_shard(late, head, zero_rank):
    late = late.reshape(-1)
    head_flat = head.reshape(-1)
    starts = [s * SHARD - SPLIT_AT - LANES128 * max(0, ((s * SHARD + 64) // LANES128 - IN_ROWS) // 16 * 16) for s in range(1, 4)]
    tail = head_flat[TAIL_AT * LANES128 : (TAIL_AT + 10) * LANES128]

    def pick(s):
        if s == 0:
            return lambda: jnp.concatenate([head_flat[:SPLIT_AT], late[: SHARD - SPLIT_AT]])
        if s == 3:
            return lambda: jnp.concatenate([late[starts[2] : starts[2] + SHARD - 10 * LANES128], tail])
        return lambda: late[starts[s - 1] : starts[s - 1] + SHARD]

    return lax.switch(zero_rank, [pick(s) for s in range(4)]).astype(F32)


UNPACK_SKEW = (EDGE + IN_ROWS) % 16


def unpack_kernel(own, near, far, both, w_out, w_mlp, w_down, packed, edges, stage, pair_rows, load_sem, edge_sem):
    zero = lax.axis_index("zero")
    shards = [(own, zero), (near, flip(zero, 0)), (far, flip(zero, 1)), (both, flip(flip(zero, 0), 1))]
    loads = [
        pltpu.make_async_copy(shard.at[pl.ds(EDGE, BODY)], packed.at[pl.ds(pl.multiple_of(STEP * s + EDGE, 16), BODY)], load_sem.at[k])
        for k, (shard, s) in enumerate(shards)
    ]
    ends = [pltpu.make_async_copy(shard.at[pl.ds(at, EDGE)], edges.at[s, h], edge_sem.at[k, h])
            for k, (shard, s) in enumerate(shards) for h, at in enumerate((0, EDGE + BODY))]
    for copy in ends + loads:
        copy.start()
    for copy in ends:
        copy.wait()
    packed[:EDGE] = edges[0, 0]
    for s in range(4):
        tile = edges[s, 1].astype(F32)
        if s < 3:
            tile = tile + edges[s + 1, 0].astype(F32)
        packed[pl.ds(STEP * (s + 1), EDGE), :] = tile.astype(BF16)
    for copy in loads:
        copy.wait()

    def fetch(first_row, count):
        stage[: count + 16] = packed[pl.ds(pl.multiple_of(first_row - UNPACK_SKEW, 16), count + 16), :].astype(F32)

    def split_pairs(first_row, target, row):
        fetch(first_row, PAIR_ROWS)
        tiles = [stage[pl.ds(UNPACK_SKEW + t, PAIR_STEP, stride=9), :] for t in range(9)]
        even, odd = pl.ds(0, PAIR_STEP, stride=2), pl.ds(1, PAIR_STEP, stride=2)
        for t in range(4):
            pair_rows[t, even, :] = tiles[t]
        pair_rows[4, even, :] = tiles[4]
        for t in range(4):
            pair_rows[t, odd, :] = jnp.concatenate([tiles[4 + t][:, 64:], tiles[5 + t][:, :64]], axis=1)
        pair_rows[4, odd, :] = jnp.concatenate([tiles[8][:, 64:], tiles[8][:, :64]], axis=1)
        at = pl.ds(pl.multiple_of(row, 2 * PAIR_STEP), 2 * PAIR_STEP)
        for t in range(4):
            target[at, t * 128 : (t + 1) * 128] = pair_rows[t].astype(BF16)
        target[at, 512:] = pair_rows[4, :, :64].astype(BF16)

    out_at = EDGE + IN_ROWS
    mlp_at = out_at + OUT_ROWS
    down_at = mlp_at + MLP_ROWS

    @pl.loop(0, WIDTH_Q // (2 * PAIR_STEP))
    def _(piece):
        split_pairs(out_at + piece * PAIR_ROWS, w_out, piece * 2 * PAIR_STEP)

    @pl.loop(0, FF // (2 * PAIR_STEP))
    def _(piece):
        split_pairs(down_at + piece * PAIR_ROWS, w_down, piece * 2 * PAIR_STEP)

    @pl.loop(0, D // WIDE_STEP)
    def _(piece):
        fetch(mlp_at + piece * WIDE_STEP * WIDE_TILES, WIDE_STEP * WIDE_TILES)
        rows = pl.ds(pl.multiple_of(piece * WIDE_STEP, WIDE_STEP), WIDE_STEP)
        for tile in range(WIDE_TILES):
            w_mlp[rows, tile * 128 : (tile + 1) * 128] = stage[pl.ds(UNPACK_SKEW + tile, WIDE_STEP, stride=WIDE_TILES), :].astype(BF16)


def unpack_weights(shards):
    shape = jax.ShapeDtypeStruct
    return pl.pallas_call(
        unpack_kernel,
        name="unpack_weights",
        in_specs=[pl.BlockSpec(memory_space=pl.ANY)] * 4,
        out_shape=[shape((WIDTH_Q, D), BF16), shape((D, 2 * FF), BF16), shape((FF, D), BF16)],
        scratch_shapes=[
            pltpu.VMEM((3 * STEP + SPAN, LANES128), BF16),
            pltpu.VMEM((4, 2, EDGE, LANES128), BF16),
            pltpu.VMEM((WIDE_STEP * WIDE_TILES + 16, 128), F32),
            pltpu.VMEM((5, 2 * PAIR_STEP, 128), F32),
            pltpu.SemaphoreType.DMA((4,)),
            pltpu.SemaphoreType.DMA((4, 2)),
        ],
        cost_estimate=pl.CostEstimate(flops=0, bytes_accessed=0, transcendentals=0),
        compiler_params=pltpu.CompilerParams(vmem_limit_bytes=VMEM_LIMIT),
    )(*shards)


def column_parts(lanes_t, dp_size):
    seqs, width, columns = lanes_t.shape
    return lanes_t.reshape(seqs, width, dp_size, columns // dp_size).transpose(2, 0, 1, 3)


def spread(parts):
    return lax.all_to_all(parts, "dp", split_axis=0, concat_axis=0, tiled=True)


def regroup(parts, order):
    dp_size, seqs, width, columns = parts.shape
    parts = jnp.take(parts.reshape(dp_size * seqs, width, columns), order, axis=0, mode="clip")
    return lax.all_to_all(parts.reshape(dp_size, seqs, width, columns), "dp", split_axis=0, concat_axis=0, tiled=True)


def joined(parts):
    dp_size, seqs, width, rows = parts.shape
    return parts.transpose(1, 2, 0, 3).reshape(seqs, width, dp_size * rows)


def exchange(values, axis, bit):
    return lax.ppermute(values, axis, [(i, i ^ (1 << bit)) for i in range(lax.axis_size(axis))])


def quarter(parts, dp_rank, order):
    size = parts.shape[1] // 4

    def rows_of(flips):
        first, second = (bit_of(dp_rank, bit) ^ flip for bit, flip in zip(order, flips))
        return lax.dynamic_slice_in_dim(parts, first * (2 * size) + second * size, size, 1)

    def sent(flips):
        mask = sum(flip << bit for bit, flip in zip(order, flips))
        return lax.ppermute(rows_of(flips), "dp", [(i, i ^ mask) for i in range(lax.axis_size("dp"))])

    return [rows_of((0, 0)), sent((1, 0)), sent((0, 1)), sent((1, 1))]


def halve(parts, dp_rank, bit):
    half = parts.shape[1] // 2
    mine = bit_of(dp_rank, bit)
    sent = lax.dynamic_slice_in_dim(parts, (1 - mine) * half, half, 1)
    return [lax.dynamic_slice_in_dim(parts, mine * half, half, 1), exchange(sent, "dp", bit)]


def added(pieces):
    return sum(piece.astype(F32) for piece in pieces).astype(BF16)


def unpack_first(first_rows, last_rows):
    w_in = first_rows[EDGE : EDGE + IN_ROWS].reshape(-1)[:SPLIT_AT].reshape(D, QKVG)
    w_in = jnp.pad(w_in, ((0, 0), (0, QKVG_PAD - QKVG)))
    rows = last_rows[GAIN_AT : GAIN_AT + 10].astype(F32)
    return w_in, rows[:9].reshape(2, D), rows[9].reshape(2, HEAD_DIM)


def local(tokens, cotangent, lengths, balance, master, moment_one, moment_two):
    dp_rank, zero_rank = lax.axis_index("dp"), lax.axis_index("zero")
    dp_size, zero_size = lax.axis_size("dp"), lax.axis_size("zero")
    seqs = tokens.shape[0]
    order = lax.dynamic_index_in_dim(balance, zero_rank, 0, keepdims=False)
    inverse = jnp.zeros_like(order).at[order].set(jnp.arange(order.shape[0], dtype=order.dtype))
    lens = lax.dynamic_slice_in_dim(lengths, (dp_rank * zero_size + zero_rank) * seqs, seqs)
    tokens_t = tokens.swapaxes(1, 2)
    cot_parts = spread(column_parts(cotangent.swapaxes(1, 2), dp_size))
    own, first_rows, last_rows = pack_master(master)
    far, near = exchange(own, "zero", 1), exchange(own, "zero", 0)
    first = unpack_first(first_rows, last_rows)
    att_t, gate, kept = layer_forward(tokens_t, lens, first)
    far, near, att_t, cot_parts = lax.optimization_barrier((far, near, att_t, cot_parts))
    both = exchange(far, "zero", 0)
    cot_here = regroup(cot_parts, inverse)
    w_out, w_mlp, w_down = unpack_weights((own, near, far, both))
    w_in, gains, head_gains = first
    gain_cols, head_gains = gains[:, :, None], head_gains[:, :, None]
    out_columns, *stash = mlp(lens, att_t, gate, tokens_t, gains, w_out, w_mlp, w_down, dp_size)
    output_parts = spread(out_columns)
    grad_hidden_t, grad_att_t, logit_delta, late, g_gain_two = mlp_back(
        lens, att_t, gate, cot_here, *stash, gains, w_out, w_mlp, w_down, LAST_WINDOW + window_rows(dp_size))
    output_parts, grad_att_t = lax.optimization_barrier((output_parts, grad_att_t))
    output_parts = regroup(output_parts, order)
    q_t, k_n, k_t, v_n, log_total, raw = kept
    dq_t, dk_t, dv_t, window = attend_back(
        q_t, k_n, k_t, v_n, grad_att_t, head_groups(log_total), head_groups(logit_delta[:, 16:]), late, dp_size)
    output_parts, dq_t = lax.optimization_barrier((output_parts, dq_t))
    dp_bits = dp_size.bit_length() - 1
    orders = [bit_order(dp_bits, kind) for kind in range(2)]
    pieces = [quarter(window[at : at + count], dp_rank, orders[kind][:2]) for kind, (at, count) in enumerate(CLASSES)]
    cosine, sine = (jnp.asarray(t) for t in rope_tables())
    grad_tokens_t, g_in, g_gain_one, g_head = project_back(
        lens, dq_t, dk_t, dv_t, logit_delta, raw, tokens_t, grad_hidden_t, w_in, gain_cols, head_gains, cosine, sine)
    pieces, g_in = lax.optimization_barrier((pieces, g_in))
    shares = [added(piece) for piece in pieces]
    head = flat_rows(g_in, head_rows(dp_size))
    gain_rows = pack_gains(g_gain_one, g_gain_two, g_head)
    for step in range(2, dp_bits):
        pieces = [halve(share, dp_rank, order[step]) for share, order in zip(shares, orders)]
        pieces, head, gain_rows = lax.optimization_barrier((pieces, head, gain_rows))
        shares = [added(piece) for piece in pieces]
    grad_tokens = grad_tokens_t.swapaxes(1, 2)
    head_sum, late_sum = sum_head(head, gain_rows, shares, window.shape[1], dp_size)
    output = joined(output_parts).swapaxes(1, 2)
    grad_shard = unpack_shard(late_sum, head_sum, zero_rank)
    gain_width = D // zero_size
    gain_sums = head_sum[TAIL_AT : TAIL_AT + 9].reshape(2, zero_size, gain_width)
    grad_gains = lax.dynamic_index_in_dim(gain_sums, zero_rank, 1, keepdims=False).astype(F32)
    next_one = BETA_ONE * moment_one + (1.0 - BETA_ONE) * grad_shard
    next_two = BETA_TWO * moment_two + (1.0 - BETA_TWO) * grad_shard * grad_shard
    update_dir = next_one / BIAS_ONE / jnp.sqrt(next_two / BIAS_TWO)
    return output, grad_tokens, grad_shard, update_dir, next_one, next_two, grad_gains


def solution(mesh):
    lanes = P(("dp", "zero"), None, None)
    return jax.shard_map(
        local,
        mesh=mesh,
        in_specs=(lanes, lanes, P(), P(), P("zero"), P("zero"), P("zero")),
        out_specs=(lanes, lanes, P("zero"), P("zero"), P("zero"), P("zero"), P(None, "zero")),
        check_vma=False,
    )
```

```python
import functools
import math

import jax
import jax.numpy as jnp
import numpy as np
from jax import lax
from jax.experimental import pallas as pl
from jax.experimental.pallas import tpu as pltpu
from jax.sharding import PartitionSpec as P

D = 576
HEADS = 9
KV_HEADS = 3
GROUP = HEADS // KV_HEADS
HEAD_DIM = 64
HALF = HEAD_DIM // 2
FF = 1536
LANE = 1024
QKVG = 969
QKVG_PAD = 1024
WIDTH_Q = HEADS * HEAD_DIM
WIDTH_K = KV_HEADS * HEAD_DIM
PARAMS = 3545408
EPSILON = 1e-05
ROPE_BASE = 100000.0
BETA_ONE = 0.9
BETA_TWO = 0.95
BIAS_ONE = 1.0 - BETA_ONE**10
BIAS_TWO = 1.0 - BETA_TWO**10
SCALE = HEAD_DIM ** (-0.5)
EXP_SCALE = SCALE * math.log2(math.e)
F32 = jnp.float32
BF16 = jnp.bfloat16
BLOCK = 256
BLOCKS = LANE // BLOCK
FF_CHUNK = 768
MLP_BLOCK = 512
MLP_BLOCKS = LANE // MLP_BLOCK
PROJ_BLOCK = 512
PROJ_BLOCKS = LANE // PROJ_BLOCK
VMEM_LIMIT = 60 * 1024 * 1024


def dot(a, b, ca, cb):
    return lax.dot_general(a, b, (((ca,), (cb,)), ((), ())), preferred_element_type=F32)


def rope_tables():
    frequency = ROPE_BASE ** (-(np.arange(HALF, dtype=np.float32) * np.float32(2.0)) / np.float32(HEAD_DIM))
    angles = np.arange(LANE, dtype=np.float32)[None, :] * frequency.astype(np.float32)[:, None]
    return np.cos(angles).astype(np.float32), np.sin(angles).astype(np.float32)


def mean_square_scale(values, axis):
    return lax.rsqrt(jnp.mean(values * values, axis=axis, keepdims=True) + EPSILON)


def block_spec(shape, index):
    return pl.BlockSpec(shape, index)


def whole(shape):
    return pl.BlockSpec(shape, lambda *_: (0,) * len(shape), pipeline_mode=pl.Buffered(1))


def full_col_map(lane, block, lens):
    return (lane, 0, block)


def last_block(lens, lane, block):
    return jnp.minimum(block, (lens[lane] - 1) // BLOCK)


def project_kernel(lens, tok_t, w_in, gain_cols, head_gains, cosine, sine, q_t, k_n, k_t, v_n, v_t, raw, gate, w_in_t):
    lane, block = pl.program_id(0), pl.program_id(1)

    @pl.when((lane == 0) & (block == 0))
    def _():
        w_in_t[...] = w_in[...].T

    @pl.when(block * PROJ_BLOCK < lens[lane])
    def _():
        x = tok_t[0].astype(F32)
        normed = (x * mean_square_scale(x, 0) * gain_cols[0]).astype(BF16)
        projected = dot(w_in_t[...], normed, 1, 0)
        raw[0] = projected[: WIDTH_Q + WIDTH_K]
        cos, sin = cosine[...], sine[...]
        for head in range(HEADS + KV_HEADS):
            u = projected[head * HEAD_DIM : (head + 1) * HEAD_DIM]
            y = u * mean_square_scale(u, 0) * head_gains[0 if head < HEADS else 1]
            y1, y2 = y[:HALF], y[HALF:]
            turned = jnp.concatenate([y1 * cos - y2 * sin, y2 * cos + y1 * sin], axis=0)
            if head < HEADS:
                q_t[0, head * HEAD_DIM : (head + 1) * HEAD_DIM] = turned.astype(BF16)
            else:
                k = head - HEADS
                k_t[0, k * HEAD_DIM : (k + 1) * HEAD_DIM] = turned.astype(BF16)
                k_n[0, k] = turned.T.astype(BF16)
        values = projected[WIDTH_Q + WIDTH_K : WIDTH_Q + 2 * WIDTH_K]
        v_t[0] = values.astype(BF16)
        for k in range(KV_HEADS):
            v_n[0, k] = values[k * HEAD_DIM : (k + 1) * HEAD_DIM].T.astype(BF16)
        gate[0] = projected[WIDTH_Q + 2 * WIDTH_K : WIDTH_Q + 2 * WIDTH_K + 16]

    @pl.when(block * PROJ_BLOCK >= lens[lane])
    def _():
        for ref in (q_t, k_n, k_t, v_n, v_t):
            ref[...] = jnp.zeros_like(ref)


def col_map(lane, block, lens):
    return (lane, 0, last_block(lens, lane, block))


def mlp_row_map(lane, block, lens):
    return (lane, jnp.minimum(block, (lens[lane] - 1) // MLP_BLOCK), 0)


def mlp_col_map(lane, block, lens):
    return (lane, 0, jnp.minimum(block, (lens[lane] - 1) // MLP_BLOCK))


def proj_col_map(lane, block, lens):
    return (lane, 0, jnp.minimum(block, (lens[lane] - 1) // PROJ_BLOCK))


def proj_table_map(lane, block, lens):
    return (0, jnp.minimum(block, (lens[lane] - 1) // PROJ_BLOCK))


def full_head_map(lane, block, lens):
    return (lane, 0, block, 0)


def project(lens, tokens_t, w_in, gain_cols, head_gains, cosine, sine):
    lanes = tokens_t.shape[0]
    shape = jax.ShapeDtypeStruct
    return pl.pallas_call(
        project_kernel,
        name="project",
        grid_spec=pltpu.PrefetchScalarGridSpec(
            num_scalar_prefetch=1,
            grid=(lanes, PROJ_BLOCKS),
            in_specs=[
                pl.BlockSpec((1, D, PROJ_BLOCK), proj_col_map),
                whole((D, QKVG_PAD)),
                whole((2, D, 1)),
                whole((2, HEAD_DIM, 1)),
                pl.BlockSpec((HALF, PROJ_BLOCK), proj_table_map),
                pl.BlockSpec((HALF, PROJ_BLOCK), proj_table_map),
            ],
            out_specs=[
                pl.BlockSpec((1, WIDTH_Q, PROJ_BLOCK), full_col_map),
                pl.BlockSpec((1, KV_HEADS, PROJ_BLOCK, HEAD_DIM), full_head_map),
                pl.BlockSpec((1, WIDTH_K, PROJ_BLOCK), full_col_map),
                pl.BlockSpec((1, KV_HEADS, PROJ_BLOCK, HEAD_DIM), full_head_map),
                pl.BlockSpec((1, WIDTH_K, PROJ_BLOCK), full_col_map),
                pl.BlockSpec((1, WIDTH_Q + WIDTH_K, PROJ_BLOCK), proj_col_map),
                pl.BlockSpec((1, 16, PROJ_BLOCK), proj_col_map),
            ],
            scratch_shapes=[pltpu.VMEM((QKVG_PAD, D), BF16)],
        ),
        out_shape=[
            shape((lanes, WIDTH_Q, LANE), BF16),
            shape((lanes, KV_HEADS, LANE, HEAD_DIM), BF16),
            shape((lanes, WIDTH_K, LANE), BF16),
            shape((lanes, KV_HEADS, LANE, HEAD_DIM), BF16),
            shape((lanes, WIDTH_K, LANE), BF16),
            shape((lanes, WIDTH_Q + WIDTH_K, LANE), F32),
            shape((lanes, 16, LANE), F32),
        ],
        cost_estimate=pl.CostEstimate(flops=0, bytes_accessed=0, transcendentals=0),
        compiler_params=pltpu.CompilerParams(vmem_limit_bytes=VMEM_LIMIT),
    )(lens, tokens_t, w_in, gain_cols, head_gains, cosine, sine)


def causal_tile(values, fill):
    key_pos = lax.broadcasted_iota(jnp.int32, values.shape, 0)
    query_pos = lax.broadcasted_iota(jnp.int32, values.shape, 1)
    return jnp.where(key_pos <= query_pos, values, fill)


def attend_kernel(lens, q_t, k_n, v_t, out_t, log_total):
    lane, block = pl.program_id(0), pl.program_id(1)
    log_total[0] = jnp.zeros((16, BLOCK), F32)

    for level in range(BLOCKS):

        @pl.when((block == level) & (level * BLOCK < lens[lane]))
        def _():
            before = level * BLOCK
            for head in range(HEADS):
                g = head // GROUP
                query = q_t[0, head * HEAD_DIM : (head + 1) * HEAD_DIM]
                values = v_t.at[0, g * HEAD_DIM : (g + 1) * HEAD_DIM]
                weights = jnp.exp2(dot(k_n[0, g, before : before + BLOCK], query, 1, 0) * EXP_SCALE)
                weights = causal_tile(weights, 0.0)
                total = jnp.sum(weights, axis=0, keepdims=True)
                mixed = dot(values[:, before : before + BLOCK], weights.astype(BF16), 1, 0)
                if before:
                    weights = jnp.exp2(dot(k_n[0, g, :before], query, 1, 0) * EXP_SCALE)
                    total += jnp.sum(weights, axis=0, keepdims=True)
                    mixed += dot(values[:, :before], weights.astype(BF16), 1, 0)
                out_t[0, head * HEAD_DIM : (head + 1) * HEAD_DIM] = mixed * (1.0 / total)
                log_total[0, head : head + 1] = jnp.log2(total)


def attend(lens, q_t, k_n, v_t):
    lanes = q_t.shape[0]
    shape = jax.ShapeDtypeStruct
    return pl.pallas_call(
        attend_kernel,
        name="attend",
        grid_spec=pltpu.PrefetchScalarGridSpec(
            num_scalar_prefetch=1,
            grid=(lanes, BLOCKS),
            in_specs=[
                pl.BlockSpec((1, WIDTH_Q, BLOCK), col_map),
                pl.BlockSpec((1, KV_HEADS, LANE, HEAD_DIM), lambda lane, block, lens: (lane, 0, 0, 0)),
                pl.BlockSpec((1, WIDTH_K, LANE), lambda lane, block, lens: (lane, 0, 0)),
            ],
            out_specs=[
                pl.BlockSpec((1, WIDTH_Q, BLOCK), col_map),
                pl.BlockSpec((1, 16, BLOCK), full_col_map),
            ],
        ),
        out_shape=[
            shape((lanes, WIDTH_Q, LANE), F32),
            shape((lanes, 16, LANE), F32),
        ],
        cost_estimate=pl.CostEstimate(flops=0, bytes_accessed=0, transcendentals=0),
        compiler_params=pltpu.CompilerParams(vmem_limit_bytes=VMEM_LIMIT),
    )(lens, q_t, k_n, v_t)


OUT_ROWS = WIDTH_Q * D // 128
MLP_ROWS = D * 2 * FF // 128
DOWN_ROWS = FF * D // 128
LATE_ROWS = OUT_ROWS + MLP_ROWS + DOWN_ROWS
WIDE_TILES = 2 * FF // 128
WIDE_STEP = 48
PAIR_STEP = 32
PAIR_ROWS = PAIR_STEP * 9


def pack_wide(source, target, stage, first_row):
    @pl.loop(0, D // WIDE_STEP)
    def _(piece):
        rows = pl.ds(pl.multiple_of(piece * WIDE_STEP, WIDE_STEP), WIDE_STEP)
        for tile in range(WIDE_TILES):
            stage[pl.ds(tile, WIDE_STEP, stride=WIDE_TILES), :] = source[rows, tile * 128 : (tile + 1) * 128]
        size = WIDE_STEP * WIDE_TILES
        target[pl.ds(pl.multiple_of(first_row + piece * size, 16), size), :] = stage[:size].astype(BF16)


def set_tiles(target, value):
    for t in range(4):
        target[t] = value[:, t * 128 : (t + 1) * 128]
    target[4, :, :64] = value[:, 512:]


def pack_pairs(rows_ref, stage):
    tiles = [rows_ref[t, pl.ds(parity, PAIR_STEP, stride=2), :] for parity in range(2) for t in range(5)]
    even, odd = tiles[:5], tiles[5:]
    for t in range(4):
        stage[pl.ds(t, PAIR_STEP, stride=9), :] = even[t]
    stage[pl.ds(4, PAIR_STEP, stride=9), :] = jnp.concatenate([even[4][:, :64], odd[0][:, :64]], axis=1)
    for t in range(4):
        right = odd[t + 1][:, :64]
        stage[pl.ds(5 + t, PAIR_STEP, stride=9), :] = jnp.concatenate([odd[t][:, 64:], right], axis=1)


def mlp_kernel(lens, att_t, gate, tok_t, gains, w_out, w_mlp, w_down, out_parts, hidden_in, act_low, gate_slope, up_slope, total):
    lane, block = pl.program_id(0), pl.program_id(1)

    @pl.when(block * MLP_BLOCK >= lens[lane])
    def _():
        out_parts[...] = jnp.zeros_like(out_parts)

    @pl.when(block * MLP_BLOCK < lens[lane])
    def _():
        att = att_t[0].reshape(HEADS, HEAD_DIM, MLP_BLOCK)
        sig = jax.nn.sigmoid(gate[0, :HEADS])[:, None, :]
        gated_t = (att * sig).reshape(WIDTH_Q, MLP_BLOCK).astype(BF16)
        hidden = tok_t[0].T.astype(F32) + dot(gated_t, w_out[...], 0, 0)
        hidden_in[0] = hidden
        mixed = (hidden * mean_square_scale(hidden, 1) * gains[1:2]).astype(BF16)
        valid_t = lax.broadcasted_iota(jnp.int32, (1, MLP_BLOCK), 1) + block * MLP_BLOCK < lens[lane]
        total[...] = hidden

        @pl.loop(0, FF // FF_CHUNK, unroll=True)
        def _(chunk):
            low = pl.ds(pl.multiple_of(chunk * FF_CHUNK, FF_CHUNK), FF_CHUNK)
            high = pl.ds(pl.multiple_of(FF + chunk * FF_CHUNK, FF_CHUNK), FF_CHUNK)
            g = dot(mixed, w_mlp[:, low], 1, 0)
            u = dot(mixed, w_mlp[:, high], 1, 0)
            s = jax.nn.sigmoid(g)
            gs = g * s
            act = (gs * u).astype(BF16)
            total[...] += dot(act, w_down[low, :], 1, 0)
            act_low[0, :, low] = act
            gate_slope[0, :, low] = (u * (s * (1.0 + g * (1.0 - s)))).astype(BF16)
            up_slope[0, :, low] = gs.astype(BF16)

        out_t = jnp.where(valid_t, total[...].T, 0.0).astype(BF16)
        width = out_parts.shape[3]
        for part in range(out_parts.shape[0]):
            out_parts[part, 0] = out_t[:, part * width : (part + 1) * width]


def part_map(lane, block, lens):
    return (block, lane, 0, 0)


def kept_part_map(lane, block, lens):
    return (jnp.minimum(block, (lens[lane] - 1) // MLP_BLOCK), lane, 0, 0)


def mlp(lens, att_t, gate, tokens_t, gains, w_out, w_mlp, w_down, dp_size):
    lanes = tokens_t.shape[0]
    width = LANE // dp_size
    shape = jax.ShapeDtypeStruct
    return pl.pallas_call(
        mlp_kernel,
        name="mlp",
        grid_spec=pltpu.PrefetchScalarGridSpec(
            num_scalar_prefetch=1,
            grid=(lanes, MLP_BLOCKS),
            in_specs=[
                pl.BlockSpec((1, WIDTH_Q, MLP_BLOCK), mlp_col_map),
                pl.BlockSpec((1, 16, MLP_BLOCK), mlp_col_map),
                pl.BlockSpec((1, D, MLP_BLOCK), mlp_col_map),
                whole((2, D)),
                whole((WIDTH_Q, D)),
                whole((D, 2 * FF)),
                whole((FF, D)),
            ],
            out_specs=[
                pl.BlockSpec((dp_size // MLP_BLOCKS, 1, D, width), part_map),
                pl.BlockSpec((1, MLP_BLOCK, D), mlp_row_map),
                pl.BlockSpec((1, MLP_BLOCK, FF), mlp_row_map),
                pl.BlockSpec((1, MLP_BLOCK, FF), mlp_row_map),
                pl.BlockSpec((1, MLP_BLOCK, FF), mlp_row_map),
            ],
            scratch_shapes=[pltpu.VMEM((MLP_BLOCK, D), F32)],
        ),
        out_shape=[
            shape((dp_size, lanes, D, width), BF16),
            shape((lanes, LANE, D), F32),
            shape((lanes, LANE, FF), BF16),
            shape((lanes, LANE, FF), BF16),
            shape((lanes, LANE, FF), BF16),
        ],
        compiler_params=pltpu.CompilerParams(vmem_limit_bytes=VMEM_LIMIT),
    )(lens, att_t, gate, tokens_t, gains, w_out, w_mlp, w_down)


def mlp_back_kernel(lens, att_t, gate, cot_parts, hidden_in, act_low, gate_slope, up_slope, gains, w_out, w_mlp, w_down,
                    grad_hidden_t, grad_att_t, logit_delta, kept, sent, g_gain,
                    back, g_out, g_mlp, g_down_t, late, stage, pair_rows, copy_sem):
    lane, block = pl.program_id(0), pl.program_id(1)

    @pl.when((lane == 0) & (block == 0))
    def _():
        g_out[...] = jnp.zeros_like(g_out)
        g_mlp[...] = jnp.zeros_like(g_mlp)
        g_down_t[...] = jnp.zeros_like(g_down_t)
        g_gain[...] = jnp.zeros_like(g_gain)

    @pl.when(block * MLP_BLOCK >= lens[lane])
    def _():
        grad_att_t[...] = jnp.zeros_like(grad_att_t)
        logit_delta[...] = jnp.zeros_like(logit_delta)

    @pl.when(block * MLP_BLOCK < lens[lane])
    def _():
        att = att_t[0].reshape(HEADS, HEAD_DIM, MLP_BLOCK)
        sig = jax.nn.sigmoid(gate[0, :HEADS])[:, None, :]
        gated_t = (att * sig).reshape(WIDTH_Q, MLP_BLOCK).astype(BF16)
        hidden = hidden_in[0]
        scale = mean_square_scale(hidden, 1)
        gain = gains[1:2]
        mixed_t = (hidden * scale * gain).astype(BF16).T
        valid_t = lax.broadcasted_iota(jnp.int32, (1, MLP_BLOCK), 1) + block * MLP_BLOCK < lens[lane]
        cot_t = jnp.concatenate([cot_parts[part, 0] for part in range(cot_parts.shape[0])], axis=1)
        grad_low_t = jnp.where(valid_t, cot_t.astype(F32), 0.0).astype(BF16)
        grad_low = grad_low_t.T
        back[...] = jnp.zeros_like(back)

        @pl.loop(0, FF // FF_CHUNK, unroll=True)
        def _(chunk):
            low = pl.ds(pl.multiple_of(chunk * FF_CHUNK, FF_CHUNK), FF_CHUNK)
            high = pl.ds(pl.multiple_of(FF + chunk * FF_CHUNK, FF_CHUNK), FF_CHUNK)
            a = dot(grad_low, w_down[low, :], 1, 1)
            grad_gate = (a * gate_slope[0, :, low].astype(F32)).astype(BF16)
            grad_up = (a * up_slope[0, :, low].astype(F32)).astype(BF16)
            back[...] += dot(grad_gate, w_mlp[:, low], 1, 1) + dot(grad_up, w_mlp[:, high], 1, 1)
            g_mlp[:, low] += dot(mixed_t, grad_gate, 1, 0)
            g_mlp[:, high] += dot(mixed_t, grad_up, 1, 0)
            g_down_t[:, low] += dot(grad_low_t, act_low[0, :, low], 1, 0)

        b = back[...]
        g_gain[0:1] += jnp.sum(b * hidden * scale, axis=0, keepdims=True)
        bg = b * gain
        grad_h = grad_low.astype(F32) + scale * bg - hidden * (scale * scale * scale * jnp.mean(hidden * bg, axis=1, keepdims=True))
        grad_hidden_t[0] = grad_h.T
        branch = grad_h.astype(BF16)
        g_out[...] += dot(gated_t, branch, 1, 0)
        c = dot(w_out[...], branch, 1, 1).reshape(HEADS, HEAD_DIM, MLP_BLOCK)
        grad_att = (c * sig).astype(BF16)
        grad_att_t[0] = grad_att.reshape(WIDTH_Q, MLP_BLOCK)
        sig2 = sig[:, 0, :]
        logit_delta[0, :HEADS] = jnp.sum(c * att, axis=1) * (sig2 * (1.0 - sig2))
        logit_delta[0, 16 : 16 + HEADS] = jnp.sum(grad_att.astype(F32) * att, axis=1)

    @pl.when((lane == pl.num_programs(0) - 1) & (block == pl.num_programs(1) - 1))
    def _():
        @pl.loop(0, WIDTH_Q // (2 * PAIR_STEP))
        def _(piece):
            set_tiles(pair_rows, g_out[pl.ds(pl.multiple_of(piece * 2 * PAIR_STEP, 2 * PAIR_STEP), 2 * PAIR_STEP), :])
            pack_pairs(pair_rows, stage)
            late[pl.ds(pl.multiple_of(piece * PAIR_ROWS, 16), PAIR_ROWS), :] = stage[:PAIR_ROWS].astype(BF16)

        pack_wide(g_mlp, late, stage, OUT_ROWS)

        @pl.loop(0, FF // 128)
        def _(piece):
            turned = g_down_t[:, pl.ds(pl.multiple_of(piece * 128, 128), 128)].T
            for h in range(128 // (2 * PAIR_STEP)):
                set_tiles(pair_rows, turned[h * 2 * PAIR_STEP : (h + 1) * 2 * PAIR_STEP])
                pack_pairs(pair_rows, stage)
                start = OUT_ROWS + MLP_ROWS + (piece * 2 + h) * PAIR_ROWS
                late[pl.ds(pl.multiple_of(start, 16), PAIR_ROWS), :] = stage[:PAIR_ROWS].astype(BF16)

        late[LATE_ROWS:] = jnp.zeros((late.shape[0] - LATE_ROWS, 128), BF16)
        low = bit_of(lax.axis_index("zero"), 0)
        copies = []
        for h in range(2):
            for side, target in enumerate((kept, sent)):
                start = pl.multiple_of(window_start(2 * h + (low if side == 0 else 1 - low)), 16)
                copies.append(pltpu.make_async_copy(late.at[pl.ds(start, kept.shape[1])], target.at[h], copy_sem.at[h, side]))
        for copy in copies:
            copy.start()
        for copy in copies:
            copy.wait()


def mlp_back(lens, att_t, gate, cot_parts, hidden_in, act_low, gate_slope, up_slope, gains, w_out, w_mlp, w_down, window):
    dp_size, lanes, _, width = cot_parts.shape
    shape = jax.ShapeDtypeStruct
    return pl.pallas_call(
        mlp_back_kernel,
        name="mlp_back",
        grid_spec=pltpu.PrefetchScalarGridSpec(
            num_scalar_prefetch=1,
            grid=(lanes, MLP_BLOCKS),
            in_specs=[
                pl.BlockSpec((1, WIDTH_Q, MLP_BLOCK), mlp_col_map),
                pl.BlockSpec((1, 16, MLP_BLOCK), mlp_col_map),
                pl.BlockSpec((dp_size // MLP_BLOCKS, 1, D, width), kept_part_map),
                pl.BlockSpec((1, MLP_BLOCK, D), mlp_row_map),
                pl.BlockSpec((1, MLP_BLOCK, FF), mlp_row_map),
                pl.BlockSpec((1, MLP_BLOCK, FF), mlp_row_map),
                pl.BlockSpec((1, MLP_BLOCK, FF), mlp_row_map),
                whole((2, D)),
                whole((WIDTH_Q, D)),
                whole((D, 2 * FF)),
                whole((FF, D)),
            ],
            out_specs=[
                pl.BlockSpec((1, D, MLP_BLOCK), mlp_col_map),
                pl.BlockSpec((1, WIDTH_Q, MLP_BLOCK), full_col_map),
                pl.BlockSpec((1, 32, MLP_BLOCK), full_col_map),
                pl.BlockSpec(memory_space=pl.ANY),
                pl.BlockSpec(memory_space=pl.ANY),
                whole((8, D)),
            ],
            scratch_shapes=[
                pltpu.VMEM((MLP_BLOCK, D), F32),
                pltpu.VMEM((WIDTH_Q, D), F32),
                pltpu.VMEM((D, 2 * FF), F32),
                pltpu.VMEM((D, FF), F32),
                pltpu.VMEM((LAST_WINDOW + window, 128), BF16),
                pltpu.VMEM((WIDE_STEP * WIDE_TILES, 128), F32),
                pltpu.VMEM((5, 2 * PAIR_STEP, 128), F32),
                pltpu.SemaphoreType.DMA((2, 2)),
            ],
        ),
        out_shape=[
            shape((lanes, D, LANE), F32),
            shape((lanes, WIDTH_Q, LANE), BF16),
            shape((lanes, 32, LANE), F32),
            shape((2, window, 128), BF16),
            shape((2, window, 128), BF16),
            shape((8, D), F32),
        ],
        compiler_params=pltpu.CompilerParams(vmem_limit_bytes=VMEM_LIMIT),
    )(lens, att_t, gate, cot_parts, hidden_in, act_low, gate_slope, up_slope, gains, w_out, w_mlp, w_down)


def project_back_kernel(lens, dq_t, dk_t, dv_t, logit_delta, raw, tok_t, grad_hidden_t, w_in, gain_cols, head_gains,
                        cosine, sine, grad_tok_t, g_in, g_gain, g_head, dproj, head_sum, gain_sum):
    lane, block = pl.program_id(0), pl.program_id(1)

    @pl.when((lane == 0) & (block == 0))
    def _():
        g_in[...] = jnp.zeros_like(g_in)
        gain_sum[...] = jnp.zeros_like(gain_sum)
        head_sum[...] = jnp.zeros_like(head_sum)

    @pl.when(block * PROJ_BLOCK >= lens[lane])
    def _():
        grad_tok_t[...] = jnp.zeros_like(grad_tok_t)

    @pl.when(block * PROJ_BLOCK < lens[lane])
    def _():
        cos, sin = cosine[...], sine[...]
        for head in range(HEADS + KV_HEADS):
            rows = slice(head * HEAD_DIM, (head + 1) * HEAD_DIM)
            side = 0 if head < HEADS else 1
            source = dq_t if head < HEADS else dk_t
            at = (head if head < HEADS else head - HEADS) * HEAD_DIM
            d1, d2 = source[0, at : at + HALF], source[0, at + HALF : at + HEAD_DIM]
            d = jnp.concatenate([d1 * cos + d2 * sin, d2 * cos - d1 * sin], axis=0)
            u = raw[0, rows]
            r = mean_square_scale(u, 0)
            ur = u * r
            head_sum[side] += d * ur
            dg = d * head_gains[side]
            dproj[rows] = (r * (dg - ur * jnp.mean(ur * dg, axis=0, keepdims=True))).astype(BF16)
        dproj[WIDTH_Q + WIDTH_K : WIDTH_Q + 2 * WIDTH_K] = dv_t[0].astype(BF16)
        row = lax.broadcasted_iota(jnp.int32, (16, PROJ_BLOCK), 0)
        logits = jnp.where(row < HEADS, logit_delta[0], 0.0).astype(BF16)
        dproj[WIDTH_Q + 2 * WIDTH_K :] = jnp.concatenate(
            [logits, jnp.zeros((QKVG_PAD - WIDTH_Q - 2 * WIDTH_K - 16, PROJ_BLOCK), BF16)], axis=0
        )
        x = tok_t[0].astype(F32)
        scale = mean_square_scale(x, 0)
        xs = x * scale
        gain = gain_cols[0]
        normed = (xs * gain).astype(BF16)
        g_in[...] += dot(normed, dproj[...], 1, 1)
        back = dot(w_in[...], dproj[...], 1, 0)
        gain_sum[...] += back * xs
        bg = back * gain
        grad_x = scale * (bg - xs * jnp.mean(xs * bg, axis=0, keepdims=True))
        grad_tok_t[0] = (grad_hidden_t[0] + grad_x).astype(BF16)

    @pl.when((lane == pl.num_programs(0) - 1) & (block == pl.num_programs(1) - 1))
    def _():
        g_head[...] = jnp.sum(head_sum[...], axis=2)
        g_gain[...] = jnp.sum(gain_sum[...], axis=1)[None]


def project_back(lens, dq_t, dk_t, dv_t, logit_delta, raw, tokens_t, grad_hidden_t, w_in, gain_cols, head_gains, cosine, sine):
    lanes = tokens_t.shape[0]
    shape = jax.ShapeDtypeStruct
    full_col = lambda lane, block, lens: (lane, 0, block)
    return pl.pallas_call(
        project_back_kernel,
        name="project_back",
        grid_spec=pltpu.PrefetchScalarGridSpec(
            num_scalar_prefetch=1,
            grid=(lanes, PROJ_BLOCKS),
            in_specs=[
                pl.BlockSpec((1, WIDTH_Q, PROJ_BLOCK), proj_col_map),
                pl.BlockSpec((1, WIDTH_K, PROJ_BLOCK), proj_col_map),
                pl.BlockSpec((1, WIDTH_K, PROJ_BLOCK), proj_col_map),
                pl.BlockSpec((1, 16, PROJ_BLOCK), proj_col_map),
                pl.BlockSpec((1, WIDTH_Q + WIDTH_K, PROJ_BLOCK), proj_col_map),
                pl.BlockSpec((1, D, PROJ_BLOCK), proj_col_map),
                pl.BlockSpec((1, D, PROJ_BLOCK), proj_col_map),
                whole((D, QKVG_PAD)),
                whole((2, D, 1)),
                whole((2, HEAD_DIM, 1)),
                pl.BlockSpec((HALF, PROJ_BLOCK), proj_table_map),
                pl.BlockSpec((HALF, PROJ_BLOCK), proj_table_map),
            ],
            out_specs=[
                pl.BlockSpec((1, D, PROJ_BLOCK), full_col),
                whole((D, QKVG_PAD)),
                whole((1, D)),
                whole((2, HEAD_DIM)),
            ],
            scratch_shapes=[
                pltpu.VMEM((QKVG_PAD, PROJ_BLOCK), BF16),
                pltpu.VMEM((2, HEAD_DIM, PROJ_BLOCK), F32),
                pltpu.VMEM((D, PROJ_BLOCK), F32),
            ],
        ),
        out_shape=[
            shape((lanes, D, LANE), BF16),
            shape((D, QKVG_PAD), F32),
            shape((1, D), F32),
            shape((2, HEAD_DIM), F32),
        ],
        cost_estimate=pl.CostEstimate(flops=20_000_000_000, bytes_accessed=60_000_000, transcendentals=0),
        compiler_params=pltpu.CompilerParams(vmem_limit_bytes=VMEM_LIMIT),
    )(lens, dq_t, dk_t, dv_t, logit_delta, raw, tokens_t, grad_hidden_t, w_in, gain_cols, head_gains, cosine, sine)


def layer_forward(tokens_t, lens, weights):
    w_in, gains, head_gains = weights
    gain_cols, head_gains = gains[:, :, None], head_gains[:, :, None]
    cosine, sine = (jnp.asarray(t) for t in rope_tables())
    q_t, k_n, k_t, v_n, v_t, raw, gate = project(lens, tokens_t, w_in, gain_cols, head_gains, cosine, sine)
    att_t, log_total = attend(lens, q_t, k_n, v_t)
    return att_t, gate, (q_t, k_n, k_t, v_n, log_total, raw)


def head_groups(rows):
    return rows[:, :HEADS].reshape(rows.shape[0], KV_HEADS, GROUP, LANE)


SHARD = PARAMS // 4
LANES128 = 128
EDGE = 16
STEP = 6928
BODY = STEP - EDGE
SPAN = STEP + EDGE
IN_ROWS = 4361
SPLIT_AT = D * QKVG
MESH = pl.DeviceIdType.MESH


def shard_shift(s):
    offset = EDGE * LANES128 - (STEP * LANES128 - SHARD) * s + (64 if s else 0)
    return offset // LANES128, offset % LANES128


def flip(index, bit):
    return index + (1 - 2 * (index // (1 << bit) % 2)) * (1 << bit)


def bit_of(index, bit):
    return index // (1 << bit) % 2


def greet(partners):
    barrier = pltpu.get_barrier_semaphore()
    for partner in partners:
        pl.semaphore_signal(barrier, inc=1, device_id=partner, device_id_type=MESH)
    pl.semaphore_wait(barrier, len(partners))


PACK_TILE = 496
FIRST_ROWS = 4368
LAST_TILE = 32
GAIN_AT = EDGE + IN_ROWS + LATE_ROWS - 3 * STEP - (SPAN - LAST_TILE)
FIRST_CUTS = (0, 1088, 2176, 3264, FIRST_ROWS)


def pack_kernel(master, own, first_rows, last_rows, rows_in, packed, load_sem, keep_sem, own_sem, send_sem, recv_sem):
    dp, zero = lax.axis_index("dp"), lax.axis_index("zero")
    core, across, side = (dp, flip(zero, 0)), (dp, flip(zero, 1)), (flip(dp, 0), zero)
    y = bit_of(dp, 0)
    load = pltpu.make_async_copy(master, rows_in.at[pl.ds(24, STEP)], load_sem)
    load.start()
    rows_in[:24] = jnp.zeros((24, LANES128), F32)
    rows_in[24 + STEP :] = jnp.zeros((24, LANES128), F32)
    greet((core, across, side))
    load.wait()
    lane = lax.broadcasted_iota(jnp.int32, (PACK_TILE, LANES128), 1)

    def shifted(start, a, k):
        if k == 0:
            return rows_in[pl.ds(start + 24 - a, PACK_TILE), :]
        here = pltpu.roll(rows_in[pl.ds(start + 24 - a, PACK_TILE), :], k, 1)
        above = pltpu.roll(rows_in[pl.ds(start + 23 - a, PACK_TILE), :], k, 1)
        return jnp.where(lane >= k, here, above)

    def pack(s, start):
        if s == 0 and start + PACK_TILE <= EDGE + IN_ROWS:
            value = shifted(start, EDGE, 0)
        elif s == 0 and start < EDGE + IN_ROWS:
            row = lax.broadcasted_iota(jnp.int32, (PACK_TILE, LANES128), 0) + start
            value = jnp.where(row < EDGE + IN_ROWS, shifted(start, EDGE, 0), shifted(start, EDGE, 64))
        elif s == 0:
            value = shifted(start, EDGE, 64)
        else:
            value = shifted(start, *shard_shift(s))
        packed[pl.ds(start, PACK_TILE), :] = value.astype(BF16)

    def piece_rows(piece):
        return pl.ds(EDGE + FIRST_CUTS[piece], FIRST_CUTS[piece + 1] - FIRST_CUTS[piece])

    def mine(piece):
        return packed.at[piece_rows(piece)]

    def theirs(piece):
        return first_rows.at[piece_rows(piece)]

    def copy(source, target, device, slot):
        return pltpu.make_async_remote_copy(source, target, send_sem.at[slot], recv_sem.at[slot],
                                            device_id=device, device_id_type=MESH)

    for s in range(4):

        @pl.when(zero == s)
        def _():
            for t in range(SPAN // PACK_TILE):
                pack(s, t * PACK_TILE)

    keep = pltpu.make_async_copy(packed, own, own_sem)
    keep.start()
    tail = packed.at[pl.ds(SPAN - LAST_TILE, LAST_TILE)]

    @pl.when(zero == 3)
    def _():
        copy(tail, last_rows, across, 9).start()
        copy(tail, last_rows, core, 8).start()
        stay = pltpu.make_async_copy(tail, last_rows, keep_sem)
        stay.start()
        stay.wait()
        copy(tail, last_rows, across, 9).wait_send()
        copy(tail, last_rows, core, 8).wait_send()

    @pl.when(zero == 1)
    def _():
        copy(last_rows, last_rows, across, 9).wait_recv()
        copy(last_rows, last_rows, core, 8).start()
        copy(last_rows, last_rows, core, 8).wait_send()

    for half in range(2):
        pieces = (2 * half, 2 * half + 1)
        others = (2 - 2 * half, 3 - 2 * half)

        @pl.when((zero == 0) & (y == half))
        def _():
            for piece in pieces:
                copy(mine(piece), theirs(piece), across, piece).start()
            for piece in range(4):
                copy(mine(piece), theirs(piece), core, 4 + piece).start()
            stay = pltpu.make_async_copy(packed.at[pl.ds(EDGE, FIRST_ROWS)], first_rows.at[pl.ds(EDGE, FIRST_ROWS)], keep_sem)
            stay.start()
            for piece in pieces:
                copy(mine(piece), theirs(piece), across, piece).wait_send()
            for piece in range(4):
                copy(mine(piece), theirs(piece), core, 4 + piece).wait_send()
            stay.wait()

        @pl.when((zero == 2) & (y == half))
        def _():
            for piece in pieces:
                copy(theirs(piece), theirs(piece), across, piece).wait_recv()
                copy(theirs(piece), theirs(piece), side, piece).start()
                copy(theirs(piece), theirs(piece), core, 4 + piece).start()
            for piece in others:
                copy(theirs(piece), theirs(piece), side, piece).wait_recv()
                copy(theirs(piece), theirs(piece), core, 4 + piece).start()
            for piece in pieces:
                copy(theirs(piece), theirs(piece), side, piece).wait_send()
            for piece in range(4):
                copy(theirs(piece), theirs(piece), core, 4 + piece).wait_send()

    @pl.when(bit_of(zero, 0) == 0)
    def _():
        copy(last_rows, last_rows, core, 8).wait_recv()

    @pl.when(bit_of(zero, 0) == 1)
    def _():
        for piece in range(4):
            copy(theirs(piece), theirs(piece), core, 4 + piece).wait_recv()

    keep.wait()


def pack_master(master):
    rows = jnp.pad(master, (0, STEP * LANES128 - SHARD)).reshape(STEP, LANES128)
    shape = jax.ShapeDtypeStruct
    return pl.pallas_call(
        pack_kernel,
        name="pack_master",
        out_shape=[shape((SPAN, LANES128), BF16), shape((EDGE + FIRST_ROWS, LANES128), BF16), shape((LAST_TILE, LANES128), BF16)],
        in_specs=[pl.BlockSpec(memory_space=pl.ANY)],
        out_specs=[pl.BlockSpec(memory_space=pl.ANY)] * 3,
        scratch_shapes=[
            pltpu.VMEM((24 + STEP + 24, LANES128), F32),
            pltpu.VMEM((SPAN, LANES128), BF16),
            pltpu.SemaphoreType.DMA,
            pltpu.SemaphoreType.DMA,
            pltpu.SemaphoreType.DMA,
            pltpu.SemaphoreType.DMA((10,)),
            pltpu.SemaphoreType.DMA((10,)),
        ],
        cost_estimate=pl.CostEstimate(flops=0, bytes_accessed=0, transcendentals=0),
        compiler_params=pltpu.CompilerParams(collective_id=0, has_side_effects=True, vmem_limit_bytes=VMEM_LIMIT),
    )(rows)


REDUCE_PARTS = 11


def window_start(s):
    return jnp.minimum(s, 1) * (((s * SHARD + 64) // LANES128 - IN_ROWS) // 16 * 16)


LAST_WINDOW = ((3 * SHARD + 64) // LANES128 - IN_ROWS) // 16 * 16


def window_rows(dp_size):
    unit = REDUCE_PARTS * 16 * dp_size
    return -(-(SHARD // LANES128 + 17) // unit) * unit


CLASSES = ((0, 6), (6, 5))


def bit_order(bits, kind):
    order = list(range(bits))
    if kind and bits > 1:
        order[0], order[1] = 1, 0
    return order


def part_region(dp, rows, bits, kind, count):
    offset, size = 0, rows
    for k in bit_order(bits, kind)[:count]:
        size = size // 2
        offset = offset + bit_of(dp, k) * size
    return offset, size


def aligned(offset, size):
    return pl.ds(pl.multiple_of(offset, 16), size)


LATE_HOP = 12.0


def arrival_order(chains, hops):
    free, order = {}, []
    pending = [(0.0, index, 0) for index in range(len(chains))]
    while pending:
        pending.sort()
        start, index, step = pending.pop(0)
        link, span = chains[index][step]
        end = max(start, free.get(link, 0.0)) + span
        free[link] = end
        hop = hops[index]
        order.append((end + hop, index, step))
        if step + 1 < len(chains[index]):
            pending.append((end + hop, index, step + 1))
    return sorted(order)


def attend_back_kernel(lens, q_t, k_n, k_t, v_n, grad_t, log_total, delta, dq_t, dk_t, dv_t):
    lane = pl.program_id(0)
    dq_t[...] = jnp.zeros_like(dq_t)
    for block in range(BLOCKS):
        keys = pl.ds(block * BLOCK, BLOCK)

        @pl.when(block * BLOCK >= lens[lane])
        def _():
            dk_t[0, :, keys] = jnp.zeros((HEAD_DIM, BLOCK), F32)
            dv_t[0, :, keys] = jnp.zeros((HEAD_DIM, BLOCK), F32)

        @pl.when(block * BLOCK < lens[lane])
        def _():
            k_rows, v_rows, k_cols = k_n[0, 0, keys, :], v_n[0, 0, keys, :], k_t[0, :, keys]
            dk = jnp.zeros((HEAD_DIM, BLOCK), F32)
            dv = jnp.zeros((HEAD_DIM, BLOCK), F32)
            cols = pl.ds(block * BLOCK, LANE - block * BLOCK)
            for r in range(GROUP):
                head = slice(r * HEAD_DIM, (r + 1) * HEAD_DIM)
                query, grad = q_t[0, head, cols], grad_t[0, head, cols]
                prob = jnp.exp2(dot(k_rows, query, 1, 0) * EXP_SCALE - log_total[0, 0, r : r + 1, cols])
                prob = causal_tile(prob, 0.0)
                grad_prob = dot(v_rows, grad, 1, 0) - delta[0, 0, r : r + 1, cols]
                grad_score = (prob * grad_prob).astype(BF16)
                dv += dot(grad, prob.astype(BF16), 1, 1)
                dk += dot(query, grad_score, 1, 1)
                dq_t[0, head, cols] += dot(k_cols, grad_score, 1, 0) * SCALE
            dk_t[0, :, keys] = dk * SCALE
            dv_t[0, :, keys] = dv


def attend_back(lens, q_t, k_n, k_t, v_n, grad_t, log_total, delta):
    lanes = q_t.shape[0]
    shape = jax.ShapeDtypeStruct
    group_rows = lambda lane, g, lens: (lane, g, 0)
    group_heads = lambda lane, g, lens: (lane, g, 0, 0)
    return pl.pallas_call(
        attend_back_kernel,
        name="attend_back",
        grid_spec=pltpu.PrefetchScalarGridSpec(
            num_scalar_prefetch=1,
            grid=(lanes, KV_HEADS),
            in_specs=[
                pl.BlockSpec((1, GROUP * HEAD_DIM, LANE), group_rows),
                pl.BlockSpec((1, 1, LANE, HEAD_DIM), group_heads),
                pl.BlockSpec((1, HEAD_DIM, LANE), group_rows),
                pl.BlockSpec((1, 1, LANE, HEAD_DIM), group_heads),
                pl.BlockSpec((1, GROUP * HEAD_DIM, LANE), group_rows),
                pl.BlockSpec((1, 1, GROUP, LANE), group_heads),
                pl.BlockSpec((1, 1, GROUP, LANE), group_heads),
            ],
            out_specs=[
                pl.BlockSpec((1, GROUP * HEAD_DIM, LANE), group_rows),
                pl.BlockSpec((1, HEAD_DIM, LANE), group_rows),
                pl.BlockSpec((1, HEAD_DIM, LANE), group_rows),
            ],
        ),
        out_shape=[
            shape((lanes, WIDTH_Q, LANE), F32),
            shape((lanes, WIDTH_K, LANE), F32),
            shape((lanes, WIDTH_K, LANE), F32),
        ],
        cost_estimate=pl.CostEstimate(flops=40_000_000_000, bytes_accessed=40_000_000, transcendentals=0),
        compiler_params=pltpu.CompilerParams(vmem_limit_bytes=VMEM_LIMIT),
    )(lens, q_t, k_n, k_t, v_n, grad_t, log_total, delta)


TAIL_AT = 4368


HEAD_PARTS = 3
HEAD_HOP = 3.0
LATE_GROUPS = ((0, 0, 3), (1, 0, 3), (0, 3, 3), (1, 3, 2))


def head_rows(dp_size):
    unit = 2 * HEAD_PARTS * 16 * 2 * dp_size
    return -(-(TAIL_AT + 16) // unit) * unit


def sum_head_kernel(bits, rows, late_rows, source, gain_rows, late_share, result, late_sum, total, *rest):
    received, (load_sem, send_sem, recv_sem, late_send, late_recv) = rest[:-5], rest[-5:]
    dp, zero = lax.axis_index("dp"), lax.axis_index("zero")
    axes = [("zero", 1)] + [("dp", k) for k in range(bits)]

    def partner(axis, k):
        return (flip(dp, k), zero) if axis == "dp" else (dp, flip(zero, k))

    def bit(axis, k):
        return bit_of(dp if axis == "dp" else zero, k)

    load = pltpu.make_async_copy(source, total, load_sem)
    load.start()
    load.wait()
    total[TAIL_AT : TAIL_AT + 16] = gain_rows[...]
    greet([partner("zero", 0)] + [partner(*axis) for axis in axes])

    def step(index, slot, source_ref, target_ref, axis):
        copy = pltpu.make_async_remote_copy(source_ref, target_ref, send_sem.at[index, slot], recv_sem.at[index, slot],
                                            device_id=partner(*axis), device_id_type=MESH)
        copy.start()
        return copy

    def order_of(index):
        return [("zero", 0)] + [axes[(index + j) % len(axes)] for j in range(len(axes))]

    def spans_of(index):
        spans = [(axis, 0.5 if axis == ("zero", 0) else 9.0 / HEAD_PARTS / (1 << slot)) for slot, axis in enumerate(order_of(index))]
        return spans + spans[::-1]

    def chain_of(index):
        order = order_of(index)
        size = rows // HEAD_PARTS
        offset = index * size
        regions = []
        for slot, axis in enumerate(order):
            half = size // 2
            mine, other = offset + bit(*axis) * half, offset + (1 - bit(*axis)) * half
            landing = received[slot].at[index]
            yield step(index, slot, total.at[aligned(other, half)], landing, axis)
            at = aligned(mine, half)
            target = total if slot + 1 < len(order) else result
            target[at] = (total[at].astype(F32) + landing[...].astype(F32)).astype(BF16)
            offset, size = mine, half
            regions.append(at)
        for slot in reversed(range(len(order))):
            place = result.at[regions[slot]]
            yield step(index, 2 * len(order) - 1 - slot, place, place, order[slot])

    def late_spans(index):
        kind, _, count = LATE_GROUPS[index]
        spans = [(("dp", k), 20.0 / (1 << slot) * count / REDUCE_PARTS) for slot, k in enumerate(bit_order(bits, kind))]
        return spans[::-1]

    def late_chain(index):
        kind, start, count = LATE_GROUPS[index]
        parts = pl.ds(CLASSES[kind][0] + start, count)
        late_sum[parts, aligned(*part_region(dp, late_rows, bits, kind, bits))] = late_share[parts]
        for slot, k in reversed(list(enumerate(bit_order(bits, kind)))):
            place = late_sum.at[parts, aligned(*part_region(dp, late_rows, bits, kind, slot + 1))]
            copy = pltpu.make_async_remote_copy(place, place, late_send.at[index, slot], late_recv.at[index, slot],
                                                device_id=partner("dp", k), device_id_type=MESH)
            copy.start()
            yield copy

    chains = [chain_of(i) for i in range(HEAD_PARTS)] + [late_chain(i) for i in range(len(LATE_GROUPS))]
    spans = [spans_of(i) for i in range(HEAD_PARTS)] + [late_spans(i) for i in range(len(LATE_GROUPS))]
    flying = [next(chain) for chain in chains]
    sent = list(flying)
    for _, index, _ in arrival_order(spans, [HEAD_HOP] * HEAD_PARTS + [LATE_HOP] * len(LATE_GROUPS)):
        flying[index].wait_recv()
        following = next(chains[index], None)
        if following is not None:
            flying[index] = following
            sent.append(following)
    for copy in sent:
        copy.wait_send()


def sum_head(source, gain_rows, share, late_rows, dp_size):
    bits = dp_size.bit_length() - 1
    rows = source.shape[0]
    steps = bits + 2
    shape = jax.ShapeDtypeStruct
    return pl.pallas_call(
        functools.partial(sum_head_kernel, bits, rows, late_rows),
        name="sum_head",
        out_shape=[shape((rows, LANES128), BF16), shape((REDUCE_PARTS, late_rows, LANES128), BF16)],
        in_specs=[pl.BlockSpec(memory_space=pl.ANY)] + [pl.BlockSpec(memory_space=pltpu.VMEM)] * 2,
        out_specs=[pl.BlockSpec(memory_space=pltpu.VMEM)] * 2,
        scratch_shapes=[
            pltpu.VMEM((rows, LANES128), BF16),
            *[pltpu.VMEM((HEAD_PARTS, rows // HEAD_PARTS >> (k + 1), LANES128), BF16) for k in range(steps)],
            pltpu.SemaphoreType.DMA,
            pltpu.SemaphoreType.DMA((HEAD_PARTS, 2 * steps)),
            pltpu.SemaphoreType.DMA((HEAD_PARTS, 2 * steps)),
            pltpu.SemaphoreType.DMA((len(LATE_GROUPS), bits)),
            pltpu.SemaphoreType.DMA((len(LATE_GROUPS), bits)),
        ],
        compiler_params=pltpu.CompilerParams(collective_id=2, has_side_effects=True, vmem_limit_bytes=VMEM_LIMIT),
    )(source, gain_rows, share)


def flat_rows(g_in, rows):
    flat = g_in[:, :QKVG].astype(BF16).reshape(-1)
    return jnp.pad(flat, (0, rows * LANES128 - SPLIT_AT)).reshape(rows, LANES128)


def pack_gains(g_gain_one, g_gain_two, g_head):
    flat = jnp.concatenate([g_gain_one[0], g_gain_two[0], g_head.reshape(-1)]).astype(BF16)
    return jnp.pad(flat.reshape(10, LANES128), ((0, 6), (0, 0)))


def unpack_shard(late, head, zero_rank):
    late = late.reshape(-1)
    head_flat = head.reshape(-1)
    starts = [s * SHARD - SPLIT_AT - LANES128 * max(0, ((s * SHARD + 64) // LANES128 - IN_ROWS) // 16 * 16) for s in range(1, 4)]
    tail = head_flat[TAIL_AT * LANES128 : (TAIL_AT + 10) * LANES128]

    def pick(s):
        if s == 0:
            return lambda: jnp.concatenate([head_flat[:SPLIT_AT], late[: SHARD - SPLIT_AT]])
        if s == 3:
            return lambda: jnp.concatenate([late[starts[2] : starts[2] + SHARD - 10 * LANES128], tail])
        return lambda: late[starts[s - 1] : starts[s - 1] + SHARD]

    return lax.switch(zero_rank, [pick(s) for s in range(4)]).astype(F32)


UNPACK_SKEW = (EDGE + IN_ROWS) % 16


def unpack_kernel(own, near, far, both, w_out, w_mlp, w_down, packed, edges, stage, pair_rows, load_sem, edge_sem):
    zero = lax.axis_index("zero")
    shards = [(own, zero), (near, flip(zero, 0)), (far, flip(zero, 1)), (both, flip(flip(zero, 0), 1))]
    loads = [
        pltpu.make_async_copy(shard.at[pl.ds(EDGE, BODY)], packed.at[pl.ds(pl.multiple_of(STEP * s + EDGE, 16), BODY)], load_sem.at[k])
        for k, (shard, s) in enumerate(shards)
    ]
    ends = [pltpu.make_async_copy(shard.at[pl.ds(at, EDGE)], edges.at[s, h], edge_sem.at[k, h])
            for k, (shard, s) in enumerate(shards) for h, at in enumerate((0, EDGE + BODY))]
    for copy in ends + loads:
        copy.start()
    for copy in ends:
        copy.wait()
    packed[:EDGE] = edges[0, 0]
    for s in range(4):
        tile = edges[s, 1].astype(F32)
        if s < 3:
            tile = tile + edges[s + 1, 0].astype(F32)
        packed[pl.ds(STEP * (s + 1), EDGE), :] = tile.astype(BF16)
    for copy in loads:
        copy.wait()

    def fetch(first_row, count):
        stage[: count + 16] = packed[pl.ds(pl.multiple_of(first_row - UNPACK_SKEW, 16), count + 16), :].astype(F32)

    def split_pairs(first_row, target, row):
        fetch(first_row, PAIR_ROWS)
        tiles = [stage[pl.ds(UNPACK_SKEW + t, PAIR_STEP, stride=9), :] for t in range(9)]
        even, odd = pl.ds(0, PAIR_STEP, stride=2), pl.ds(1, PAIR_STEP, stride=2)
        for t in range(4):
            pair_rows[t, even, :] = tiles[t]
        pair_rows[4, even, :] = tiles[4]
        for t in range(4):
            pair_rows[t, odd, :] = jnp.concatenate([tiles[4 + t][:, 64:], tiles[5 + t][:, :64]], axis=1)
        pair_rows[4, odd, :] = jnp.concatenate([tiles[8][:, 64:], tiles[8][:, :64]], axis=1)
        at = pl.ds(pl.multiple_of(row, 2 * PAIR_STEP), 2 * PAIR_STEP)
        for t in range(4):
            target[at, t * 128 : (t + 1) * 128] = pair_rows[t].astype(BF16)
        target[at, 512:] = pair_rows[4, :, :64].astype(BF16)

    out_at = EDGE + IN_ROWS
    mlp_at = out_at + OUT_ROWS
    down_at = mlp_at + MLP_ROWS

    @pl.loop(0, WIDTH_Q // (2 * PAIR_STEP))
    def _(piece):
        split_pairs(out_at + piece * PAIR_ROWS, w_out, piece * 2 * PAIR_STEP)

    @pl.loop(0, FF // (2 * PAIR_STEP))
    def _(piece):
        split_pairs(down_at + piece * PAIR_ROWS, w_down, piece * 2 * PAIR_STEP)

    @pl.loop(0, D // WIDE_STEP)
    def _(piece):
        fetch(mlp_at + piece * WIDE_STEP * WIDE_TILES, WIDE_STEP * WIDE_TILES)
        rows = pl.ds(pl.multiple_of(piece * WIDE_STEP, WIDE_STEP), WIDE_STEP)
        for tile in range(WIDE_TILES):
            w_mlp[rows, tile * 128 : (tile + 1) * 128] = stage[pl.ds(UNPACK_SKEW + tile, WIDE_STEP, stride=WIDE_TILES), :].astype(BF16)


def unpack_weights(shards):
    shape = jax.ShapeDtypeStruct
    return pl.pallas_call(
        unpack_kernel,
        name="unpack_weights",
        in_specs=[pl.BlockSpec(memory_space=pl.ANY)] * 4,
        out_shape=[shape((WIDTH_Q, D), BF16), shape((D, 2 * FF), BF16), shape((FF, D), BF16)],
        scratch_shapes=[
            pltpu.VMEM((3 * STEP + SPAN, LANES128), BF16),
            pltpu.VMEM((4, 2, EDGE, LANES128), BF16),
            pltpu.VMEM((WIDE_STEP * WIDE_TILES + 16, 128), F32),
            pltpu.VMEM((5, 2 * PAIR_STEP, 128), F32),
            pltpu.SemaphoreType.DMA((4,)),
            pltpu.SemaphoreType.DMA((4, 2)),
        ],
        cost_estimate=pl.CostEstimate(flops=0, bytes_accessed=0, transcendentals=0),
        compiler_params=pltpu.CompilerParams(vmem_limit_bytes=VMEM_LIMIT),
    )(*shards)


def column_parts(lanes_t, dp_size):
    seqs, width, columns = lanes_t.shape
    return lanes_t.reshape(seqs, width, dp_size, columns // dp_size).transpose(2, 0, 1, 3)


def spread(parts):
    return lax.all_to_all(parts, "dp", split_axis=0, concat_axis=0, tiled=True)


def regroup(parts, order):
    dp_size, seqs, width, columns = parts.shape
    parts = jnp.take(parts.reshape(dp_size * seqs, width, columns), order, axis=0, mode="clip")
    return lax.all_to_all(parts.reshape(dp_size, seqs, width, columns), "dp", split_axis=0, concat_axis=0, tiled=True)


def joined(parts):
    dp_size, seqs, width, rows = parts.shape
    return parts.transpose(1, 2, 0, 3).reshape(seqs, width, dp_size * rows)


def exchange(values, axis, bit):
    return lax.ppermute(values, axis, [(i, i ^ (1 << bit)) for i in range(lax.axis_size(axis))])


def quarters(window, dp_rank):
    size = window.shape[1] // 4

    def rows_for(mask, kind):
        at, count = CLASSES[kind]
        first, second = (bit_of(dp_rank, bit) ^ (mask >> bit & 1) for bit in bit_order(2, kind))
        return lax.dynamic_slice_in_dim(window[at : at + count], first * (2 * size) + second * size, size, 1)

    return [jnp.concatenate([rows_for(mask, kind) for kind in range(2)]) for mask in range(4)]


def exchange_quarters(rows):
    def sent(values, mask):
        return lax.ppermute(values, "dp", [(i, i ^ mask) for i in range(lax.axis_size("dp"))])

    return [rows[0]] + [sent(rows[mask], mask) for mask in range(1, 4)]


def halve(parts, dp_rank, bit):
    half = parts.shape[1] // 2
    mine = bit_of(dp_rank, bit)
    sent = lax.dynamic_slice_in_dim(parts, (1 - mine) * half, half, 1)
    return [lax.dynamic_slice_in_dim(parts, mine * half, half, 1), exchange(sent, "dp", bit)]


def added(pieces):
    return sum(piece.astype(F32) for piece in pieces).astype(BF16)


def unpack_first(first_rows, last_rows):
    w_in = first_rows[EDGE : EDGE + IN_ROWS].reshape(-1)[:SPLIT_AT].reshape(D, QKVG)
    w_in = jnp.pad(w_in, ((0, 0), (0, QKVG_PAD - QKVG)))
    rows = last_rows[GAIN_AT : GAIN_AT + 10].astype(F32)
    return w_in, rows[:9].reshape(2, D), rows[9].reshape(2, HEAD_DIM)


def local(tokens, cotangent, lengths, balance, master, moment_one, moment_two):
    dp_rank, zero_rank = lax.axis_index("dp"), lax.axis_index("zero")
    dp_size, zero_size = lax.axis_size("dp"), lax.axis_size("zero")
    seqs = tokens.shape[0]
    order = lax.dynamic_index_in_dim(balance, zero_rank, 0, keepdims=False)
    inverse = jnp.zeros_like(order).at[order].set(jnp.arange(order.shape[0], dtype=order.dtype))
    lens = lax.dynamic_slice_in_dim(lengths, (dp_rank * zero_size + zero_rank) * seqs, seqs)
    tokens_t = tokens.swapaxes(1, 2)
    cot_parts = spread(column_parts(cotangent.swapaxes(1, 2), dp_size))
    own, first_rows, last_rows = pack_master(master)
    far, near = exchange(own, "zero", 1), exchange(own, "zero", 0)
    first = unpack_first(first_rows, last_rows)
    att_t, gate, kept = layer_forward(tokens_t, lens, first)
    far, near, att_t, cot_parts = lax.optimization_barrier((far, near, att_t, cot_parts))
    both = exchange(far, "zero", 0)
    cot_here = regroup(cot_parts, inverse)
    w_out, w_mlp, w_down = unpack_weights((own, near, far, both))
    w_in, gains, head_gains = first
    gain_cols, head_gains = gains[:, :, None], head_gains[:, :, None]
    out_columns, *stash = mlp(lens, att_t, gate, tokens_t, gains, w_out, w_mlp, w_down, dp_size)
    output_parts = spread(out_columns)
    grad_hidden_t, grad_att_t, logit_delta, late_kept, late_sent, g_gain_two = mlp_back(
        lens, att_t, gate, cot_here, *stash, gains, w_out, w_mlp, w_down, window_rows(dp_size))
    late_in = exchange(late_sent, "zero", 0)
    output_parts, grad_att_t = lax.optimization_barrier((output_parts, grad_att_t))
    output_parts = regroup(output_parts, order)
    q_t, k_n, k_t, v_n, log_total, raw = kept
    high = bit_of(zero_rank, 1)
    side = lambda windows, h: lax.dynamic_index_in_dim(windows, h, 0, keepdims=False)
    crossing = added([side(late_kept, 1 - high), side(late_in, 1 - high)])
    crossing, grad_att_t = lax.optimization_barrier((crossing, grad_att_t))
    crossed = exchange(crossing, "zero", 1)
    dq_t, dk_t, dv_t = attend_back(
        lens, q_t, k_n, k_t, v_n, grad_att_t, head_groups(log_total), head_groups(logit_delta[:, 16:]))
    dq_t, crossed = lax.optimization_barrier((dq_t, crossed))
    window = added([side(late_kept, high), side(late_in, high), crossed]).reshape(REDUCE_PARTS, -1, LANES128)
    dp_bits = dp_size.bit_length() - 1
    rows, dq_t = lax.optimization_barrier((quarters(window, dp_rank), dq_t))
    pieces = exchange_quarters(rows)
    cosine, sine = (jnp.asarray(t) for t in rope_tables())
    grad_tokens_t, g_in, g_gain_one, g_head = project_back(
        lens, dq_t, dk_t, dv_t, logit_delta, raw, tokens_t, grad_hidden_t, w_in, gain_cols, head_gains, cosine, sine)
    pieces, g_in, output_parts = lax.optimization_barrier((pieces, g_in, output_parts))
    share = added(pieces)
    head = flat_rows(g_in, head_rows(dp_size))
    gain_rows = pack_gains(g_gain_one, g_gain_two, g_head)
    for step in range(2, dp_bits):
        pieces = halve(share, dp_rank, step)
        pieces, head, gain_rows = lax.optimization_barrier((pieces, head, gain_rows))
        share = added(pieces)
    grad_tokens = grad_tokens_t.swapaxes(1, 2)
    head_sum, late_sum = sum_head(head, gain_rows, share, window.shape[1], dp_size)
    output = joined(output_parts).swapaxes(1, 2)
    grad_shard = unpack_shard(late_sum, head_sum, zero_rank)
    gain_width = D // zero_size
    gain_sums = head_sum[TAIL_AT : TAIL_AT + 9].reshape(2, zero_size, gain_width)
    grad_gains = lax.dynamic_index_in_dim(gain_sums, zero_rank, 1, keepdims=False).astype(F32)
    next_one = BETA_ONE * moment_one + (1.0 - BETA_ONE) * grad_shard
    next_two = BETA_TWO * moment_two + (1.0 - BETA_TWO) * grad_shard * grad_shard
    update_dir = next_one / BIAS_ONE / jnp.sqrt(next_two / BIAS_TWO)
    return output, grad_tokens, grad_shard, update_dir, next_one, next_two, grad_gains


def solution(mesh):
    lanes = P(("dp", "zero"), None, None)
    return jax.shard_map(
        local,
        mesh=mesh,
        in_specs=(lanes, lanes, P(), P(), P("zero"), P("zero"), P("zero")),
        out_specs=(lanes, lanes, P("zero"), P("zero"), P("zero"), P("zero"), P(None, "zero")),
        check_vma=False,
    )
```

```python
import functools
import math

import jax
import jax.numpy as jnp
import numpy as np
from jax import lax
from jax.experimental import pallas as pl
from jax.experimental.pallas import tpu as pltpu
from jax.sharding import PartitionSpec as P

D = 576
HEADS = 9
KV_HEADS = 3
GROUP = HEADS // KV_HEADS
HEAD_DIM = 64
HALF = HEAD_DIM // 2
FF = 1536
LANE = 1024
QKVG = 969
QKVG_PAD = 1024
WIDTH_Q = HEADS * HEAD_DIM
WIDTH_K = KV_HEADS * HEAD_DIM
PARAMS = 3545408
EPSILON = 1e-05
ROPE_BASE = 100000.0
BETA_ONE = 0.9
BETA_TWO = 0.95
BIAS_ONE = 1.0 - BETA_ONE**10
BIAS_TWO = 1.0 - BETA_TWO**10
SCALE = HEAD_DIM ** (-0.5)
EXP_SCALE = SCALE * math.log2(math.e)
F32 = jnp.float32
BF16 = jnp.bfloat16
BLOCK = 256
BLOCKS = LANE // BLOCK
FF_CHUNK = 768
MLP_BLOCK = 512
MLP_BLOCKS = LANE // MLP_BLOCK
PROJ_BLOCK = 512
PROJ_BLOCKS = LANE // PROJ_BLOCK
VMEM_LIMIT = 60 * 1024 * 1024


def dot(a, b, ca, cb):
    return lax.dot_general(a, b, (((ca,), (cb,)), ((), ())), preferred_element_type=F32)


def rope_tables():
    frequency = ROPE_BASE ** (-(np.arange(HALF, dtype=np.float32) * np.float32(2.0)) / np.float32(HEAD_DIM))
    angles = np.arange(LANE, dtype=np.float32)[None, :] * frequency.astype(np.float32)[:, None]
    return np.cos(angles).astype(np.float32), np.sin(angles).astype(np.float32)


def mean_square_scale(values, axis):
    return lax.rsqrt(jnp.mean(values * values, axis=axis, keepdims=True) + EPSILON)


def block_spec(shape, index):
    return pl.BlockSpec(shape, index)


def whole(shape):
    return pl.BlockSpec(shape, lambda *_: (0,) * len(shape), pipeline_mode=pl.Buffered(1))


def full_col_map(lane, block, lens):
    return (lane, 0, block)


def last_block(lens, lane, block):
    return jnp.minimum(block, (lens[lane] - 1) // BLOCK)


def project_kernel(lens, tok_t, w_in, gain_cols, head_gains, cosine, sine, q_t, k_n, k_t, v_n, v_t, raw, gate, w_in_t):
    lane, block = pl.program_id(0), pl.program_id(1)

    @pl.when((lane == 0) & (block == 0))
    def _():
        w_in_t[...] = w_in[...].T

    @pl.when(block * PROJ_BLOCK < lens[lane])
    def _():
        x = tok_t[0].astype(F32)
        normed = (x * mean_square_scale(x, 0) * gain_cols[0]).astype(BF16)
        projected = dot(w_in_t[...], normed, 1, 0)
        raw[0] = projected[: WIDTH_Q + WIDTH_K]
        cos, sin = cosine[...], sine[...]
        for head in range(HEADS + KV_HEADS):
            u = projected[head * HEAD_DIM : (head + 1) * HEAD_DIM]
            y = u * mean_square_scale(u, 0) * head_gains[0 if head < HEADS else 1]
            y1, y2 = y[:HALF], y[HALF:]
            turned = jnp.concatenate([y1 * cos - y2 * sin, y2 * cos + y1 * sin], axis=0)
            if head < HEADS:
                q_t[0, head * HEAD_DIM : (head + 1) * HEAD_DIM] = turned.astype(BF16)
            else:
                k = head - HEADS
                k_t[0, k * HEAD_DIM : (k + 1) * HEAD_DIM] = turned.astype(BF16)
                k_n[0, k] = turned.T.astype(BF16)
        values = projected[WIDTH_Q + WIDTH_K : WIDTH_Q + 2 * WIDTH_K]
        v_t[0] = values.astype(BF16)
        for k in range(KV_HEADS):
            v_n[0, k] = values[k * HEAD_DIM : (k + 1) * HEAD_DIM].T.astype(BF16)
        gate[0] = projected[WIDTH_Q + 2 * WIDTH_K : WIDTH_Q + 2 * WIDTH_K + 16]

    @pl.when(block * PROJ_BLOCK >= lens[lane])
    def _():
        for ref in (q_t, k_n, k_t, v_n, v_t):
            ref[...] = jnp.zeros_like(ref)


def col_map(lane, block, lens):
    return (lane, 0, last_block(lens, lane, block))


def mlp_row_map(lane, block, lens):
    return (lane, jnp.minimum(block, (lens[lane] - 1) // MLP_BLOCK), 0)


def mlp_col_map(lane, block, lens):
    return (lane, 0, jnp.minimum(block, (lens[lane] - 1) // MLP_BLOCK))


def proj_col_map(lane, block, lens):
    return (lane, 0, jnp.minimum(block, (lens[lane] - 1) // PROJ_BLOCK))


def proj_table_map(lane, block, lens):
    return (0, jnp.minimum(block, (lens[lane] - 1) // PROJ_BLOCK))


def full_head_map(lane, block, lens):
    return (lane, 0, block, 0)


def project(lens, tokens_t, w_in, gain_cols, head_gains, cosine, sine):
    lanes = tokens_t.shape[0]
    shape = jax.ShapeDtypeStruct
    return pl.pallas_call(
        project_kernel,
        name="project",
        grid_spec=pltpu.PrefetchScalarGridSpec(
            num_scalar_prefetch=1,
            grid=(lanes, PROJ_BLOCKS),
            in_specs=[
                pl.BlockSpec((1, D, PROJ_BLOCK), proj_col_map),
                whole((D, QKVG_PAD)),
                whole((2, D, 1)),
                whole((2, HEAD_DIM, 1)),
                pl.BlockSpec((HALF, PROJ_BLOCK), proj_table_map),
                pl.BlockSpec((HALF, PROJ_BLOCK), proj_table_map),
            ],
            out_specs=[
                pl.BlockSpec((1, WIDTH_Q, PROJ_BLOCK), full_col_map),
                pl.BlockSpec((1, KV_HEADS, PROJ_BLOCK, HEAD_DIM), full_head_map),
                pl.BlockSpec((1, WIDTH_K, PROJ_BLOCK), full_col_map),
                pl.BlockSpec((1, KV_HEADS, PROJ_BLOCK, HEAD_DIM), full_head_map),
                pl.BlockSpec((1, WIDTH_K, PROJ_BLOCK), full_col_map),
                pl.BlockSpec((1, WIDTH_Q + WIDTH_K, PROJ_BLOCK), proj_col_map),
                pl.BlockSpec((1, 16, PROJ_BLOCK), proj_col_map),
            ],
            scratch_shapes=[pltpu.VMEM((QKVG_PAD, D), BF16)],
        ),
        out_shape=[
            shape((lanes, WIDTH_Q, LANE), BF16),
            shape((lanes, KV_HEADS, LANE, HEAD_DIM), BF16),
            shape((lanes, WIDTH_K, LANE), BF16),
            shape((lanes, KV_HEADS, LANE, HEAD_DIM), BF16),
            shape((lanes, WIDTH_K, LANE), BF16),
            shape((lanes, WIDTH_Q + WIDTH_K, LANE), F32),
            shape((lanes, 16, LANE), F32),
        ],
        cost_estimate=pl.CostEstimate(flops=0, bytes_accessed=0, transcendentals=0),
        compiler_params=pltpu.CompilerParams(vmem_limit_bytes=VMEM_LIMIT),
    )(lens, tokens_t, w_in, gain_cols, head_gains, cosine, sine)


def causal_tile(values, fill):
    key_pos = lax.broadcasted_iota(jnp.int32, values.shape, 0)
    query_pos = lax.broadcasted_iota(jnp.int32, values.shape, 1)
    return jnp.where(key_pos <= query_pos, values, fill)


def attend_kernel(lens, q_t, k_n, v_t, out_t, log_total):
    lane, block = pl.program_id(0), pl.program_id(1)
    log_total[0] = jnp.zeros((16, BLOCK), F32)

    for level in range(BLOCKS):

        @pl.when((block == level) & (level * BLOCK < lens[lane]))
        def _():
            before = level * BLOCK
            for head in range(HEADS):
                g = head // GROUP
                query = q_t[0, head * HEAD_DIM : (head + 1) * HEAD_DIM]
                values = v_t.at[0, g * HEAD_DIM : (g + 1) * HEAD_DIM]
                weights = jnp.exp2(dot(k_n[0, g, before : before + BLOCK], query, 1, 0) * EXP_SCALE)
                weights = causal_tile(weights, 0.0)
                total = jnp.sum(weights, axis=0, keepdims=True)
                mixed = dot(values[:, before : before + BLOCK], weights.astype(BF16), 1, 0)
                if before:
                    weights = jnp.exp2(dot(k_n[0, g, :before], query, 1, 0) * EXP_SCALE)
                    total += jnp.sum(weights, axis=0, keepdims=True)
                    mixed += dot(values[:, :before], weights.astype(BF16), 1, 0)
                out_t[0, head * HEAD_DIM : (head + 1) * HEAD_DIM] = mixed * (1.0 / total)
                log_total[0, head : head + 1] = jnp.log2(total)


def attend(lens, q_t, k_n, v_t):
    lanes = q_t.shape[0]
    shape = jax.ShapeDtypeStruct
    return pl.pallas_call(
        attend_kernel,
        name="attend",
        grid_spec=pltpu.PrefetchScalarGridSpec(
            num_scalar_prefetch=1,
            grid=(lanes, BLOCKS),
            in_specs=[
                pl.BlockSpec((1, WIDTH_Q, BLOCK), col_map),
                pl.BlockSpec((1, KV_HEADS, LANE, HEAD_DIM), lambda lane, block, lens: (lane, 0, 0, 0)),
                pl.BlockSpec((1, WIDTH_K, LANE), lambda lane, block, lens: (lane, 0, 0)),
            ],
            out_specs=[
                pl.BlockSpec((1, WIDTH_Q, BLOCK), col_map),
                pl.BlockSpec((1, 16, BLOCK), full_col_map),
            ],
        ),
        out_shape=[
            shape((lanes, WIDTH_Q, LANE), F32),
            shape((lanes, 16, LANE), F32),
        ],
        cost_estimate=pl.CostEstimate(flops=0, bytes_accessed=0, transcendentals=0),
        compiler_params=pltpu.CompilerParams(vmem_limit_bytes=VMEM_LIMIT),
    )(lens, q_t, k_n, v_t)


OUT_ROWS = WIDTH_Q * D // 128
MLP_ROWS = D * 2 * FF // 128
DOWN_ROWS = FF * D // 128
LATE_ROWS = OUT_ROWS + MLP_ROWS + DOWN_ROWS
WIDE_TILES = 2 * FF // 128
WIDE_STEP = 48
PAIR_STEP = 32
PAIR_ROWS = PAIR_STEP * 9


def pack_wide(source, target, stage, first_row):
    @pl.loop(0, D // WIDE_STEP)
    def _(piece):
        rows = pl.ds(pl.multiple_of(piece * WIDE_STEP, WIDE_STEP), WIDE_STEP)
        for tile in range(WIDE_TILES):
            stage[pl.ds(tile, WIDE_STEP, stride=WIDE_TILES), :] = source[rows, tile * 128 : (tile + 1) * 128]
        size = WIDE_STEP * WIDE_TILES
        target[pl.ds(pl.multiple_of(first_row + piece * size, 16), size), :] = stage[:size].astype(BF16)


def set_tiles(target, value):
    for t in range(4):
        target[t] = value[:, t * 128 : (t + 1) * 128]
    target[4, :, :64] = value[:, 512:]


def pack_pairs(rows_ref, stage):
    tiles = [rows_ref[t, pl.ds(parity, PAIR_STEP, stride=2), :] for parity in range(2) for t in range(5)]
    even, odd = tiles[:5], tiles[5:]
    for t in range(4):
        stage[pl.ds(t, PAIR_STEP, stride=9), :] = even[t]
    stage[pl.ds(4, PAIR_STEP, stride=9), :] = jnp.concatenate([even[4][:, :64], odd[0][:, :64]], axis=1)
    for t in range(4):
        right = odd[t + 1][:, :64]
        stage[pl.ds(5 + t, PAIR_STEP, stride=9), :] = jnp.concatenate([odd[t][:, 64:], right], axis=1)


def mlp_kernel(lens, att_t, gate, tok_t, gains, w_out, w_mlp, w_down, out_parts, hidden_in, act_low, gate_slope, up_slope, total):
    lane, block = pl.program_id(0), pl.program_id(1)

    @pl.when(block * MLP_BLOCK >= lens[lane])
    def _():
        out_parts[...] = jnp.zeros_like(out_parts)

    @pl.when(block * MLP_BLOCK < lens[lane])
    def _():
        att = att_t[0].reshape(HEADS, HEAD_DIM, MLP_BLOCK)
        sig = jax.nn.sigmoid(gate[0, :HEADS])[:, None, :]
        gated_t = (att * sig).reshape(WIDTH_Q, MLP_BLOCK).astype(BF16)
        hidden = tok_t[0].T.astype(F32) + dot(gated_t, w_out[...], 0, 0)
        hidden_in[0] = hidden
        mixed = (hidden * mean_square_scale(hidden, 1) * gains[1:2]).astype(BF16)
        valid_t = lax.broadcasted_iota(jnp.int32, (1, MLP_BLOCK), 1) + block * MLP_BLOCK < lens[lane]
        total[...] = hidden

        @pl.loop(0, FF // FF_CHUNK, unroll=True)
        def _(chunk):
            low = pl.ds(pl.multiple_of(chunk * FF_CHUNK, FF_CHUNK), FF_CHUNK)
            high = pl.ds(pl.multiple_of(FF + chunk * FF_CHUNK, FF_CHUNK), FF_CHUNK)
            g = dot(mixed, w_mlp[:, low], 1, 0)
            u = dot(mixed, w_mlp[:, high], 1, 0)
            s = jax.nn.sigmoid(g)
            gs = g * s
            act = (gs * u).astype(BF16)
            total[...] += dot(act, w_down[low, :], 1, 0)
            act_low[0, :, low] = act
            gate_slope[0, :, low] = (u * (s * (1.0 + g * (1.0 - s)))).astype(BF16)
            up_slope[0, :, low] = gs.astype(BF16)

        out_t = jnp.where(valid_t, total[...].T, 0.0).astype(BF16)
        width = out_parts.shape[3]
        for part in range(out_parts.shape[0]):
            out_parts[part, 0] = out_t[:, part * width : (part + 1) * width]


def part_map(lane, block, lens):
    return (block, lane, 0, 0)


def kept_part_map(lane, block, lens):
    return (jnp.minimum(block, (lens[lane] - 1) // MLP_BLOCK), lane, 0, 0)


def mlp(lens, att_t, gate, tokens_t, gains, w_out, w_mlp, w_down, dp_size):
    lanes = tokens_t.shape[0]
    width = LANE // dp_size
    shape = jax.ShapeDtypeStruct
    return pl.pallas_call(
        mlp_kernel,
        name="mlp",
        grid_spec=pltpu.PrefetchScalarGridSpec(
            num_scalar_prefetch=1,
            grid=(lanes, MLP_BLOCKS),
            in_specs=[
                pl.BlockSpec((1, WIDTH_Q, MLP_BLOCK), mlp_col_map),
                pl.BlockSpec((1, 16, MLP_BLOCK), mlp_col_map),
                pl.BlockSpec((1, D, MLP_BLOCK), mlp_col_map),
                whole((2, D)),
                whole((WIDTH_Q, D)),
                whole((D, 2 * FF)),
                whole((FF, D)),
            ],
            out_specs=[
                pl.BlockSpec((dp_size // MLP_BLOCKS, 1, D, width), part_map),
                pl.BlockSpec((1, MLP_BLOCK, D), mlp_row_map),
                pl.BlockSpec((1, MLP_BLOCK, FF), mlp_row_map),
                pl.BlockSpec((1, MLP_BLOCK, FF), mlp_row_map),
                pl.BlockSpec((1, MLP_BLOCK, FF), mlp_row_map),
            ],
            scratch_shapes=[pltpu.VMEM((MLP_BLOCK, D), F32)],
        ),
        out_shape=[
            shape((dp_size, lanes, D, width), BF16),
            shape((lanes, LANE, D), F32),
            shape((lanes, LANE, FF), BF16),
            shape((lanes, LANE, FF), BF16),
            shape((lanes, LANE, FF), BF16),
        ],
        compiler_params=pltpu.CompilerParams(vmem_limit_bytes=VMEM_LIMIT),
    )(lens, att_t, gate, tokens_t, gains, w_out, w_mlp, w_down)


def mlp_back_kernel(lens, att_t, gate, cot_parts, hidden_in, act_low, gate_slope, up_slope, gains, w_out, w_mlp, w_down,
                    grad_hidden_t, grad_att_t, logit_delta, kept, sent, g_gain,
                    back, g_out, g_mlp, g_down_t, late, stage, pair_rows, copy_sem):
    lane, block = pl.program_id(0), pl.program_id(1)

    @pl.when((lane == 0) & (block == 0))
    def _():
        g_out[...] = jnp.zeros_like(g_out)
        g_mlp[...] = jnp.zeros_like(g_mlp)
        g_down_t[...] = jnp.zeros_like(g_down_t)
        g_gain[...] = jnp.zeros_like(g_gain)

    @pl.when(block * MLP_BLOCK >= lens[lane])
    def _():
        grad_att_t[...] = jnp.zeros_like(grad_att_t)
        logit_delta[...] = jnp.zeros_like(logit_delta)

    @pl.when(block * MLP_BLOCK < lens[lane])
    def _():
        att = att_t[0].reshape(HEADS, HEAD_DIM, MLP_BLOCK)
        sig = jax.nn.sigmoid(gate[0, :HEADS])[:, None, :]
        gated_t = (att * sig).reshape(WIDTH_Q, MLP_BLOCK).astype(BF16)
        hidden = hidden_in[0]
        scale = mean_square_scale(hidden, 1)
        gain = gains[1:2]
        mixed_t = (hidden * scale * gain).astype(BF16).T
        valid_t = lax.broadcasted_iota(jnp.int32, (1, MLP_BLOCK), 1) + block * MLP_BLOCK < lens[lane]
        cot_t = jnp.concatenate([cot_parts[part, 0] for part in range(cot_parts.shape[0])], axis=1)
        grad_low_t = jnp.where(valid_t, cot_t.astype(F32), 0.0).astype(BF16)
        grad_low = grad_low_t.T
        back[...] = jnp.zeros_like(back)

        @pl.loop(0, FF // FF_CHUNK, unroll=True)
        def _(chunk):
            low = pl.ds(pl.multiple_of(chunk * FF_CHUNK, FF_CHUNK), FF_CHUNK)
            high = pl.ds(pl.multiple_of(FF + chunk * FF_CHUNK, FF_CHUNK), FF_CHUNK)
            a = dot(grad_low, w_down[low, :], 1, 1)
            grad_gate = (a * gate_slope[0, :, low].astype(F32)).astype(BF16)
            grad_up = (a * up_slope[0, :, low].astype(F32)).astype(BF16)
            back[...] += dot(grad_gate, w_mlp[:, low], 1, 1) + dot(grad_up, w_mlp[:, high], 1, 1)
            g_mlp[:, low] += dot(mixed_t, grad_gate, 1, 0)
            g_mlp[:, high] += dot(mixed_t, grad_up, 1, 0)
            g_down_t[:, low] += dot(grad_low_t, act_low[0, :, low], 1, 0)

        b = back[...]
        g_gain[0:1] += jnp.sum(b * hidden * scale, axis=0, keepdims=True)
        bg = b * gain
        grad_h = grad_low.astype(F32) + scale * bg - hidden * (scale * scale * scale * jnp.mean(hidden * bg, axis=1, keepdims=True))
        grad_hidden_t[0] = grad_h.T
        branch = grad_h.astype(BF16)
        g_out[...] += dot(gated_t, branch, 1, 0)
        c = dot(w_out[...], branch, 1, 1).reshape(HEADS, HEAD_DIM, MLP_BLOCK)
        grad_att = (c * sig).astype(BF16)
        grad_att_t[0] = grad_att.reshape(WIDTH_Q, MLP_BLOCK)
        sig2 = sig[:, 0, :]
        logit_delta[0, :HEADS] = jnp.sum(c * att, axis=1) * (sig2 * (1.0 - sig2))
        logit_delta[0, 16 : 16 + HEADS] = jnp.sum(grad_att.astype(F32) * att, axis=1)

    @pl.when((lane == pl.num_programs(0) - 1) & (block == pl.num_programs(1) - 1))
    def _():
        @pl.loop(0, WIDTH_Q // (2 * PAIR_STEP))
        def _(piece):
            set_tiles(pair_rows, g_out[pl.ds(pl.multiple_of(piece * 2 * PAIR_STEP, 2 * PAIR_STEP), 2 * PAIR_STEP), :])
            pack_pairs(pair_rows, stage)
            late[pl.ds(pl.multiple_of(piece * PAIR_ROWS, 16), PAIR_ROWS), :] = stage[:PAIR_ROWS].astype(BF16)

        pack_wide(g_mlp, late, stage, OUT_ROWS)

        @pl.loop(0, FF // 128)
        def _(piece):
            turned = g_down_t[:, pl.ds(pl.multiple_of(piece * 128, 128), 128)].T
            for h in range(128 // (2 * PAIR_STEP)):
                set_tiles(pair_rows, turned[h * 2 * PAIR_STEP : (h + 1) * 2 * PAIR_STEP])
                pack_pairs(pair_rows, stage)
                start = OUT_ROWS + MLP_ROWS + (piece * 2 + h) * PAIR_ROWS
                late[pl.ds(pl.multiple_of(start, 16), PAIR_ROWS), :] = stage[:PAIR_ROWS].astype(BF16)

        late[LATE_ROWS:] = jnp.zeros((late.shape[0] - LATE_ROWS, 128), BF16)
        low = bit_of(lax.axis_index("zero"), 0)
        copies = []
        for h in range(2):
            for side, target in enumerate((kept, sent)):
                start = pl.multiple_of(window_start(2 * h + (low if side == 0 else 1 - low)), 16)
                copies.append(pltpu.make_async_copy(late.at[pl.ds(start, kept.shape[1])], target.at[h], copy_sem.at[h, side]))
        for copy in copies:
            copy.start()
        for copy in copies:
            copy.wait()


def mlp_back(lens, att_t, gate, cot_parts, hidden_in, act_low, gate_slope, up_slope, gains, w_out, w_mlp, w_down, window):
    dp_size, lanes, _, width = cot_parts.shape
    shape = jax.ShapeDtypeStruct
    return pl.pallas_call(
        mlp_back_kernel,
        name="mlp_back",
        grid_spec=pltpu.PrefetchScalarGridSpec(
            num_scalar_prefetch=1,
            grid=(lanes, MLP_BLOCKS),
            in_specs=[
                pl.BlockSpec((1, WIDTH_Q, MLP_BLOCK), mlp_col_map),
                pl.BlockSpec((1, 16, MLP_BLOCK), mlp_col_map),
                pl.BlockSpec((dp_size // MLP_BLOCKS, 1, D, width), kept_part_map),
                pl.BlockSpec((1, MLP_BLOCK, D), mlp_row_map),
                pl.BlockSpec((1, MLP_BLOCK, FF), mlp_row_map),
                pl.BlockSpec((1, MLP_BLOCK, FF), mlp_row_map),
                pl.BlockSpec((1, MLP_BLOCK, FF), mlp_row_map),
                whole((2, D)),
                whole((WIDTH_Q, D)),
                whole((D, 2 * FF)),
                whole((FF, D)),
            ],
            out_specs=[
                pl.BlockSpec((1, D, MLP_BLOCK), mlp_col_map),
                pl.BlockSpec((1, WIDTH_Q, MLP_BLOCK), full_col_map),
                pl.BlockSpec((1, 32, MLP_BLOCK), full_col_map),
                pl.BlockSpec(memory_space=pl.ANY),
                pl.BlockSpec(memory_space=pl.ANY),
                whole((8, D)),
            ],
            scratch_shapes=[
                pltpu.VMEM((MLP_BLOCK, D), F32),
                pltpu.VMEM((WIDTH_Q, D), F32),
                pltpu.VMEM((D, 2 * FF), F32),
                pltpu.VMEM((D, FF), F32),
                pltpu.VMEM((LAST_WINDOW + window, 128), BF16),
                pltpu.VMEM((WIDE_STEP * WIDE_TILES, 128), F32),
                pltpu.VMEM((5, 2 * PAIR_STEP, 128), F32),
                pltpu.SemaphoreType.DMA((2, 2)),
            ],
        ),
        out_shape=[
            shape((lanes, D, LANE), F32),
            shape((lanes, WIDTH_Q, LANE), BF16),
            shape((lanes, 32, LANE), F32),
            shape((2, window, 128), BF16),
            shape((2, window, 128), BF16),
            shape((8, D), F32),
        ],
        compiler_params=pltpu.CompilerParams(vmem_limit_bytes=VMEM_LIMIT),
    )(lens, att_t, gate, cot_parts, hidden_in, act_low, gate_slope, up_slope, gains, w_out, w_mlp, w_down)


def project_back_kernel(lens, dq_t, dk_t, dv_t, logit_delta, raw, tok_t, grad_hidden_t, w_in, gain_cols, head_gains,
                        cosine, sine, grad_tok_t, g_in, g_gain, g_head, dproj, head_sum, gain_sum):
    lane, block = pl.program_id(0), pl.program_id(1)

    @pl.when((lane == 0) & (block == 0))
    def _():
        g_in[...] = jnp.zeros_like(g_in)
        gain_sum[...] = jnp.zeros_like(gain_sum)
        head_sum[...] = jnp.zeros_like(head_sum)

    @pl.when(block * PROJ_BLOCK >= lens[lane])
    def _():
        grad_tok_t[...] = jnp.zeros_like(grad_tok_t)

    @pl.when(block * PROJ_BLOCK < lens[lane])
    def _():
        cos, sin = cosine[...], sine[...]
        for head in range(HEADS + KV_HEADS):
            rows = slice(head * HEAD_DIM, (head + 1) * HEAD_DIM)
            side = 0 if head < HEADS else 1
            source = dq_t if head < HEADS else dk_t
            at = (head if head < HEADS else head - HEADS) * HEAD_DIM
            d1, d2 = source[0, at : at + HALF], source[0, at + HALF : at + HEAD_DIM]
            d = jnp.concatenate([d1 * cos + d2 * sin, d2 * cos - d1 * sin], axis=0)
            u = raw[0, rows]
            r = mean_square_scale(u, 0)
            ur = u * r
            head_sum[side] += d * ur
            dg = d * head_gains[side]
            dproj[rows] = (r * (dg - ur * jnp.mean(ur * dg, axis=0, keepdims=True))).astype(BF16)
        dproj[WIDTH_Q + WIDTH_K : WIDTH_Q + 2 * WIDTH_K] = dv_t[0].astype(BF16)
        row = lax.broadcasted_iota(jnp.int32, (16, PROJ_BLOCK), 0)
        logits = jnp.where(row < HEADS, logit_delta[0], 0.0).astype(BF16)
        dproj[WIDTH_Q + 2 * WIDTH_K :] = jnp.concatenate(
            [logits, jnp.zeros((QKVG_PAD - WIDTH_Q - 2 * WIDTH_K - 16, PROJ_BLOCK), BF16)], axis=0
        )
        x = tok_t[0].astype(F32)
        scale = mean_square_scale(x, 0)
        xs = x * scale
        gain = gain_cols[0]
        normed = (xs * gain).astype(BF16)
        g_in[...] += dot(normed, dproj[...], 1, 1)
        back = dot(w_in[...], dproj[...], 1, 0)
        gain_sum[...] += back * xs
        bg = back * gain
        grad_x = scale * (bg - xs * jnp.mean(xs * bg, axis=0, keepdims=True))
        grad_tok_t[0] = (grad_hidden_t[0] + grad_x).astype(BF16)

    @pl.when((lane == pl.num_programs(0) - 1) & (block == pl.num_programs(1) - 1))
    def _():
        g_head[...] = jnp.sum(head_sum[...], axis=2)
        g_gain[...] = jnp.sum(gain_sum[...], axis=1)[None]


def project_back(lens, dq_t, dk_t, dv_t, logit_delta, raw, tokens_t, grad_hidden_t, w_in, gain_cols, head_gains, cosine, sine):
    lanes = tokens_t.shape[0]
    shape = jax.ShapeDtypeStruct
    full_col = lambda lane, block, lens: (lane, 0, block)
    return pl.pallas_call(
        project_back_kernel,
        name="project_back",
        grid_spec=pltpu.PrefetchScalarGridSpec(
            num_scalar_prefetch=1,
            grid=(lanes, PROJ_BLOCKS),
            in_specs=[
                pl.BlockSpec((1, WIDTH_Q, PROJ_BLOCK), proj_col_map),
                pl.BlockSpec((1, WIDTH_K, PROJ_BLOCK), proj_col_map),
                pl.BlockSpec((1, WIDTH_K, PROJ_BLOCK), proj_col_map),
                pl.BlockSpec((1, 16, PROJ_BLOCK), proj_col_map),
                pl.BlockSpec((1, WIDTH_Q + WIDTH_K, PROJ_BLOCK), proj_col_map),
                pl.BlockSpec((1, D, PROJ_BLOCK), proj_col_map),
                pl.BlockSpec((1, D, PROJ_BLOCK), proj_col_map),
                whole((D, QKVG_PAD)),
                whole((2, D, 1)),
                whole((2, HEAD_DIM, 1)),
                pl.BlockSpec((HALF, PROJ_BLOCK), proj_table_map),
                pl.BlockSpec((HALF, PROJ_BLOCK), proj_table_map),
            ],
            out_specs=[
                pl.BlockSpec((1, D, PROJ_BLOCK), full_col),
                whole((D, QKVG_PAD)),
                whole((1, D)),
                whole((2, HEAD_DIM)),
            ],
            scratch_shapes=[
                pltpu.VMEM((QKVG_PAD, PROJ_BLOCK), BF16),
                pltpu.VMEM((2, HEAD_DIM, PROJ_BLOCK), F32),
                pltpu.VMEM((D, PROJ_BLOCK), F32),
            ],
        ),
        out_shape=[
            shape((lanes, D, LANE), BF16),
            shape((D, QKVG_PAD), F32),
            shape((1, D), F32),
            shape((2, HEAD_DIM), F32),
        ],
        cost_estimate=pl.CostEstimate(flops=20_000_000_000, bytes_accessed=60_000_000, transcendentals=0),
        compiler_params=pltpu.CompilerParams(vmem_limit_bytes=VMEM_LIMIT),
    )(lens, dq_t, dk_t, dv_t, logit_delta, raw, tokens_t, grad_hidden_t, w_in, gain_cols, head_gains, cosine, sine)


def layer_forward(tokens_t, lens, weights):
    w_in, gains, head_gains = weights
    gain_cols, head_gains = gains[:, :, None], head_gains[:, :, None]
    cosine, sine = (jnp.asarray(t) for t in rope_tables())
    q_t, k_n, k_t, v_n, v_t, raw, gate = project(lens, tokens_t, w_in, gain_cols, head_gains, cosine, sine)
    att_t, log_total = attend(lens, q_t, k_n, v_t)
    return att_t, gate, (q_t, k_n, k_t, v_n, log_total, raw)


def head_groups(rows):
    return rows[:, :HEADS].reshape(rows.shape[0], KV_HEADS, GROUP, LANE)


SHARD = PARAMS // 4
LANES128 = 128
EDGE = 16
STEP = 6928
BODY = STEP - EDGE
SPAN = STEP + EDGE
IN_ROWS = 4361
SPLIT_AT = D * QKVG
MESH = pl.DeviceIdType.MESH


def shard_shift(s):
    offset = EDGE * LANES128 - (STEP * LANES128 - SHARD) * s + (64 if s else 0)
    return offset // LANES128, offset % LANES128


def flip(index, bit):
    return index + (1 - 2 * (index // (1 << bit) % 2)) * (1 << bit)


def bit_of(index, bit):
    return index // (1 << bit) % 2


def greet(partners):
    barrier = pltpu.get_barrier_semaphore()
    for partner in partners:
        pl.semaphore_signal(barrier, inc=1, device_id=partner, device_id_type=MESH)
    pl.semaphore_wait(barrier, len(partners))


PACK_TILE = 496
FIRST_ROWS = 4368
LAST_TILE = 32
GAIN_AT = EDGE + IN_ROWS + LATE_ROWS - 3 * STEP - (SPAN - LAST_TILE)
FIRST_PIECES = 8
FIRST_CUTS = (0, 544, 1088, 1632, 2176, 2720, 3264, 3808, FIRST_ROWS)
FIRST_TILES = -(-(EDGE + FIRST_ROWS) // PACK_TILE)


def pack_kernel(master, own, first_rows, last_rows, rows_in, packed, load_sem, keep_sem, own_sem, send_sem, recv_sem):
    dp, zero = lax.axis_index("dp"), lax.axis_index("zero")
    core, across, side = (dp, flip(zero, 0)), (dp, flip(zero, 1)), (flip(dp, 0), zero)
    y = bit_of(dp, 0)
    load = pltpu.make_async_copy(master, rows_in.at[pl.ds(24, STEP)], load_sem)
    load.start()
    rows_in[:24] = jnp.zeros((24, LANES128), F32)
    rows_in[24 + STEP :] = jnp.zeros((24, LANES128), F32)
    greet((core, across, side))
    load.wait()
    lane = lax.broadcasted_iota(jnp.int32, (PACK_TILE, LANES128), 1)

    def shifted(start, a, k):
        if k == 0:
            return rows_in[pl.ds(start + 24 - a, PACK_TILE), :]
        here = pltpu.roll(rows_in[pl.ds(start + 24 - a, PACK_TILE), :], k, 1)
        above = pltpu.roll(rows_in[pl.ds(start + 23 - a, PACK_TILE), :], k, 1)
        return jnp.where(lane >= k, here, above)

    def pack(s, start):
        if s == 0 and start + PACK_TILE <= EDGE + IN_ROWS:
            value = shifted(start, EDGE, 0)
        elif s == 0 and start < EDGE + IN_ROWS:
            row = lax.broadcasted_iota(jnp.int32, (PACK_TILE, LANES128), 0) + start
            value = jnp.where(row < EDGE + IN_ROWS, shifted(start, EDGE, 0), shifted(start, EDGE, 64))
        elif s == 0:
            value = shifted(start, EDGE, 64)
        else:
            value = shifted(start, *shard_shift(s))
        packed[pl.ds(start, PACK_TILE), :] = value.astype(BF16)

    def piece_rows(piece):
        return pl.ds(EDGE + FIRST_CUTS[piece], FIRST_CUTS[piece + 1] - FIRST_CUTS[piece])

    def mine(piece):
        return packed.at[piece_rows(piece)]

    def theirs(piece):
        return first_rows.at[piece_rows(piece)]

    def copy(source, target, device, slot):
        return pltpu.make_async_remote_copy(source, target, send_sem.at[slot], recv_sem.at[slot],
                                            device_id=device, device_id_type=MESH)

    def pieces_of(half):
        return range(half * FIRST_PIECES // 2, (half + 1) * FIRST_PIECES // 2)

    def send_first():
        for half in range(2):

            @pl.when(y == half)
            def _():
                for piece in pieces_of(half):
                    copy(mine(piece), theirs(piece), across, piece).start()

        for piece in range(FIRST_PIECES):
            copy(mine(piece), theirs(piece), core, FIRST_PIECES + piece).start()

    for s in range(4):

        @pl.when(zero == s)
        def _():
            for t in range(SPAN // PACK_TILE):
                pack(s, t * PACK_TILE)
                if s == 0 and t + 1 == FIRST_TILES:
                    send_first()

    keep = pltpu.make_async_copy(packed, own, own_sem)
    keep.start()
    tail = packed.at[pl.ds(SPAN - LAST_TILE, LAST_TILE)]

    @pl.when(zero == 3)
    def _():
        copy(tail, last_rows, across, 2 * FIRST_PIECES + 1).start()
        copy(tail, last_rows, core, 2 * FIRST_PIECES).start()
        stay = pltpu.make_async_copy(tail, last_rows, keep_sem)
        stay.start()
        stay.wait()
        copy(tail, last_rows, across, 2 * FIRST_PIECES + 1).wait_send()
        copy(tail, last_rows, core, 2 * FIRST_PIECES).wait_send()

    @pl.when(zero == 1)
    def _():
        copy(last_rows, last_rows, across, 2 * FIRST_PIECES + 1).wait_recv()
        copy(last_rows, last_rows, core, 2 * FIRST_PIECES).start()
        copy(last_rows, last_rows, core, 2 * FIRST_PIECES).wait_send()

    for half in range(2):
        pieces, others = pieces_of(half), pieces_of(1 - half)

        @pl.when((zero == 0) & (y == half))
        def _():
            stay = pltpu.make_async_copy(packed.at[pl.ds(EDGE, FIRST_ROWS)], first_rows.at[pl.ds(EDGE, FIRST_ROWS)], keep_sem)
            stay.start()
            for piece in pieces:
                copy(mine(piece), theirs(piece), across, piece).wait_send()
            for piece in range(FIRST_PIECES):
                copy(mine(piece), theirs(piece), core, FIRST_PIECES + piece).wait_send()
            stay.wait()

        @pl.when((zero == 2) & (y == half))
        def _():
            for piece in pieces:
                copy(theirs(piece), theirs(piece), across, piece).wait_recv()
                copy(theirs(piece), theirs(piece), side, piece).start()
                copy(theirs(piece), theirs(piece), core, FIRST_PIECES + piece).start()
            for piece in others:
                copy(theirs(piece), theirs(piece), side, piece).wait_recv()
                copy(theirs(piece), theirs(piece), core, FIRST_PIECES + piece).start()
            for piece in pieces:
                copy(theirs(piece), theirs(piece), side, piece).wait_send()
            for piece in range(FIRST_PIECES):
                copy(theirs(piece), theirs(piece), core, FIRST_PIECES + piece).wait_send()

    @pl.when(bit_of(zero, 0) == 0)
    def _():
        copy(last_rows, last_rows, core, 2 * FIRST_PIECES).wait_recv()

    @pl.when(bit_of(zero, 0) == 1)
    def _():
        for piece in range(FIRST_PIECES):
            copy(theirs(piece), theirs(piece), core, FIRST_PIECES + piece).wait_recv()

    keep.wait()


def pack_master(master):
    rows = jnp.pad(master, (0, STEP * LANES128 - SHARD)).reshape(STEP, LANES128)
    shape = jax.ShapeDtypeStruct
    return pl.pallas_call(
        pack_kernel,
        name="pack_master",
        out_shape=[shape((SPAN, LANES128), BF16), shape((EDGE + FIRST_ROWS, LANES128), BF16), shape((LAST_TILE, LANES128), BF16)],
        in_specs=[pl.BlockSpec(memory_space=pl.ANY)],
        out_specs=[pl.BlockSpec(memory_space=pl.ANY)] * 3,
        scratch_shapes=[
            pltpu.VMEM((24 + STEP + 24, LANES128), F32),
            pltpu.VMEM((SPAN, LANES128), BF16),
            pltpu.SemaphoreType.DMA,
            pltpu.SemaphoreType.DMA,
            pltpu.SemaphoreType.DMA,
            pltpu.SemaphoreType.DMA((2 * FIRST_PIECES + 2,)),
            pltpu.SemaphoreType.DMA((2 * FIRST_PIECES + 2,)),
        ],
        cost_estimate=pl.CostEstimate(flops=0, bytes_accessed=0, transcendentals=0),
        compiler_params=pltpu.CompilerParams(collective_id=0, has_side_effects=True, vmem_limit_bytes=VMEM_LIMIT),
    )(rows)


REDUCE_PARTS = 11


def window_start(s):
    return jnp.minimum(s, 1) * (((s * SHARD + 64) // LANES128 - IN_ROWS) // 16 * 16)


LAST_WINDOW = ((3 * SHARD + 64) // LANES128 - IN_ROWS) // 16 * 16


def window_rows(dp_size):
    unit = REDUCE_PARTS * 16 * dp_size
    return -(-(SHARD // LANES128 + 17) // unit) * unit


CLASSES = ((0, 6), (6, 5))


def bit_order(bits, kind):
    order = list(range(bits))
    if kind and bits > 1:
        order[0], order[1] = 1, 0
    return order


def part_region(dp, rows, bits, kind, count):
    offset, size = 0, rows
    for k in bit_order(bits, kind)[:count]:
        size = size // 2
        offset = offset + bit_of(dp, k) * size
    return offset, size


def aligned(offset, size):
    return pl.ds(pl.multiple_of(offset, 16), size)


LATE_HOP = 12.0


def arrival_order(chains, hops):
    free, order = {}, []
    pending = [(0.0, index, 0) for index in range(len(chains))]
    while pending:
        pending.sort()
        start, index, step = pending.pop(0)
        link, span = chains[index][step]
        end = max(start, free.get(link, 0.0)) + span
        free[link] = end
        hop = hops[index]
        order.append((end + hop, index, step))
        if step + 1 < len(chains[index]):
            pending.append((end + hop, index, step + 1))
    return sorted(order)


def attend_back_kernel(lens, q_t, k_n, k_t, v_n, grad_t, log_total, delta, dq_t, dk_t, dv_t):
    lane = pl.program_id(0)
    dq_t[...] = jnp.zeros_like(dq_t)
    for block in range(BLOCKS):
        keys = pl.ds(block * BLOCK, BLOCK)

        @pl.when(block * BLOCK >= lens[lane])
        def _():
            dk_t[0, :, keys] = jnp.zeros((HEAD_DIM, BLOCK), F32)
            dv_t[0, :, keys] = jnp.zeros((HEAD_DIM, BLOCK), F32)

        @pl.when(block * BLOCK < lens[lane])
        def _():
            k_rows, v_rows, k_cols = k_n[0, 0, keys, :], v_n[0, 0, keys, :], k_t[0, :, keys]
            dk = jnp.zeros((HEAD_DIM, BLOCK), F32)
            dv = jnp.zeros((HEAD_DIM, BLOCK), F32)
            cols = pl.ds(block * BLOCK, LANE - block * BLOCK)
            for r in range(GROUP):
                head = slice(r * HEAD_DIM, (r + 1) * HEAD_DIM)
                query, grad = q_t[0, head, cols], grad_t[0, head, cols]
                prob = jnp.exp2(dot(k_rows, query, 1, 0) * EXP_SCALE - log_total[0, 0, r : r + 1, cols])
                prob = causal_tile(prob, 0.0)
                grad_prob = dot(v_rows, grad, 1, 0) - delta[0, 0, r : r + 1, cols]
                grad_score = (prob * grad_prob).astype(BF16)
                dv += dot(grad, prob.astype(BF16), 1, 1)
                dk += dot(query, grad_score, 1, 1)
                dq_t[0, head, cols] += dot(k_cols, grad_score, 1, 0) * SCALE
            dk_t[0, :, keys] = dk * SCALE
            dv_t[0, :, keys] = dv


def attend_back(lens, q_t, k_n, k_t, v_n, grad_t, log_total, delta):
    lanes = q_t.shape[0]
    shape = jax.ShapeDtypeStruct
    group_rows = lambda lane, g, lens: (lane, g, 0)
    group_heads = lambda lane, g, lens: (lane, g, 0, 0)
    return pl.pallas_call(
        attend_back_kernel,
        name="attend_back",
        grid_spec=pltpu.PrefetchScalarGridSpec(
            num_scalar_prefetch=1,
            grid=(lanes, KV_HEADS),
            in_specs=[
                pl.BlockSpec((1, GROUP * HEAD_DIM, LANE), group_rows),
                pl.BlockSpec((1, 1, LANE, HEAD_DIM), group_heads),
                pl.BlockSpec((1, HEAD_DIM, LANE), group_rows),
                pl.BlockSpec((1, 1, LANE, HEAD_DIM), group_heads),
                pl.BlockSpec((1, GROUP * HEAD_DIM, LANE), group_rows),
                pl.BlockSpec((1, 1, GROUP, LANE), group_heads),
                pl.BlockSpec((1, 1, GROUP, LANE), group_heads),
            ],
            out_specs=[
                pl.BlockSpec((1, GROUP * HEAD_DIM, LANE), group_rows),
                pl.BlockSpec((1, HEAD_DIM, LANE), group_rows),
                pl.BlockSpec((1, HEAD_DIM, LANE), group_rows),
            ],
        ),
        out_shape=[
            shape((lanes, WIDTH_Q, LANE), F32),
            shape((lanes, WIDTH_K, LANE), F32),
            shape((lanes, WIDTH_K, LANE), F32),
        ],
        cost_estimate=pl.CostEstimate(flops=40_000_000_000, bytes_accessed=40_000_000, transcendentals=0),
        compiler_params=pltpu.CompilerParams(vmem_limit_bytes=VMEM_LIMIT),
    )(lens, q_t, k_n, k_t, v_n, grad_t, log_total, delta)


TAIL_AT = 4368


HEAD_PARTS = 3
HEAD_HOP = 3.0
LATE_GROUPS = ((0, 0, 3), (1, 0, 3), (0, 3, 3), (1, 3, 2))


def head_rows(dp_size):
    unit = 2 * HEAD_PARTS * 16 * 2 * dp_size
    return -(-(TAIL_AT + 16) // unit) * unit


def sum_head_kernel(bits, rows, late_rows, source, gain_rows, late_share, result, late_sum, total, *rest):
    received, (load_sem, send_sem, recv_sem, late_send, late_recv) = rest[:-5], rest[-5:]
    dp, zero = lax.axis_index("dp"), lax.axis_index("zero")
    axes = [("zero", 1)] + [("dp", k) for k in range(bits)]

    def partner(axis, k):
        return (flip(dp, k), zero) if axis == "dp" else (dp, flip(zero, k))

    def bit(axis, k):
        return bit_of(dp if axis == "dp" else zero, k)

    load = pltpu.make_async_copy(source, total, load_sem)
    load.start()
    load.wait()
    total[TAIL_AT : TAIL_AT + 16] = gain_rows[...]
    greet([partner("zero", 0)] + [partner(*axis) for axis in axes])

    def step(index, slot, source_ref, target_ref, axis):
        copy = pltpu.make_async_remote_copy(source_ref, target_ref, send_sem.at[index, slot], recv_sem.at[index, slot],
                                            device_id=partner(*axis), device_id_type=MESH)
        copy.start()
        return copy

    def order_of(index):
        return [("zero", 0)] + [axes[(index + j) % len(axes)] for j in range(len(axes))]

    def spans_of(index):
        spans = [(axis, 0.5 if axis == ("zero", 0) else 9.0 / HEAD_PARTS / (1 << slot)) for slot, axis in enumerate(order_of(index))]
        return spans + spans[::-1]

    def chain_of(index):
        order = order_of(index)
        size = rows // HEAD_PARTS
        offset = index * size
        regions = []
        for slot, axis in enumerate(order):
            half = size // 2
            mine, other = offset + bit(*axis) * half, offset + (1 - bit(*axis)) * half
            landing = received[slot].at[index]
            yield step(index, slot, total.at[aligned(other, half)], landing, axis)
            at = aligned(mine, half)
            target = total if slot + 1 < len(order) else result
            target[at] = (total[at].astype(F32) + landing[...].astype(F32)).astype(BF16)
            offset, size = mine, half
            regions.append(at)
        for slot in reversed(range(len(order))):
            place = result.at[regions[slot]]
            yield step(index, 2 * len(order) - 1 - slot, place, place, order[slot])

    def late_spans(index):
        kind, _, count = LATE_GROUPS[index]
        spans = [(("dp", k), 20.0 / (1 << slot) * count / REDUCE_PARTS) for slot, k in enumerate(bit_order(bits, kind))]
        return spans[::-1]

    def late_chain(index):
        kind, start, count = LATE_GROUPS[index]
        parts = pl.ds(CLASSES[kind][0] + start, count)
        late_sum[parts, aligned(*part_region(dp, late_rows, bits, kind, bits))] = late_share[parts]
        for slot, k in reversed(list(enumerate(bit_order(bits, kind)))):
            place = late_sum.at[parts, aligned(*part_region(dp, late_rows, bits, kind, slot + 1))]
            copy = pltpu.make_async_remote_copy(place, place, late_send.at[index, slot], late_recv.at[index, slot],
                                                device_id=partner("dp", k), device_id_type=MESH)
            copy.start()
            yield copy

    chains = [chain_of(i) for i in range(HEAD_PARTS)] + [late_chain(i) for i in range(len(LATE_GROUPS))]
    spans = [spans_of(i) for i in range(HEAD_PARTS)] + [late_spans(i) for i in range(len(LATE_GROUPS))]
    flying = [next(chain) for chain in chains]
    sent = list(flying)
    for _, index, _ in arrival_order(spans, [HEAD_HOP] * HEAD_PARTS + [LATE_HOP] * len(LATE_GROUPS)):
        flying[index].wait_recv()
        following = next(chains[index], None)
        if following is not None:
            flying[index] = following
            sent.append(following)
    for copy in sent:
        copy.wait_send()


def sum_head(source, gain_rows, share, late_rows, dp_size):
    bits = dp_size.bit_length() - 1
    rows = source.shape[0]
    steps = bits + 2
    shape = jax.ShapeDtypeStruct
    return pl.pallas_call(
        functools.partial(sum_head_kernel, bits, rows, late_rows),
        name="sum_head",
        out_shape=[shape((rows, LANES128), BF16), shape((REDUCE_PARTS, late_rows, LANES128), BF16)],
        in_specs=[pl.BlockSpec(memory_space=pl.ANY)] + [pl.BlockSpec(memory_space=pltpu.VMEM)] * 2,
        out_specs=[pl.BlockSpec(memory_space=pltpu.VMEM)] * 2,
        scratch_shapes=[
            pltpu.VMEM((rows, LANES128), BF16),
            *[pltpu.VMEM((HEAD_PARTS, rows // HEAD_PARTS >> (k + 1), LANES128), BF16) for k in range(steps)],
            pltpu.SemaphoreType.DMA,
            pltpu.SemaphoreType.DMA((HEAD_PARTS, 2 * steps)),
            pltpu.SemaphoreType.DMA((HEAD_PARTS, 2 * steps)),
            pltpu.SemaphoreType.DMA((len(LATE_GROUPS), bits)),
            pltpu.SemaphoreType.DMA((len(LATE_GROUPS), bits)),
        ],
        compiler_params=pltpu.CompilerParams(collective_id=2, has_side_effects=True, vmem_limit_bytes=VMEM_LIMIT),
    )(source, gain_rows, share)


def flat_rows(g_in, rows):
    flat = g_in[:, :QKVG].astype(BF16).reshape(-1)
    return jnp.pad(flat, (0, rows * LANES128 - SPLIT_AT)).reshape(rows, LANES128)


def pack_gains(g_gain_one, g_gain_two, g_head):
    flat = jnp.concatenate([g_gain_one[0], g_gain_two[0], g_head.reshape(-1)]).astype(BF16)
    return jnp.pad(flat.reshape(10, LANES128), ((0, 6), (0, 0)))


def unpack_shard(late, head, zero_rank):
    late = late.reshape(-1)
    head_flat = head.reshape(-1)
    starts = [s * SHARD - SPLIT_AT - LANES128 * max(0, ((s * SHARD + 64) // LANES128 - IN_ROWS) // 16 * 16) for s in range(1, 4)]
    tail = head_flat[TAIL_AT * LANES128 : (TAIL_AT + 10) * LANES128]

    def pick(s):
        if s == 0:
            return lambda: jnp.concatenate([head_flat[:SPLIT_AT], late[: SHARD - SPLIT_AT]])
        if s == 3:
            return lambda: jnp.concatenate([late[starts[2] : starts[2] + SHARD - 10 * LANES128], tail])
        return lambda: late[starts[s - 1] : starts[s - 1] + SHARD]

    return lax.switch(zero_rank, [pick(s) for s in range(4)]).astype(F32)


UNPACK_SKEW = (EDGE + IN_ROWS) % 16


def unpack_kernel(own, near, far, both, w_out, w_mlp, w_down, packed, edges, stage, pair_rows, load_sem, edge_sem):
    zero = lax.axis_index("zero")
    shards = [(own, zero), (near, flip(zero, 0)), (far, flip(zero, 1)), (both, flip(flip(zero, 0), 1))]
    loads = [
        pltpu.make_async_copy(shard.at[pl.ds(EDGE, BODY)], packed.at[pl.ds(pl.multiple_of(STEP * s + EDGE, 16), BODY)], load_sem.at[k])
        for k, (shard, s) in enumerate(shards)
    ]
    ends = [pltpu.make_async_copy(shard.at[pl.ds(at, EDGE)], edges.at[s, h], edge_sem.at[k, h])
            for k, (shard, s) in enumerate(shards) for h, at in enumerate((0, EDGE + BODY))]
    for copy in ends + loads:
        copy.start()
    for copy in ends:
        copy.wait()
    packed[:EDGE] = edges[0, 0]
    for s in range(4):
        tile = edges[s, 1].astype(F32)
        if s < 3:
            tile = tile + edges[s + 1, 0].astype(F32)
        packed[pl.ds(STEP * (s + 1), EDGE), :] = tile.astype(BF16)
    for copy in loads:
        copy.wait()

    def fetch(first_row, count):
        stage[: count + 16] = packed[pl.ds(pl.multiple_of(first_row - UNPACK_SKEW, 16), count + 16), :].astype(F32)

    def split_pairs(first_row, target, row):
        fetch(first_row, PAIR_ROWS)
        tiles = [stage[pl.ds(UNPACK_SKEW + t, PAIR_STEP, stride=9), :] for t in range(9)]
        even, odd = pl.ds(0, PAIR_STEP, stride=2), pl.ds(1, PAIR_STEP, stride=2)
        for t in range(4):
            pair_rows[t, even, :] = tiles[t]
        pair_rows[4, even, :] = tiles[4]
        for t in range(4):
            pair_rows[t, odd, :] = jnp.concatenate([tiles[4 + t][:, 64:], tiles[5 + t][:, :64]], axis=1)
        pair_rows[4, odd, :] = jnp.concatenate([tiles[8][:, 64:], tiles[8][:, :64]], axis=1)
        at = pl.ds(pl.multiple_of(row, 2 * PAIR_STEP), 2 * PAIR_STEP)
        for t in range(4):
            target[at, t * 128 : (t + 1) * 128] = pair_rows[t].astype(BF16)
        target[at, 512:] = pair_rows[4, :, :64].astype(BF16)

    out_at = EDGE + IN_ROWS
    mlp_at = out_at + OUT_ROWS
    down_at = mlp_at + MLP_ROWS

    @pl.loop(0, WIDTH_Q // (2 * PAIR_STEP))
    def _(piece):
        split_pairs(out_at + piece * PAIR_ROWS, w_out, piece * 2 * PAIR_STEP)

    @pl.loop(0, FF // (2 * PAIR_STEP))
    def _(piece):
        split_pairs(down_at + piece * PAIR_ROWS, w_down, piece * 2 * PAIR_STEP)

    @pl.loop(0, D // WIDE_STEP)
    def _(piece):
        fetch(mlp_at + piece * WIDE_STEP * WIDE_TILES, WIDE_STEP * WIDE_TILES)
        rows = pl.ds(pl.multiple_of(piece * WIDE_STEP, WIDE_STEP), WIDE_STEP)
        for tile in range(WIDE_TILES):
            w_mlp[rows, tile * 128 : (tile + 1) * 128] = stage[pl.ds(UNPACK_SKEW + tile, WIDE_STEP, stride=WIDE_TILES), :].astype(BF16)


def unpack_weights(shards):
    shape = jax.ShapeDtypeStruct
    return pl.pallas_call(
        unpack_kernel,
        name="unpack_weights",
        in_specs=[pl.BlockSpec(memory_space=pl.ANY)] * 4,
        out_shape=[shape((WIDTH_Q, D), BF16), shape((D, 2 * FF), BF16), shape((FF, D), BF16)],
        scratch_shapes=[
            pltpu.VMEM((3 * STEP + SPAN, LANES128), BF16),
            pltpu.VMEM((4, 2, EDGE, LANES128), BF16),
            pltpu.VMEM((WIDE_STEP * WIDE_TILES + 16, 128), F32),
            pltpu.VMEM((5, 2 * PAIR_STEP, 128), F32),
            pltpu.SemaphoreType.DMA((4,)),
            pltpu.SemaphoreType.DMA((4, 2)),
        ],
        cost_estimate=pl.CostEstimate(flops=0, bytes_accessed=0, transcendentals=0),
        compiler_params=pltpu.CompilerParams(vmem_limit_bytes=VMEM_LIMIT),
    )(*shards)


def column_parts(lanes_t, dp_size):
    seqs, width, columns = lanes_t.shape
    return lanes_t.reshape(seqs, width, dp_size, columns // dp_size).transpose(2, 0, 1, 3)


def spread(parts):
    return lax.all_to_all(parts, "dp", split_axis=0, concat_axis=0, tiled=True)


def regroup(parts, order):
    dp_size, seqs, width, columns = parts.shape
    parts = jnp.take(parts.reshape(dp_size * seqs, width, columns), order, axis=0, mode="clip")
    return lax.all_to_all(parts.reshape(dp_size, seqs, width, columns), "dp", split_axis=0, concat_axis=0, tiled=True)


def joined(parts):
    dp_size, seqs, width, rows = parts.shape
    return parts.transpose(1, 2, 0, 3).reshape(seqs, width, dp_size * rows)


def exchange(values, axis, bit):
    return lax.ppermute(values, axis, [(i, i ^ (1 << bit)) for i in range(lax.axis_size(axis))])


def quarters(window, dp_rank):
    size = window.shape[1] // 4

    def rows_for(mask, kind):
        at, count = CLASSES[kind]
        first, second = (bit_of(dp_rank, bit) ^ (mask >> bit & 1) for bit in bit_order(2, kind))
        return lax.dynamic_slice_in_dim(window[at : at + count], first * (2 * size) + second * size, size, 1)

    return [jnp.concatenate([rows_for(mask, kind) for kind in range(2)]) for mask in range(4)]


def exchange_quarters(rows):
    def sent(values, mask):
        return lax.ppermute(values, "dp", [(i, i ^ mask) for i in range(lax.axis_size("dp"))])

    return [rows[0]] + [sent(rows[mask], mask) for mask in range(1, 4)]


def halve(parts, dp_rank, bit):
    half = parts.shape[1] // 2
    mine = bit_of(dp_rank, bit)
    sent = lax.dynamic_slice_in_dim(parts, (1 - mine) * half, half, 1)
    return [lax.dynamic_slice_in_dim(parts, mine * half, half, 1), exchange(sent, "dp", bit)]


def added(pieces):
    return sum(piece.astype(F32) for piece in pieces).astype(BF16)


def unpack_first(first_rows, last_rows):
    w_in = first_rows[EDGE : EDGE + IN_ROWS].reshape(-1)[:SPLIT_AT].reshape(D, QKVG)
    w_in = jnp.pad(w_in, ((0, 0), (0, QKVG_PAD - QKVG)))
    rows = last_rows[GAIN_AT : GAIN_AT + 10].astype(F32)
    return w_in, rows[:9].reshape(2, D), rows[9].reshape(2, HEAD_DIM)


def local(tokens, cotangent, lengths, balance, master, moment_one, moment_two):
    dp_rank, zero_rank = lax.axis_index("dp"), lax.axis_index("zero")
    dp_size, zero_size = lax.axis_size("dp"), lax.axis_size("zero")
    seqs = tokens.shape[0]
    order = lax.dynamic_index_in_dim(balance, zero_rank, 0, keepdims=False)
    inverse = jnp.zeros_like(order).at[order].set(jnp.arange(order.shape[0], dtype=order.dtype))
    lens = lax.dynamic_slice_in_dim(lengths, (dp_rank * zero_size + zero_rank) * seqs, seqs)
    tokens_t = tokens.swapaxes(1, 2)
    cot_parts = spread(column_parts(cotangent.swapaxes(1, 2), dp_size))
    own, first_rows, last_rows = pack_master(master)
    far, near = exchange(own, "zero", 1), exchange(own, "zero", 0)
    first = unpack_first(first_rows, last_rows)
    att_t, gate, kept = layer_forward(tokens_t, lens, first)
    far, near, att_t, cot_parts = lax.optimization_barrier((far, near, att_t, cot_parts))
    both = exchange(far, "zero", 0)
    cot_here = regroup(cot_parts, inverse)
    w_out, w_mlp, w_down = unpack_weights((own, near, far, both))
    w_in, gains, head_gains = first
    gain_cols, head_gains = gains[:, :, None], head_gains[:, :, None]
    out_columns, *stash = mlp(lens, att_t, gate, tokens_t, gains, w_out, w_mlp, w_down, dp_size)
    output_parts = spread(out_columns)
    grad_hidden_t, grad_att_t, logit_delta, late_kept, late_sent, g_gain_two = mlp_back(
        lens, att_t, gate, cot_here, *stash, gains, w_out, w_mlp, w_down, window_rows(dp_size))
    late_in = exchange(late_sent, "zero", 0)
    output_parts, grad_att_t = lax.optimization_barrier((output_parts, grad_att_t))
    output_parts = regroup(output_parts, order)
    q_t, k_n, k_t, v_n, log_total, raw = kept
    high = bit_of(zero_rank, 1)
    side = lambda windows, h: lax.dynamic_index_in_dim(windows, h, 0, keepdims=False)
    crossing = added([side(late_kept, 1 - high), side(late_in, 1 - high)])
    crossing, grad_att_t = lax.optimization_barrier((crossing, grad_att_t))
    crossed = exchange(crossing, "zero", 1)
    dq_t, dk_t, dv_t = attend_back(
        lens, q_t, k_n, k_t, v_n, grad_att_t, head_groups(log_total), head_groups(logit_delta[:, 16:]))
    dq_t, crossed = lax.optimization_barrier((dq_t, crossed))
    window = added([side(late_kept, high), side(late_in, high), crossed]).reshape(REDUCE_PARTS, -1, LANES128)
    dp_bits = dp_size.bit_length() - 1
    rows, dq_t = lax.optimization_barrier((quarters(window, dp_rank), dq_t))
    pieces = exchange_quarters(rows)
    cosine, sine = (jnp.asarray(t) for t in rope_tables())
    grad_tokens_t, g_in, g_gain_one, g_head = project_back(
        lens, dq_t, dk_t, dv_t, logit_delta, raw, tokens_t, grad_hidden_t, w_in, gain_cols, head_gains, cosine, sine)
    pieces, g_in, output_parts = lax.optimization_barrier((pieces, g_in, output_parts))
    share = added(pieces)
    head = flat_rows(g_in, head_rows(dp_size))
    gain_rows = pack_gains(g_gain_one, g_gain_two, g_head)
    for step in range(2, dp_bits):
        pieces = halve(share, dp_rank, step)
        pieces, head, gain_rows = lax.optimization_barrier((pieces, head, gain_rows))
        share = added(pieces)
    grad_tokens = grad_tokens_t.swapaxes(1, 2)
    head_sum, late_sum = sum_head(head, gain_rows, share, window.shape[1], dp_size)
    output = joined(output_parts).swapaxes(1, 2)
    grad_shard = unpack_shard(late_sum, head_sum, zero_rank)
    gain_width = D // zero_size
    gain_sums = head_sum[TAIL_AT : TAIL_AT + 9].reshape(2, zero_size, gain_width)
    grad_gains = lax.dynamic_index_in_dim(gain_sums, zero_rank, 1, keepdims=False).astype(F32)
    next_one = BETA_ONE * moment_one + (1.0 - BETA_ONE) * grad_shard
    next_two = BETA_TWO * moment_two + (1.0 - BETA_TWO) * grad_shard * grad_shard
    update_dir = next_one / BIAS_ONE / jnp.sqrt(next_two / BIAS_TWO)
    return output, grad_tokens, grad_shard, update_dir, next_one, next_two, grad_gains


def solution(mesh):
    lanes = P(("dp", "zero"), None, None)
    return jax.shard_map(
        local,
        mesh=mesh,
        in_specs=(lanes, lanes, P(), P(), P("zero"), P("zero"), P("zero")),
        out_specs=(lanes, lanes, P("zero"), P("zero"), P("zero"), P("zero"), P(None, "zero")),
        check_vma=False,
    )
```

```python
import functools
import math

import jax
import jax.numpy as jnp
import numpy as np
from jax import lax
from jax.experimental import pallas as pl
from jax.experimental.pallas import tpu as pltpu
from jax.sharding import PartitionSpec as P

D = 576
HEADS = 9
KV_HEADS = 3
GROUP = HEADS // KV_HEADS
HEAD_DIM = 64
HALF = HEAD_DIM // 2
FF = 1536
LANE = 1024
QKVG = 969
QKVG_PAD = 1024
WIDTH_Q = HEADS * HEAD_DIM
WIDTH_K = KV_HEADS * HEAD_DIM
PARAMS = 3545408
EPSILON = 1e-05
ROPE_BASE = 100000.0
BETA_ONE = 0.9
BETA_TWO = 0.95
BIAS_ONE = 1.0 - BETA_ONE**10
BIAS_TWO = 1.0 - BETA_TWO**10
SCALE = HEAD_DIM ** (-0.5)
EXP_SCALE = SCALE * math.log2(math.e)
F32 = jnp.float32
BF16 = jnp.bfloat16
BLOCK = 256
BLOCKS = LANE // BLOCK
FF_CHUNK = 768
MLP_BLOCK = 512
MLP_BLOCKS = LANE // MLP_BLOCK
PROJ_BLOCK = 512
PROJ_BLOCKS = LANE // PROJ_BLOCK
VMEM_LIMIT = 60 * 1024 * 1024


def dot(a, b, ca, cb):
    return lax.dot_general(a, b, (((ca,), (cb,)), ((), ())), preferred_element_type=F32)


def rope_tables():
    frequency = ROPE_BASE ** (-(np.arange(HALF, dtype=np.float32) * np.float32(2.0)) / np.float32(HEAD_DIM))
    angles = np.arange(LANE, dtype=np.float32)[None, :] * frequency.astype(np.float32)[:, None]
    return np.cos(angles).astype(np.float32), np.sin(angles).astype(np.float32)


def mean_square_scale(values, axis):
    return lax.rsqrt(jnp.mean(values * values, axis=axis, keepdims=True) + EPSILON)


def block_spec(shape, index):
    return pl.BlockSpec(shape, index)


def whole(shape):
    return pl.BlockSpec(shape, lambda *_: (0,) * len(shape), pipeline_mode=pl.Buffered(1))


def full_col_map(lane, block, lens):
    return (lane, 0, block)


def last_block(lens, lane, block):
    return jnp.minimum(block, (lens[lane] - 1) // BLOCK)


def project_kernel(lens, tok_t, w_in, gain_cols, head_gains, cosine, sine, q_t, k_n, k_t, v_n, v_t, raw, gate, w_in_t):
    lane, block = pl.program_id(0), pl.program_id(1)

    @pl.when((lane == 0) & (block == 0))
    def _():
        w_in_t[...] = w_in[...].T

    @pl.when(block * PROJ_BLOCK < lens[lane])
    def _():
        x = tok_t[0].astype(F32)
        normed = (x * mean_square_scale(x, 0) * gain_cols[0]).astype(BF16)
        projected = dot(w_in_t[...], normed, 1, 0)
        raw[0] = projected[: WIDTH_Q + WIDTH_K]
        cos, sin = cosine[...], sine[...]
        for head in range(HEADS + KV_HEADS):
            u = projected[head * HEAD_DIM : (head + 1) * HEAD_DIM]
            y = u * mean_square_scale(u, 0) * head_gains[0 if head < HEADS else 1]
            y1, y2 = y[:HALF], y[HALF:]
            turned = jnp.concatenate([y1 * cos - y2 * sin, y2 * cos + y1 * sin], axis=0)
            if head < HEADS:
                q_t[0, head * HEAD_DIM : (head + 1) * HEAD_DIM] = turned.astype(BF16)
            else:
                k = head - HEADS
                k_t[0, k * HEAD_DIM : (k + 1) * HEAD_DIM] = turned.astype(BF16)
                k_n[0, k] = turned.T.astype(BF16)
        values = projected[WIDTH_Q + WIDTH_K : WIDTH_Q + 2 * WIDTH_K]
        v_t[0] = values.astype(BF16)
        for k in range(KV_HEADS):
            v_n[0, k] = values[k * HEAD_DIM : (k + 1) * HEAD_DIM].T.astype(BF16)
        gate[0] = projected[WIDTH_Q + 2 * WIDTH_K : WIDTH_Q + 2 * WIDTH_K + 16]

    @pl.when(block * PROJ_BLOCK >= lens[lane])
    def _():
        for ref in (q_t, k_n, k_t, v_n, v_t):
            ref[...] = jnp.zeros_like(ref)


def col_map(lane, block, lens):
    return (lane, 0, last_block(lens, lane, block))


def mlp_row_map(lane, block, lens):
    return (lane, jnp.minimum(block, (lens[lane] - 1) // MLP_BLOCK), 0)


def mlp_col_map(lane, block, lens):
    return (lane, 0, jnp.minimum(block, (lens[lane] - 1) // MLP_BLOCK))


def proj_col_map(lane, block, lens):
    return (lane, 0, jnp.minimum(block, (lens[lane] - 1) // PROJ_BLOCK))


def proj_table_map(lane, block, lens):
    return (0, jnp.minimum(block, (lens[lane] - 1) // PROJ_BLOCK))


def full_head_map(lane, block, lens):
    return (lane, 0, block, 0)


def project(lens, tokens_t, w_in, gain_cols, head_gains, cosine, sine):
    lanes = tokens_t.shape[0]
    shape = jax.ShapeDtypeStruct
    return pl.pallas_call(
        project_kernel,
        name="project",
        grid_spec=pltpu.PrefetchScalarGridSpec(
            num_scalar_prefetch=1,
            grid=(lanes, PROJ_BLOCKS),
            in_specs=[
                pl.BlockSpec((1, D, PROJ_BLOCK), proj_col_map),
                whole((D, QKVG_PAD)),
                whole((2, D, 1)),
                whole((2, HEAD_DIM, 1)),
                pl.BlockSpec((HALF, PROJ_BLOCK), proj_table_map),
                pl.BlockSpec((HALF, PROJ_BLOCK), proj_table_map),
            ],
            out_specs=[
                pl.BlockSpec((1, WIDTH_Q, PROJ_BLOCK), full_col_map),
                pl.BlockSpec((1, KV_HEADS, PROJ_BLOCK, HEAD_DIM), full_head_map),
                pl.BlockSpec((1, WIDTH_K, PROJ_BLOCK), full_col_map),
                pl.BlockSpec((1, KV_HEADS, PROJ_BLOCK, HEAD_DIM), full_head_map),
                pl.BlockSpec((1, WIDTH_K, PROJ_BLOCK), full_col_map),
                pl.BlockSpec((1, WIDTH_Q + WIDTH_K, PROJ_BLOCK), proj_col_map),
                pl.BlockSpec((1, 16, PROJ_BLOCK), proj_col_map),
            ],
            scratch_shapes=[pltpu.VMEM((QKVG_PAD, D), BF16)],
        ),
        out_shape=[
            shape((lanes, WIDTH_Q, LANE), BF16),
            shape((lanes, KV_HEADS, LANE, HEAD_DIM), BF16),
            shape((lanes, WIDTH_K, LANE), BF16),
            shape((lanes, KV_HEADS, LANE, HEAD_DIM), BF16),
            shape((lanes, WIDTH_K, LANE), BF16),
            shape((lanes, WIDTH_Q + WIDTH_K, LANE), F32),
            shape((lanes, 16, LANE), F32),
        ],
        cost_estimate=pl.CostEstimate(flops=0, bytes_accessed=0, transcendentals=0),
        compiler_params=pltpu.CompilerParams(vmem_limit_bytes=VMEM_LIMIT),
    )(lens, tokens_t, w_in, gain_cols, head_gains, cosine, sine)


def causal_tile(values, fill):
    key_pos = lax.broadcasted_iota(jnp.int32, values.shape, 0)
    query_pos = lax.broadcasted_iota(jnp.int32, values.shape, 1)
    return jnp.where(key_pos <= query_pos, values, fill)


def attend_kernel(lens, q_t, k_n, v_t, out_t, log_total):
    lane, block = pl.program_id(0), pl.program_id(1)
    log_total[0] = jnp.zeros((16, BLOCK), F32)

    for level in range(BLOCKS):

        @pl.when((block == level) & (level * BLOCK < lens[lane]))
        def _():
            before = level * BLOCK
            for head in range(HEADS):
                g = head // GROUP
                query = q_t[0, head * HEAD_DIM : (head + 1) * HEAD_DIM]
                values = v_t.at[0, g * HEAD_DIM : (g + 1) * HEAD_DIM]
                weights = jnp.exp2(dot(k_n[0, g, before : before + BLOCK], query, 1, 0) * EXP_SCALE)
                weights = causal_tile(weights, 0.0)
                total = jnp.sum(weights, axis=0, keepdims=True)
                mixed = dot(values[:, before : before + BLOCK], weights.astype(BF16), 1, 0)
                if before:
                    weights = jnp.exp2(dot(k_n[0, g, :before], query, 1, 0) * EXP_SCALE)
                    total += jnp.sum(weights, axis=0, keepdims=True)
                    mixed += dot(values[:, :before], weights.astype(BF16), 1, 0)
                out_t[0, head * HEAD_DIM : (head + 1) * HEAD_DIM] = mixed * (1.0 / total)
                log_total[0, head : head + 1] = jnp.log2(total)


def attend(lens, q_t, k_n, v_t):
    lanes = q_t.shape[0]
    shape = jax.ShapeDtypeStruct
    return pl.pallas_call(
        attend_kernel,
        name="attend",
        grid_spec=pltpu.PrefetchScalarGridSpec(
            num_scalar_prefetch=1,
            grid=(lanes, BLOCKS),
            in_specs=[
                pl.BlockSpec((1, WIDTH_Q, BLOCK), col_map),
                pl.BlockSpec((1, KV_HEADS, LANE, HEAD_DIM), lambda lane, block, lens: (lane, 0, 0, 0)),
                pl.BlockSpec((1, WIDTH_K, LANE), lambda lane, block, lens: (lane, 0, 0)),
            ],
            out_specs=[
                pl.BlockSpec((1, WIDTH_Q, BLOCK), col_map),
                pl.BlockSpec((1, 16, BLOCK), full_col_map),
            ],
        ),
        out_shape=[
            shape((lanes, WIDTH_Q, LANE), F32),
            shape((lanes, 16, LANE), F32),
        ],
        cost_estimate=pl.CostEstimate(flops=0, bytes_accessed=0, transcendentals=0),
        compiler_params=pltpu.CompilerParams(vmem_limit_bytes=VMEM_LIMIT),
    )(lens, q_t, k_n, v_t)


OUT_ROWS = WIDTH_Q * D // 128
MLP_ROWS = D * 2 * FF // 128
DOWN_ROWS = FF * D // 128
LATE_ROWS = OUT_ROWS + MLP_ROWS + DOWN_ROWS
WIDE_TILES = 2 * FF // 128
WIDE_STEP = 48
PAIR_STEP = 32
PAIR_ROWS = PAIR_STEP * 9


def pack_wide(source, target, stage, first_row):
    @pl.loop(0, D // WIDE_STEP)
    def _(piece):
        rows = pl.ds(pl.multiple_of(piece * WIDE_STEP, WIDE_STEP), WIDE_STEP)
        for tile in range(WIDE_TILES):
            stage[pl.ds(tile, WIDE_STEP, stride=WIDE_TILES), :] = source[rows, tile * 128 : (tile + 1) * 128]
        size = WIDE_STEP * WIDE_TILES
        target[pl.ds(pl.multiple_of(first_row + piece * size, 16), size), :] = stage[:size].astype(BF16)


def set_tiles(target, value):
    for t in range(4):
        target[t] = value[:, t * 128 : (t + 1) * 128]
    target[4, :, :64] = value[:, 512:]


def pack_pairs(rows_ref, stage):
    tiles = [rows_ref[t, pl.ds(parity, PAIR_STEP, stride=2), :] for parity in range(2) for t in range(5)]
    even, odd = tiles[:5], tiles[5:]
    for t in range(4):
        stage[pl.ds(t, PAIR_STEP, stride=9), :] = even[t]
    stage[pl.ds(4, PAIR_STEP, stride=9), :] = jnp.concatenate([even[4][:, :64], odd[0][:, :64]], axis=1)
    for t in range(4):
        right = odd[t + 1][:, :64]
        stage[pl.ds(5 + t, PAIR_STEP, stride=9), :] = jnp.concatenate([odd[t][:, 64:], right], axis=1)


def mlp_kernel(lens, att_t, gate, tok_t, gains, w_out, w_mlp, w_down, out_parts, hidden_in, act_low, gate_slope, up_slope, total):
    lane, block = pl.program_id(0), pl.program_id(1)

    @pl.when(block * MLP_BLOCK >= lens[lane])
    def _():
        out_parts[...] = jnp.zeros_like(out_parts)

    @pl.when(block * MLP_BLOCK < lens[lane])
    def _():
        att = att_t[0].reshape(HEADS, HEAD_DIM, MLP_BLOCK)
        sig = jax.nn.sigmoid(gate[0, :HEADS])[:, None, :]
        gated_t = (att * sig).reshape(WIDTH_Q, MLP_BLOCK).astype(BF16)
        hidden = tok_t[0].T.astype(F32) + dot(gated_t, w_out[...], 0, 0)
        hidden_in[0] = hidden
        mixed = (hidden * mean_square_scale(hidden, 1) * gains[1:2]).astype(BF16)
        valid_t = lax.broadcasted_iota(jnp.int32, (1, MLP_BLOCK), 1) + block * MLP_BLOCK < lens[lane]
        total[...] = hidden

        @pl.loop(0, FF // FF_CHUNK, unroll=True)
        def _(chunk):
            low = pl.ds(pl.multiple_of(chunk * FF_CHUNK, FF_CHUNK), FF_CHUNK)
            high = pl.ds(pl.multiple_of(FF + chunk * FF_CHUNK, FF_CHUNK), FF_CHUNK)
            g = dot(mixed, w_mlp[:, low], 1, 0)
            u = dot(mixed, w_mlp[:, high], 1, 0)
            s = jax.nn.sigmoid(g)
            gs = g * s
            act = (gs * u).astype(BF16)
            total[...] += dot(act, w_down[low, :], 1, 0)
            act_low[0, :, low] = act
            gate_slope[0, :, low] = (u * (s * (1.0 + g * (1.0 - s)))).astype(BF16)
            up_slope[0, :, low] = gs.astype(BF16)

        out_t = jnp.where(valid_t, total[...].T, 0.0).astype(BF16)
        width = out_parts.shape[3]
        for part in range(out_parts.shape[0]):
            out_parts[part, 0] = out_t[:, part * width : (part + 1) * width]


def part_map(lane, block, lens):
    return (block, lane, 0, 0)


def kept_part_map(lane, block, lens):
    return (jnp.minimum(block, (lens[lane] - 1) // MLP_BLOCK), lane, 0, 0)


def mlp(lens, att_t, gate, tokens_t, gains, w_out, w_mlp, w_down, dp_size):
    lanes = tokens_t.shape[0]
    width = LANE // dp_size
    shape = jax.ShapeDtypeStruct
    return pl.pallas_call(
        mlp_kernel,
        name="mlp",
        grid_spec=pltpu.PrefetchScalarGridSpec(
            num_scalar_prefetch=1,
            grid=(lanes, MLP_BLOCKS),
            in_specs=[
                pl.BlockSpec((1, WIDTH_Q, MLP_BLOCK), mlp_col_map),
                pl.BlockSpec((1, 16, MLP_BLOCK), mlp_col_map),
                pl.BlockSpec((1, D, MLP_BLOCK), mlp_col_map),
                whole((2, D)),
                whole((WIDTH_Q, D)),
                whole((D, 2 * FF)),
                whole((FF, D)),
            ],
            out_specs=[
                pl.BlockSpec((dp_size // MLP_BLOCKS, 1, D, width), part_map),
                pl.BlockSpec((1, MLP_BLOCK, D), mlp_row_map),
                pl.BlockSpec((1, MLP_BLOCK, FF), mlp_row_map),
                pl.BlockSpec((1, MLP_BLOCK, FF), mlp_row_map),
                pl.BlockSpec((1, MLP_BLOCK, FF), mlp_row_map),
            ],
            scratch_shapes=[pltpu.VMEM((MLP_BLOCK, D), F32)],
        ),
        out_shape=[
            shape((dp_size, lanes, D, width), BF16),
            shape((lanes, LANE, D), F32),
            shape((lanes, LANE, FF), BF16),
            shape((lanes, LANE, FF), BF16),
            shape((lanes, LANE, FF), BF16),
        ],
        compiler_params=pltpu.CompilerParams(vmem_limit_bytes=VMEM_LIMIT),
    )(lens, att_t, gate, tokens_t, gains, w_out, w_mlp, w_down)


def mlp_back_kernel(lens, att_t, gate, cot_parts, hidden_in, act_low, gate_slope, up_slope, gains, w_out, w_mlp, w_down,
                    grad_hidden_t, grad_att_t, logit_delta, kept, sent, g_gain,
                    back, g_out, g_mlp, g_down_t, late, stage, pair_rows, copy_sem):
    lane, block = pl.program_id(0), pl.program_id(1)

    @pl.when((lane == 0) & (block == 0))
    def _():
        g_out[...] = jnp.zeros_like(g_out)
        g_mlp[...] = jnp.zeros_like(g_mlp)
        g_down_t[...] = jnp.zeros_like(g_down_t)
        g_gain[...] = jnp.zeros_like(g_gain)

    @pl.when(block * MLP_BLOCK >= lens[lane])
    def _():
        grad_att_t[...] = jnp.zeros_like(grad_att_t)
        logit_delta[...] = jnp.zeros_like(logit_delta)

    @pl.when(block * MLP_BLOCK < lens[lane])
    def _():
        att = att_t[0].reshape(HEADS, HEAD_DIM, MLP_BLOCK)
        sig = jax.nn.sigmoid(gate[0, :HEADS])[:, None, :]
        gated_t = (att * sig).reshape(WIDTH_Q, MLP_BLOCK).astype(BF16)
        hidden = hidden_in[0]
        scale = mean_square_scale(hidden, 1)
        gain = gains[1:2]
        mixed_t = (hidden * scale * gain).astype(BF16).T
        valid_t = lax.broadcasted_iota(jnp.int32, (1, MLP_BLOCK), 1) + block * MLP_BLOCK < lens[lane]
        cot_t = jnp.concatenate([cot_parts[part, 0] for part in range(cot_parts.shape[0])], axis=1)
        grad_low_t = jnp.where(valid_t, cot_t.astype(F32), 0.0).astype(BF16)
        grad_low = grad_low_t.T
        back[...] = jnp.zeros_like(back)

        @pl.loop(0, FF // FF_CHUNK, unroll=True)
        def _(chunk):
            low = pl.ds(pl.multiple_of(chunk * FF_CHUNK, FF_CHUNK), FF_CHUNK)
            high = pl.ds(pl.multiple_of(FF + chunk * FF_CHUNK, FF_CHUNK), FF_CHUNK)
            a = dot(grad_low, w_down[low, :], 1, 1)
            grad_gate = (a * gate_slope[0, :, low].astype(F32)).astype(BF16)
            grad_up = (a * up_slope[0, :, low].astype(F32)).astype(BF16)
            back[...] += dot(grad_gate, w_mlp[:, low], 1, 1) + dot(grad_up, w_mlp[:, high], 1, 1)
            g_mlp[:, low] += dot(mixed_t, grad_gate, 1, 0)
            g_mlp[:, high] += dot(mixed_t, grad_up, 1, 0)
            g_down_t[:, low] += dot(grad_low_t, act_low[0, :, low], 1, 0)

        b = back[...]
        g_gain[0:1] += jnp.sum(b * hidden * scale, axis=0, keepdims=True)
        bg = b * gain
        grad_h = grad_low.astype(F32) + scale * bg - hidden * (scale * scale * scale * jnp.mean(hidden * bg, axis=1, keepdims=True))
        grad_hidden_t[0] = grad_h.T
        branch = grad_h.astype(BF16)
        g_out[...] += dot(gated_t, branch, 1, 0)
        c = dot(w_out[...], branch, 1, 1).reshape(HEADS, HEAD_DIM, MLP_BLOCK)
        grad_att = (c * sig).astype(BF16)
        grad_att_t[0] = grad_att.reshape(WIDTH_Q, MLP_BLOCK)
        sig2 = sig[:, 0, :]
        logit_delta[0, :HEADS] = jnp.sum(c * att, axis=1) * (sig2 * (1.0 - sig2))
        logit_delta[0, 16 : 16 + HEADS] = jnp.sum(grad_att.astype(F32) * att, axis=1)

    @pl.when((lane == pl.num_programs(0) - 1) & (block == pl.num_programs(1) - 1))
    def _():
        @pl.loop(0, WIDTH_Q // (2 * PAIR_STEP))
        def _(piece):
            set_tiles(pair_rows, g_out[pl.ds(pl.multiple_of(piece * 2 * PAIR_STEP, 2 * PAIR_STEP), 2 * PAIR_STEP), :])
            pack_pairs(pair_rows, stage)
            late[pl.ds(pl.multiple_of(piece * PAIR_ROWS, 16), PAIR_ROWS), :] = stage[:PAIR_ROWS].astype(BF16)

        pack_wide(g_mlp, late, stage, OUT_ROWS)

        @pl.loop(0, FF // 128)
        def _(piece):
            turned = g_down_t[:, pl.ds(pl.multiple_of(piece * 128, 128), 128)].T
            for h in range(128 // (2 * PAIR_STEP)):
                set_tiles(pair_rows, turned[h * 2 * PAIR_STEP : (h + 1) * 2 * PAIR_STEP])
                pack_pairs(pair_rows, stage)
                start = OUT_ROWS + MLP_ROWS + (piece * 2 + h) * PAIR_ROWS
                late[pl.ds(pl.multiple_of(start, 16), PAIR_ROWS), :] = stage[:PAIR_ROWS].astype(BF16)

        late[LATE_ROWS:] = jnp.zeros((late.shape[0] - LATE_ROWS, 128), BF16)
        low = bit_of(lax.axis_index("zero"), 0)
        copies = []
        for h in range(2):
            for side, target in enumerate((kept, sent)):
                start = pl.multiple_of(window_start(2 * h + (low if side == 0 else 1 - low)), 16)
                copies.append(pltpu.make_async_copy(late.at[pl.ds(start, kept.shape[1])], target.at[h], copy_sem.at[h, side]))
        for copy in copies:
            copy.start()
        for copy in copies:
            copy.wait()


def mlp_back(lens, att_t, gate, cot_parts, hidden_in, act_low, gate_slope, up_slope, gains, w_out, w_mlp, w_down, window):
    dp_size, lanes, _, width = cot_parts.shape
    shape = jax.ShapeDtypeStruct
    return pl.pallas_call(
        mlp_back_kernel,
        name="mlp_back",
        grid_spec=pltpu.PrefetchScalarGridSpec(
            num_scalar_prefetch=1,
            grid=(lanes, MLP_BLOCKS),
            in_specs=[
                pl.BlockSpec((1, WIDTH_Q, MLP_BLOCK), mlp_col_map),
                pl.BlockSpec((1, 16, MLP_BLOCK), mlp_col_map),
                pl.BlockSpec((dp_size // MLP_BLOCKS, 1, D, width), kept_part_map),
                pl.BlockSpec((1, MLP_BLOCK, D), mlp_row_map),
                pl.BlockSpec((1, MLP_BLOCK, FF), mlp_row_map),
                pl.BlockSpec((1, MLP_BLOCK, FF), mlp_row_map),
                pl.BlockSpec((1, MLP_BLOCK, FF), mlp_row_map),
                whole((2, D)),
                whole((WIDTH_Q, D)),
                whole((D, 2 * FF)),
                whole((FF, D)),
            ],
            out_specs=[
                pl.BlockSpec((1, D, MLP_BLOCK), mlp_col_map),
                pl.BlockSpec((1, WIDTH_Q, MLP_BLOCK), full_col_map),
                pl.BlockSpec((1, 32, MLP_BLOCK), full_col_map),
                pl.BlockSpec(memory_space=pl.ANY),
                pl.BlockSpec(memory_space=pl.ANY),
                whole((8, D)),
            ],
            scratch_shapes=[
                pltpu.VMEM((MLP_BLOCK, D), F32),
                pltpu.VMEM((WIDTH_Q, D), F32),
                pltpu.VMEM((D, 2 * FF), F32),
                pltpu.VMEM((D, FF), F32),
                pltpu.VMEM((LAST_WINDOW + window, 128), BF16),
                pltpu.VMEM((WIDE_STEP * WIDE_TILES, 128), F32),
                pltpu.VMEM((5, 2 * PAIR_STEP, 128), F32),
                pltpu.SemaphoreType.DMA((2, 2)),
            ],
        ),
        out_shape=[
            shape((lanes, D, LANE), F32),
            shape((lanes, WIDTH_Q, LANE), BF16),
            shape((lanes, 32, LANE), F32),
            shape((2, window, 128), BF16),
            shape((2, window, 128), BF16),
            shape((8, D), F32),
        ],
        compiler_params=pltpu.CompilerParams(vmem_limit_bytes=VMEM_LIMIT),
    )(lens, att_t, gate, cot_parts, hidden_in, act_low, gate_slope, up_slope, gains, w_out, w_mlp, w_down)


def project_back_kernel(lens, dq_t, dk_t, dv_t, logit_delta, raw, tok_t, grad_hidden_t, w_in, gain_cols, head_gains,
                        cosine, sine, grad_tok_t, g_in, g_gain, g_head, dproj, head_sum, gain_sum):
    lane, block = pl.program_id(0), pl.program_id(1)

    @pl.when((lane == 0) & (block == 0))
    def _():
        g_in[...] = jnp.zeros_like(g_in)
        gain_sum[...] = jnp.zeros_like(gain_sum)
        head_sum[...] = jnp.zeros_like(head_sum)

    @pl.when(block * PROJ_BLOCK >= lens[lane])
    def _():
        grad_tok_t[...] = jnp.zeros_like(grad_tok_t)

    @pl.when(block * PROJ_BLOCK < lens[lane])
    def _():
        cos, sin = cosine[...], sine[...]
        for head in range(HEADS + KV_HEADS):
            rows = slice(head * HEAD_DIM, (head + 1) * HEAD_DIM)
            side = 0 if head < HEADS else 1
            source = dq_t if head < HEADS else dk_t
            at = (head if head < HEADS else head - HEADS) * HEAD_DIM
            d1, d2 = source[0, at : at + HALF], source[0, at + HALF : at + HEAD_DIM]
            d = jnp.concatenate([d1 * cos + d2 * sin, d2 * cos - d1 * sin], axis=0)
            u = raw[0, rows]
            r = mean_square_scale(u, 0)
            ur = u * r
            head_sum[side] += d * ur
            dg = d * head_gains[side]
            dproj[rows] = (r * (dg - ur * jnp.mean(ur * dg, axis=0, keepdims=True))).astype(BF16)
        dproj[WIDTH_Q + WIDTH_K : WIDTH_Q + 2 * WIDTH_K] = dv_t[0].astype(BF16)
        row = lax.broadcasted_iota(jnp.int32, (16, PROJ_BLOCK), 0)
        logits = jnp.where(row < HEADS, logit_delta[0], 0.0).astype(BF16)
        dproj[WIDTH_Q + 2 * WIDTH_K :] = jnp.concatenate(
            [logits, jnp.zeros((QKVG_PAD - WIDTH_Q - 2 * WIDTH_K - 16, PROJ_BLOCK), BF16)], axis=0
        )
        x = tok_t[0].astype(F32)
        scale = mean_square_scale(x, 0)
        xs = x * scale
        gain = gain_cols[0]
        normed = (xs * gain).astype(BF16)
        g_in[...] += dot(normed, dproj[...], 1, 1)
        back = dot(w_in[...], dproj[...], 1, 0)
        gain_sum[...] += back * xs
        bg = back * gain
        grad_x = scale * (bg - xs * jnp.mean(xs * bg, axis=0, keepdims=True))
        grad_tok_t[0] = (grad_hidden_t[0] + grad_x).astype(BF16)

    @pl.when((lane == pl.num_programs(0) - 1) & (block == pl.num_programs(1) - 1))
    def _():
        g_head[...] = jnp.sum(head_sum[...], axis=2)
        g_gain[...] = jnp.sum(gain_sum[...], axis=1)[None]


def project_back(lens, dq_t, dk_t, dv_t, logit_delta, raw, tokens_t, grad_hidden_t, w_in, gain_cols, head_gains, cosine, sine):
    lanes = tokens_t.shape[0]
    shape = jax.ShapeDtypeStruct
    full_col = lambda lane, block, lens: (lane, 0, block)
    return pl.pallas_call(
        project_back_kernel,
        name="project_back",
        grid_spec=pltpu.PrefetchScalarGridSpec(
            num_scalar_prefetch=1,
            grid=(lanes, PROJ_BLOCKS),
            in_specs=[
                pl.BlockSpec((1, WIDTH_Q, PROJ_BLOCK), proj_col_map),
                pl.BlockSpec((1, WIDTH_K, PROJ_BLOCK), proj_col_map),
                pl.BlockSpec((1, WIDTH_K, PROJ_BLOCK), proj_col_map),
                pl.BlockSpec((1, 16, PROJ_BLOCK), proj_col_map),
                pl.BlockSpec((1, WIDTH_Q + WIDTH_K, PROJ_BLOCK), proj_col_map),
                pl.BlockSpec((1, D, PROJ_BLOCK), proj_col_map),
                pl.BlockSpec((1, D, PROJ_BLOCK), proj_col_map),
                whole((D, QKVG_PAD)),
                whole((2, D, 1)),
                whole((2, HEAD_DIM, 1)),
                pl.BlockSpec((HALF, PROJ_BLOCK), proj_table_map),
                pl.BlockSpec((HALF, PROJ_BLOCK), proj_table_map),
            ],
            out_specs=[
                pl.BlockSpec((1, D, PROJ_BLOCK), full_col),
                whole((D, QKVG_PAD)),
                whole((1, D)),
                whole((2, HEAD_DIM)),
            ],
            scratch_shapes=[
                pltpu.VMEM((QKVG_PAD, PROJ_BLOCK), BF16),
                pltpu.VMEM((2, HEAD_DIM, PROJ_BLOCK), F32),
                pltpu.VMEM((D, PROJ_BLOCK), F32),
            ],
        ),
        out_shape=[
            shape((lanes, D, LANE), BF16),
            shape((D, QKVG_PAD), F32),
            shape((1, D), F32),
            shape((2, HEAD_DIM), F32),
        ],
        cost_estimate=pl.CostEstimate(flops=20_000_000_000, bytes_accessed=60_000_000, transcendentals=0),
        compiler_params=pltpu.CompilerParams(vmem_limit_bytes=VMEM_LIMIT),
    )(lens, dq_t, dk_t, dv_t, logit_delta, raw, tokens_t, grad_hidden_t, w_in, gain_cols, head_gains, cosine, sine)


def layer_forward(tokens_t, lens, weights):
    w_in, gains, head_gains = weights
    gain_cols, head_gains = gains[:, :, None], head_gains[:, :, None]
    cosine, sine = (jnp.asarray(t) for t in rope_tables())
    q_t, k_n, k_t, v_n, v_t, raw, gate = project(lens, tokens_t, w_in, gain_cols, head_gains, cosine, sine)
    att_t, log_total = attend(lens, q_t, k_n, v_t)
    return att_t, gate, (q_t, k_n, k_t, v_n, log_total, raw)


def head_groups(rows):
    return rows[:, :HEADS].reshape(rows.shape[0], KV_HEADS, GROUP, LANE)


SHARD = PARAMS // 4
LANES128 = 128
EDGE = 16
STEP = 6928
BODY = STEP - EDGE
SPAN = STEP + EDGE
IN_ROWS = 4361
SPLIT_AT = D * QKVG
MESH = pl.DeviceIdType.MESH


def shard_shift(s):
    offset = EDGE * LANES128 - (STEP * LANES128 - SHARD) * s + (64 if s else 0)
    return offset // LANES128, offset % LANES128


def flip(index, bit):
    return index + (1 - 2 * (index // (1 << bit) % 2)) * (1 << bit)


def bit_of(index, bit):
    return index // (1 << bit) % 2


def greet(partners):
    barrier = pltpu.get_barrier_semaphore()
    for partner in partners:
        pl.semaphore_signal(barrier, inc=1, device_id=partner, device_id_type=MESH)
    pl.semaphore_wait(barrier, len(partners))


PACK_TILE = 496
FIRST_ROWS = 4368
LAST_TILE = 32
GAIN_AT = EDGE + IN_ROWS + LATE_ROWS - 3 * STEP - (SPAN - LAST_TILE)
FIRST_PIECES = 8
FIRST_CUTS = (0, 544, 1088, 1632, 2176, 2720, 3264, 3808, FIRST_ROWS)
FIRST_TILES = -(-(EDGE + FIRST_ROWS) // PACK_TILE)


def pack_kernel(master, own, first_rows, last_rows, rows_in, packed, load_sem, keep_sem, own_sem, send_sem, recv_sem):
    dp, zero = lax.axis_index("dp"), lax.axis_index("zero")
    core, across, side = (dp, flip(zero, 0)), (dp, flip(zero, 1)), (flip(dp, 0), zero)
    y = bit_of(dp, 0)
    load = pltpu.make_async_copy(master, rows_in.at[pl.ds(24, STEP)], load_sem)
    load.start()
    rows_in[:24] = jnp.zeros((24, LANES128), F32)
    rows_in[24 + STEP :] = jnp.zeros((24, LANES128), F32)
    greet((core, across, side))
    load.wait()
    lane = lax.broadcasted_iota(jnp.int32, (PACK_TILE, LANES128), 1)

    def shifted(start, a, k):
        if k == 0:
            return rows_in[pl.ds(start + 24 - a, PACK_TILE), :]
        here = pltpu.roll(rows_in[pl.ds(start + 24 - a, PACK_TILE), :], k, 1)
        above = pltpu.roll(rows_in[pl.ds(start + 23 - a, PACK_TILE), :], k, 1)
        return jnp.where(lane >= k, here, above)

    def pack(s, start):
        if s == 0 and start + PACK_TILE <= EDGE + IN_ROWS:
            value = shifted(start, EDGE, 0)
        elif s == 0 and start < EDGE + IN_ROWS:
            row = lax.broadcasted_iota(jnp.int32, (PACK_TILE, LANES128), 0) + start
            value = jnp.where(row < EDGE + IN_ROWS, shifted(start, EDGE, 0), shifted(start, EDGE, 64))
        elif s == 0:
            value = shifted(start, EDGE, 64)
        else:
            value = shifted(start, *shard_shift(s))
        packed[pl.ds(start, PACK_TILE), :] = value.astype(BF16)

    def piece_rows(piece):
        return pl.ds(EDGE + FIRST_CUTS[piece], FIRST_CUTS[piece + 1] - FIRST_CUTS[piece])

    def mine(piece):
        return packed.at[piece_rows(piece)]

    def theirs(piece):
        return first_rows.at[piece_rows(piece)]

    def copy(source, target, device, slot):
        return pltpu.make_async_remote_copy(source, target, send_sem.at[slot], recv_sem.at[slot],
                                            device_id=device, device_id_type=MESH)

    def pieces_of(half):
        return range(half * FIRST_PIECES // 2, (half + 1) * FIRST_PIECES // 2)

    def send_first():
        for half in range(2):

            @pl.when(y == half)
            def _():
                for piece in pieces_of(half):
                    copy(mine(piece), theirs(piece), across, piece).start()

        for piece in range(FIRST_PIECES):
            copy(mine(piece), theirs(piece), core, FIRST_PIECES + piece).start()

    for s in range(4):

        @pl.when(zero == s)
        def _():
            for t in range(SPAN // PACK_TILE):
                pack(s, t * PACK_TILE)
                if s == 0 and t + 1 == FIRST_TILES:
                    send_first()

    keep = pltpu.make_async_copy(packed, own, own_sem)
    keep.start()
    tail = packed.at[pl.ds(SPAN - LAST_TILE, LAST_TILE)]

    @pl.when(zero == 3)
    def _():
        copy(tail, last_rows, across, 2 * FIRST_PIECES + 1).start()
        copy(tail, last_rows, core, 2 * FIRST_PIECES).start()
        stay = pltpu.make_async_copy(tail, last_rows, keep_sem)
        stay.start()
        stay.wait()
        copy(tail, last_rows, across, 2 * FIRST_PIECES + 1).wait_send()
        copy(tail, last_rows, core, 2 * FIRST_PIECES).wait_send()

    @pl.when(zero == 1)
    def _():
        copy(last_rows, last_rows, across, 2 * FIRST_PIECES + 1).wait_recv()
        copy(last_rows, last_rows, core, 2 * FIRST_PIECES).start()
        copy(last_rows, last_rows, core, 2 * FIRST_PIECES).wait_send()

    for half in range(2):
        pieces, others = pieces_of(half), pieces_of(1 - half)

        @pl.when((zero == 0) & (y == half))
        def _():
            stay = pltpu.make_async_copy(packed.at[pl.ds(EDGE, FIRST_ROWS)], first_rows.at[pl.ds(EDGE, FIRST_ROWS)], keep_sem)
            stay.start()
            for piece in pieces:
                copy(mine(piece), theirs(piece), across, piece).wait_send()
            for piece in range(FIRST_PIECES):
                copy(mine(piece), theirs(piece), core, FIRST_PIECES + piece).wait_send()
            stay.wait()

        @pl.when((zero == 2) & (y == half))
        def _():
            for piece in pieces:
                copy(theirs(piece), theirs(piece), across, piece).wait_recv()
                copy(theirs(piece), theirs(piece), side, piece).start()
                copy(theirs(piece), theirs(piece), core, FIRST_PIECES + piece).start()
            for piece in others:
                copy(theirs(piece), theirs(piece), side, piece).wait_recv()
                copy(theirs(piece), theirs(piece), core, FIRST_PIECES + piece).start()
            for piece in pieces:
                copy(theirs(piece), theirs(piece), side, piece).wait_send()
            for piece in range(FIRST_PIECES):
                copy(theirs(piece), theirs(piece), core, FIRST_PIECES + piece).wait_send()

    @pl.when(bit_of(zero, 0) == 0)
    def _():
        copy(last_rows, last_rows, core, 2 * FIRST_PIECES).wait_recv()

    @pl.when(bit_of(zero, 0) == 1)
    def _():
        for piece in range(FIRST_PIECES):
            copy(theirs(piece), theirs(piece), core, FIRST_PIECES + piece).wait_recv()

    keep.wait()


def pack_master(master):
    rows = jnp.pad(master, (0, STEP * LANES128 - SHARD)).reshape(STEP, LANES128)
    shape = jax.ShapeDtypeStruct
    return pl.pallas_call(
        pack_kernel,
        name="pack_master",
        out_shape=[shape((SPAN, LANES128), BF16), shape((EDGE + FIRST_ROWS, LANES128), BF16), shape((LAST_TILE, LANES128), BF16)],
        in_specs=[pl.BlockSpec(memory_space=pl.ANY)],
        out_specs=[pl.BlockSpec(memory_space=pl.ANY)] * 3,
        scratch_shapes=[
            pltpu.VMEM((24 + STEP + 24, LANES128), F32),
            pltpu.VMEM((SPAN, LANES128), BF16),
            pltpu.SemaphoreType.DMA,
            pltpu.SemaphoreType.DMA,
            pltpu.SemaphoreType.DMA,
            pltpu.SemaphoreType.DMA((2 * FIRST_PIECES + 2,)),
            pltpu.SemaphoreType.DMA((2 * FIRST_PIECES + 2,)),
        ],
        cost_estimate=pl.CostEstimate(flops=0, bytes_accessed=0, transcendentals=0),
        compiler_params=pltpu.CompilerParams(collective_id=0, has_side_effects=True, vmem_limit_bytes=VMEM_LIMIT),
    )(rows)


REDUCE_PARTS = 11


def window_start(s):
    return jnp.minimum(s, 1) * (((s * SHARD + 64) // LANES128 - IN_ROWS) // 16 * 16)


LAST_WINDOW = ((3 * SHARD + 64) // LANES128 - IN_ROWS) // 16 * 16


def window_rows(dp_size):
    unit = REDUCE_PARTS * 16 * dp_size
    return -(-(SHARD // LANES128 + 17) // unit) * unit


CLASSES = ((0, 6), (6, 5))


def bit_order(bits, kind):
    order = list(range(bits))
    if kind and bits > 1:
        order[0], order[1] = 1, 0
    return order


def part_region(dp, rows, bits, kind, count):
    offset, size = 0, rows
    for k in bit_order(bits, kind)[:count]:
        size = size // 2
        offset = offset + bit_of(dp, k) * size
    return offset, size


def aligned(offset, size):
    return pl.ds(pl.multiple_of(offset, 16), size)


LATE_HOP = 12.0


def arrival_order(chains, hops):
    free, order = {}, []
    pending = [(0.0, index, 0) for index in range(len(chains))]
    while pending:
        pending.sort()
        start, index, step = pending.pop(0)
        link, span = chains[index][step]
        end = max(start, free.get(link, 0.0)) + span
        free[link] = end
        hop = hops[index]
        order.append((end + hop, index, step))
        if step + 1 < len(chains[index]):
            pending.append((end + hop, index, step + 1))
    return sorted(order)


def attend_back_kernel(lens, q_t, k_n, k_t, v_n, grad_t, log_total, delta, dq_t, dk_t, dv_t):
    lane = pl.program_id(0)
    dq_t[...] = jnp.zeros_like(dq_t)
    for block in range(BLOCKS):
        keys = pl.ds(block * BLOCK, BLOCK)

        @pl.when(block * BLOCK >= lens[lane])
        def _():
            dk_t[0, :, keys] = jnp.zeros((HEAD_DIM, BLOCK), F32)
            dv_t[0, :, keys] = jnp.zeros((HEAD_DIM, BLOCK), F32)

        @pl.when(block * BLOCK < lens[lane])
        def _():
            k_rows, v_rows, k_cols = k_n[0, 0, keys, :], v_n[0, 0, keys, :], k_t[0, :, keys]
            dk = jnp.zeros((HEAD_DIM, BLOCK), F32)
            dv = jnp.zeros((HEAD_DIM, BLOCK), F32)
            cols = pl.ds(block * BLOCK, LANE - block * BLOCK)
            for r in range(GROUP):
                head = slice(r * HEAD_DIM, (r + 1) * HEAD_DIM)
                query, grad = q_t[0, head, cols], grad_t[0, head, cols]
                prob = jnp.exp2(dot(k_rows, query, 1, 0) * EXP_SCALE - log_total[0, 0, r : r + 1, cols])
                prob = causal_tile(prob, 0.0)
                grad_prob = dot(v_rows, grad, 1, 0) - delta[0, 0, r : r + 1, cols]
                grad_score = (prob * grad_prob).astype(BF16)
                dv += dot(grad, prob.astype(BF16), 1, 1)
                dk += dot(query, grad_score, 1, 1)
                dq_t[0, head, cols] += dot(k_cols, grad_score, 1, 0) * SCALE
            dk_t[0, :, keys] = dk * SCALE
            dv_t[0, :, keys] = dv


def attend_back(lens, q_t, k_n, k_t, v_n, grad_t, log_total, delta):
    lanes = q_t.shape[0]
    shape = jax.ShapeDtypeStruct
    group_rows = lambda lane, g, lens: (lane, g, 0)
    group_heads = lambda lane, g, lens: (lane, g, 0, 0)
    return pl.pallas_call(
        attend_back_kernel,
        name="attend_back",
        grid_spec=pltpu.PrefetchScalarGridSpec(
            num_scalar_prefetch=1,
            grid=(lanes, KV_HEADS),
            in_specs=[
                pl.BlockSpec((1, GROUP * HEAD_DIM, LANE), group_rows),
                pl.BlockSpec((1, 1, LANE, HEAD_DIM), group_heads),
                pl.BlockSpec((1, HEAD_DIM, LANE), group_rows),
                pl.BlockSpec((1, 1, LANE, HEAD_DIM), group_heads),
                pl.BlockSpec((1, GROUP * HEAD_DIM, LANE), group_rows),
                pl.BlockSpec((1, 1, GROUP, LANE), group_heads),
                pl.BlockSpec((1, 1, GROUP, LANE), group_heads),
            ],
            out_specs=[
                pl.BlockSpec((1, GROUP * HEAD_DIM, LANE), group_rows),
                pl.BlockSpec((1, HEAD_DIM, LANE), group_rows),
                pl.BlockSpec((1, HEAD_DIM, LANE), group_rows),
            ],
        ),
        out_shape=[
            shape((lanes, WIDTH_Q, LANE), F32),
            shape((lanes, WIDTH_K, LANE), F32),
            shape((lanes, WIDTH_K, LANE), F32),
        ],
        cost_estimate=pl.CostEstimate(flops=40_000_000_000, bytes_accessed=40_000_000, transcendentals=0),
        compiler_params=pltpu.CompilerParams(vmem_limit_bytes=VMEM_LIMIT),
    )(lens, q_t, k_n, k_t, v_n, grad_t, log_total, delta)


TAIL_AT = 4368


HEAD_PARTS = 3
HEAD_HOP = 3.0
LATE_GROUPS = ((0, 0, 3), (1, 0, 3), (0, 3, 3), (1, 3, 2))


def head_rows(dp_size):
    unit = 2 * HEAD_PARTS * 16 * 2 * dp_size
    return -(-(TAIL_AT + 16) // unit) * unit


def sum_head_kernel(bits, rows, late_rows, source, gain_rows, late_share, result, late_sum, total, *rest):
    received, (load_sem, send_sem, recv_sem, late_send, late_recv) = rest[:-5], rest[-5:]
    dp, zero = lax.axis_index("dp"), lax.axis_index("zero")
    axes = [("zero", 1)] + [("dp", k) for k in range(bits)]

    def partner(axis, k):
        return (flip(dp, k), zero) if axis == "dp" else (dp, flip(zero, k))

    def bit(axis, k):
        return bit_of(dp if axis == "dp" else zero, k)

    load = pltpu.make_async_copy(source, total, load_sem)
    load.start()
    load.wait()
    total[TAIL_AT : TAIL_AT + 16] = gain_rows[...]
    greet([partner("zero", 0)] + [partner(*axis) for axis in axes])

    def step(index, slot, source_ref, target_ref, axis):
        copy = pltpu.make_async_remote_copy(source_ref, target_ref, send_sem.at[index, slot], recv_sem.at[index, slot],
                                            device_id=partner(*axis), device_id_type=MESH)
        copy.start()
        return copy

    def order_of(index):
        return [("zero", 0)] + [axes[(index + j) % len(axes)] for j in range(len(axes))]

    def spans_of(index):
        spans = [(axis, 0.5 if axis == ("zero", 0) else 9.0 / HEAD_PARTS / (1 << slot)) for slot, axis in enumerate(order_of(index))]
        return spans + spans[::-1]

    def chain_of(index):
        order = order_of(index)
        size = rows // HEAD_PARTS
        offset = index * size
        regions = []
        for slot, axis in enumerate(order):
            half = size // 2
            mine, other = offset + bit(*axis) * half, offset + (1 - bit(*axis)) * half
            landing = received[slot].at[index]
            yield step(index, slot, total.at[aligned(other, half)], landing, axis)
            at = aligned(mine, half)
            target = total if slot + 1 < len(order) else result
            target[at] = (total[at].astype(F32) + landing[...].astype(F32)).astype(BF16)
            offset, size = mine, half
            regions.append(at)
        for slot in reversed(range(len(order))):
            place = result.at[regions[slot]]
            yield step(index, 2 * len(order) - 1 - slot, place, place, order[slot])

    def late_spans(index):
        kind, _, count = LATE_GROUPS[index]
        spans = [(("dp", k), 20.0 / (1 << slot) * count / REDUCE_PARTS) for slot, k in enumerate(bit_order(bits, kind))]
        return spans[::-1]

    def late_chain(index):
        kind, start, count = LATE_GROUPS[index]
        parts = pl.ds(CLASSES[kind][0] + start, count)
        late_sum[parts, aligned(*part_region(dp, late_rows, bits, kind, bits))] = late_share[parts]
        for slot, k in reversed(list(enumerate(bit_order(bits, kind)))):
            place = late_sum.at[parts, aligned(*part_region(dp, late_rows, bits, kind, slot + 1))]
            copy = pltpu.make_async_remote_copy(place, place, late_send.at[index, slot], late_recv.at[index, slot],
                                                device_id=partner("dp", k), device_id_type=MESH)
            copy.start()
            yield copy

    chains = [chain_of(i) for i in range(HEAD_PARTS)] + [late_chain(i) for i in range(len(LATE_GROUPS))]
    spans = [spans_of(i) for i in range(HEAD_PARTS)] + [late_spans(i) for i in range(len(LATE_GROUPS))]
    flying = [next(chain) for chain in chains]
    sent = list(flying)
    for _, index, _ in arrival_order(spans, [HEAD_HOP] * HEAD_PARTS + [LATE_HOP] * len(LATE_GROUPS)):
        flying[index].wait_recv()
        following = next(chains[index], None)
        if following is not None:
            flying[index] = following
            sent.append(following)
    for copy in sent:
        copy.wait_send()


def sum_head(source, gain_rows, share, late_rows, dp_size):
    bits = dp_size.bit_length() - 1
    rows = source.shape[0]
    steps = bits + 2
    shape = jax.ShapeDtypeStruct
    return pl.pallas_call(
        functools.partial(sum_head_kernel, bits, rows, late_rows),
        name="sum_head",
        out_shape=[shape((rows, LANES128), BF16), shape((REDUCE_PARTS, late_rows, LANES128), BF16)],
        in_specs=[pl.BlockSpec(memory_space=pl.ANY)] + [pl.BlockSpec(memory_space=pltpu.VMEM)] * 2,
        out_specs=[pl.BlockSpec(memory_space=pltpu.VMEM)] * 2,
        scratch_shapes=[
            pltpu.VMEM((rows, LANES128), BF16),
            *[pltpu.VMEM((HEAD_PARTS, rows // HEAD_PARTS >> (k + 1), LANES128), BF16) for k in range(steps)],
            pltpu.SemaphoreType.DMA,
            pltpu.SemaphoreType.DMA((HEAD_PARTS, 2 * steps)),
            pltpu.SemaphoreType.DMA((HEAD_PARTS, 2 * steps)),
            pltpu.SemaphoreType.DMA((len(LATE_GROUPS), bits)),
            pltpu.SemaphoreType.DMA((len(LATE_GROUPS), bits)),
        ],
        compiler_params=pltpu.CompilerParams(collective_id=2, has_side_effects=True, vmem_limit_bytes=VMEM_LIMIT),
    )(source, gain_rows, share)


def flat_rows(g_in, rows):
    flat = g_in[:, :QKVG].astype(BF16).reshape(-1)
    return jnp.pad(flat, (0, rows * LANES128 - SPLIT_AT)).reshape(rows, LANES128)


def pack_gains(g_gain_one, g_gain_two, g_head):
    flat = jnp.concatenate([g_gain_one[0], g_gain_two[0], g_head.reshape(-1)]).astype(BF16)
    return jnp.pad(flat.reshape(10, LANES128), ((0, 6), (0, 0)))


def unpack_shard(late, head, zero_rank):
    late = late.reshape(-1)
    head_flat = head.reshape(-1)
    starts = [s * SHARD - SPLIT_AT - LANES128 * max(0, ((s * SHARD + 64) // LANES128 - IN_ROWS) // 16 * 16) for s in range(1, 4)]
    tail = head_flat[TAIL_AT * LANES128 : (TAIL_AT + 10) * LANES128]

    def pick(s):
        if s == 0:
            return lambda: jnp.concatenate([head_flat[:SPLIT_AT], late[: SHARD - SPLIT_AT]])
        if s == 3:
            return lambda: jnp.concatenate([late[starts[2] : starts[2] + SHARD - 10 * LANES128], tail])
        return lambda: late[starts[s - 1] : starts[s - 1] + SHARD]

    return lax.switch(zero_rank, [pick(s) for s in range(4)]).astype(F32)


UNPACK_SKEW = (EDGE + IN_ROWS) % 16


def unpack_kernel(own, near, far, both, w_out, w_mlp, w_down, packed, edges, stage, pair_rows, load_sem, edge_sem):
    zero = lax.axis_index("zero")
    shards = [(own, zero), (near, flip(zero, 0)), (far, flip(zero, 1)), (both, flip(flip(zero, 0), 1))]
    loads = [
        pltpu.make_async_copy(shard.at[pl.ds(EDGE, BODY)], packed.at[pl.ds(pl.multiple_of(STEP * s + EDGE, 16), BODY)], load_sem.at[k])
        for k, (shard, s) in enumerate(shards)
    ]
    ends = [pltpu.make_async_copy(shard.at[pl.ds(at, EDGE)], edges.at[s, h], edge_sem.at[k, h])
            for k, (shard, s) in enumerate(shards) for h, at in enumerate((0, EDGE + BODY))]
    for copy in ends + loads:
        copy.start()
    for copy in ends:
        copy.wait()
    packed[:EDGE] = edges[0, 0]
    for s in range(4):
        tile = edges[s, 1].astype(F32)
        if s < 3:
            tile = tile + edges[s + 1, 0].astype(F32)
        packed[pl.ds(STEP * (s + 1), EDGE), :] = tile.astype(BF16)
    for copy in loads:
        copy.wait()

    def fetch(first_row, count):
        stage[: count + 16] = packed[pl.ds(pl.multiple_of(first_row - UNPACK_SKEW, 16), count + 16), :].astype(F32)

    def split_pairs(first_row, target, row):
        fetch(first_row, PAIR_ROWS)
        tiles = [stage[pl.ds(UNPACK_SKEW + t, PAIR_STEP, stride=9), :] for t in range(9)]
        even, odd = pl.ds(0, PAIR_STEP, stride=2), pl.ds(1, PAIR_STEP, stride=2)
        for t in range(4):
            pair_rows[t, even, :] = tiles[t]
        pair_rows[4, even, :] = tiles[4]
        for t in range(4):
            pair_rows[t, odd, :] = jnp.concatenate([tiles[4 + t][:, 64:], tiles[5 + t][:, :64]], axis=1)
        pair_rows[4, odd, :] = jnp.concatenate([tiles[8][:, 64:], tiles[8][:, :64]], axis=1)
        at = pl.ds(pl.multiple_of(row, 2 * PAIR_STEP), 2 * PAIR_STEP)
        for t in range(4):
            target[at, t * 128 : (t + 1) * 128] = pair_rows[t].astype(BF16)
        target[at, 512:] = pair_rows[4, :, :64].astype(BF16)

    out_at = EDGE + IN_ROWS
    mlp_at = out_at + OUT_ROWS
    down_at = mlp_at + MLP_ROWS

    @pl.loop(0, WIDTH_Q // (2 * PAIR_STEP))
    def _(piece):
        split_pairs(out_at + piece * PAIR_ROWS, w_out, piece * 2 * PAIR_STEP)

    @pl.loop(0, FF // (2 * PAIR_STEP))
    def _(piece):
        split_pairs(down_at + piece * PAIR_ROWS, w_down, piece * 2 * PAIR_STEP)

    @pl.loop(0, D // WIDE_STEP)
    def _(piece):
        fetch(mlp_at + piece * WIDE_STEP * WIDE_TILES, WIDE_STEP * WIDE_TILES)
        rows = pl.ds(pl.multiple_of(piece * WIDE_STEP, WIDE_STEP), WIDE_STEP)
        for tile in range(WIDE_TILES):
            w_mlp[rows, tile * 128 : (tile + 1) * 128] = stage[pl.ds(UNPACK_SKEW + tile, WIDE_STEP, stride=WIDE_TILES), :].astype(BF16)


def unpack_weights(shards):
    shape = jax.ShapeDtypeStruct
    return pl.pallas_call(
        unpack_kernel,
        name="unpack_weights",
        in_specs=[pl.BlockSpec(memory_space=pl.ANY)] * 4,
        out_shape=[shape((WIDTH_Q, D), BF16), shape((D, 2 * FF), BF16), shape((FF, D), BF16)],
        scratch_shapes=[
            pltpu.VMEM((3 * STEP + SPAN, LANES128), BF16),
            pltpu.VMEM((4, 2, EDGE, LANES128), BF16),
            pltpu.VMEM((WIDE_STEP * WIDE_TILES + 16, 128), F32),
            pltpu.VMEM((5, 2 * PAIR_STEP, 128), F32),
            pltpu.SemaphoreType.DMA((4,)),
            pltpu.SemaphoreType.DMA((4, 2)),
        ],
        cost_estimate=pl.CostEstimate(flops=0, bytes_accessed=0, transcendentals=0),
        compiler_params=pltpu.CompilerParams(vmem_limit_bytes=VMEM_LIMIT),
    )(*shards)


def column_parts(lanes_t, dp_size):
    seqs, width, columns = lanes_t.shape
    return lanes_t.reshape(seqs, width, dp_size, columns // dp_size).transpose(2, 0, 1, 3)


def spread(parts):
    return lax.all_to_all(parts, "dp", split_axis=0, concat_axis=0, tiled=True)


def regroup(parts, order):
    dp_size, seqs, width, columns = parts.shape
    parts = jnp.take(parts.reshape(dp_size * seqs, width, columns), order, axis=0, mode="clip")
    return lax.all_to_all(parts.reshape(dp_size, seqs, width, columns), "dp", split_axis=0, concat_axis=0, tiled=True)


def joined(parts):
    dp_size, seqs, width, rows = parts.shape
    return parts.transpose(1, 2, 0, 3).reshape(seqs, width, dp_size * rows)


def exchange(values, axis, bit):
    return lax.ppermute(values, axis, [(i, i ^ (1 << bit)) for i in range(lax.axis_size(axis))])


def quarters(window, dp_rank):
    size = window.shape[1] // 4

    def rows_for(mask, kind):
        at, count = CLASSES[kind]
        first, second = (bit_of(dp_rank, bit) ^ (mask >> bit & 1) for bit in bit_order(2, kind))
        return lax.dynamic_slice_in_dim(window[at : at + count], first * (2 * size) + second * size, size, 1)

    return [jnp.concatenate([rows_for(mask, kind) for kind in range(2)]) for mask in range(4)]


def exchange_quarters(rows):
    def sent(values, mask):
        return lax.ppermute(values, "dp", [(i, i ^ mask) for i in range(lax.axis_size("dp"))])

    return [rows[0]] + [sent(rows[mask], mask) for mask in range(1, 4)]


def halve(parts, dp_rank, bit):
    half = parts.shape[1] // 2
    mine = bit_of(dp_rank, bit)
    sent = lax.dynamic_slice_in_dim(parts, (1 - mine) * half, half, 1)
    return [lax.dynamic_slice_in_dim(parts, mine * half, half, 1), exchange(sent, "dp", bit)]


def added(pieces):
    return sum(piece.astype(F32) for piece in pieces).astype(BF16)


def unpack_first(first_rows, last_rows):
    w_in = first_rows[EDGE : EDGE + IN_ROWS].reshape(-1)[:SPLIT_AT].reshape(D, QKVG)
    w_in = jnp.pad(w_in, ((0, 0), (0, QKVG_PAD - QKVG)))
    rows = last_rows[GAIN_AT : GAIN_AT + 10].astype(F32)
    return w_in, rows[:9].reshape(2, D), rows[9].reshape(2, HEAD_DIM)


def local(tokens, cotangent, lengths, balance, master, moment_one, moment_two):
    dp_rank, zero_rank = lax.axis_index("dp"), lax.axis_index("zero")
    dp_size, zero_size = lax.axis_size("dp"), lax.axis_size("zero")
    seqs = tokens.shape[0]
    order = lax.dynamic_index_in_dim(balance, zero_rank, 0, keepdims=False)
    inverse = jnp.zeros_like(order).at[order].set(jnp.arange(order.shape[0], dtype=order.dtype))
    lens = lax.dynamic_slice_in_dim(lengths, (dp_rank * zero_size + zero_rank) * seqs, seqs)
    tokens_t = tokens.swapaxes(1, 2)
    cot_parts = spread(column_parts(cotangent.swapaxes(1, 2), dp_size))
    own, first_rows, last_rows = pack_master(master)
    far, near = exchange(own, "zero", 1), exchange(own, "zero", 0)
    first = unpack_first(first_rows, last_rows)
    att_t, gate, kept = layer_forward(tokens_t, lens, first)
    far, near, att_t = lax.optimization_barrier((far, near, att_t))
    both = exchange(far, "zero", 0)
    both, cot_parts = lax.optimization_barrier((both, cot_parts))
    cot_here = regroup(cot_parts, inverse)
    w_out, w_mlp, w_down = unpack_weights((own, near, far, both))
    w_in, gains, head_gains = first
    gain_cols, head_gains = gains[:, :, None], head_gains[:, :, None]
    out_columns, *stash = mlp(lens, att_t, gate, tokens_t, gains, w_out, w_mlp, w_down, dp_size)
    output_parts = spread(out_columns)
    grad_hidden_t, grad_att_t, logit_delta, late_kept, late_sent, g_gain_two = mlp_back(
        lens, att_t, gate, cot_here, *stash, gains, w_out, w_mlp, w_down, window_rows(dp_size))
    late_in = exchange(late_sent, "zero", 0)
    output_parts, grad_att_t = lax.optimization_barrier((output_parts, grad_att_t))
    output_parts = regroup(output_parts, order)
    q_t, k_n, k_t, v_n, log_total, raw = kept
    high = bit_of(zero_rank, 1)
    side = lambda windows, h: lax.dynamic_index_in_dim(windows, h, 0, keepdims=False)
    crossing = added([side(late_kept, 1 - high), side(late_in, 1 - high)])
    crossing, grad_att_t = lax.optimization_barrier((crossing, grad_att_t))
    crossed = exchange(crossing, "zero", 1)
    dq_t, dk_t, dv_t = attend_back(
        lens, q_t, k_n, k_t, v_n, grad_att_t, head_groups(log_total), head_groups(logit_delta[:, 16:]))
    dq_t, crossed = lax.optimization_barrier((dq_t, crossed))
    window = added([side(late_kept, high), side(late_in, high), crossed]).reshape(REDUCE_PARTS, -1, LANES128)
    dp_bits = dp_size.bit_length() - 1
    rows, dq_t = lax.optimization_barrier((quarters(window, dp_rank), dq_t))
    pieces = exchange_quarters(rows)
    cosine, sine = (jnp.asarray(t) for t in rope_tables())
    grad_tokens_t, g_in, g_gain_one, g_head = project_back(
        lens, dq_t, dk_t, dv_t, logit_delta, raw, tokens_t, grad_hidden_t, w_in, gain_cols, head_gains, cosine, sine)
    pieces, g_in, output_parts = lax.optimization_barrier((pieces, g_in, output_parts))
    share = added(pieces)
    head = flat_rows(g_in, head_rows(dp_size))
    gain_rows = pack_gains(g_gain_one, g_gain_two, g_head)
    for step in range(2, dp_bits):
        pieces = halve(share, dp_rank, step)
        pieces, head, gain_rows = lax.optimization_barrier((pieces, head, gain_rows))
        share = added(pieces)
    grad_tokens = grad_tokens_t.swapaxes(1, 2)
    head_sum, late_sum = sum_head(head, gain_rows, share, window.shape[1], dp_size)
    output = joined(output_parts).swapaxes(1, 2)
    grad_shard = unpack_shard(late_sum, head_sum, zero_rank)
    gain_width = D // zero_size
    gain_sums = head_sum[TAIL_AT : TAIL_AT + 9].reshape(2, zero_size, gain_width)
    grad_gains = lax.dynamic_index_in_dim(gain_sums, zero_rank, 1, keepdims=False).astype(F32)
    next_one = BETA_ONE * moment_one + (1.0 - BETA_ONE) * grad_shard
    next_two = BETA_TWO * moment_two + (1.0 - BETA_TWO) * grad_shard * grad_shard
    update_dir = next_one / BIAS_ONE / jnp.sqrt(next_two / BIAS_TWO)
    return output, grad_tokens, grad_shard, update_dir, next_one, next_two, grad_gains


def solution(mesh):
    lanes = P(("dp", "zero"), None, None)
    return jax.shard_map(
        local,
        mesh=mesh,
        in_specs=(lanes, lanes, P(), P(), P("zero"), P("zero"), P("zero")),
        out_specs=(lanes, lanes, P("zero"), P("zero"), P("zero"), P("zero"), P(None, "zero")),
        check_vma=False,
    )
```
